128 devices in a mesh: dp: 16 (over z, y), mp: 8 (over x, core).
Axes of the slice: x: 4, y: 4, z: 4, core: 2. Of those that a mesh axis runs over, the one named last changes fastest.
Arguments:
- stream: float32 [16384, 1600], P('dp', 'mp'), may hold values from -40 to 40
- first_gain: float32 [1600], P('mp'), may hold values from 0.1 to 1.9
- first_shift: float32 [1600], P('mp'), may hold values from -3 to 3
- triple_weight: bfloat16 [1600, 3, 1600], P(None, None, 'mp'), may hold values from -0.15625 to 0.15625
- triple_bias: float32 [2, 1600], P(None, 'mp'), may hold values from -3 to 3
- mixer_weight: bfloat16 [1600, 1600], P('mp'), may hold values from -1.75 to 1.75
- mixer_bias: float32 [1600], P('mp'), may hold values from -3 to 3
- second_gain: float32 [1600], P('mp'), may hold values from 0.1 to 1.9
- second_shift: float32 [1600], P('mp'), may hold values from -3 to 3
- expand_weight: bfloat16 [1600, 6400], P(None, 'mp'), may hold values from -1 to 1
- expand_bias: float32 [6400], P('mp'), may hold values from -3 to 3
- reduce_weight: bfloat16 [6400, 1600], P('mp'), may hold values from -0.078125 to 0.078125
- reduce_bias: float32 [1600], P('mp'), may hold values from -3 to 3
- cotangent: float32 [16384, 1600], P('dp', 'mp'), may hold values from -6 to 6
Outputs:
- result: float32 [16384, 1600], P('dp', 'mp')
- grad_stream: float32 [16384, 1600], P('dp', 'mp')
- grad_first_gain: float32 [1600], P('mp')
- grad_first_shift: float32 [1600], P('mp')
- grad_triple_weight: float32 [1600, 3, 1600], P('dp', None, 'mp')
- grad_triple_bias: float32 [2, 1600], P(None, 'mp')
- grad_mixer_weight: float32 [1600, 1600], P('mp', 'dp')
- grad_mixer_bias: float32 [1600], P('mp')
- grad_second_gain: float32 [1600], P('mp')
- grad_second_shift: float32 [1600], P('mp')
- grad_expand_weight: float32 [1600, 6400], P('dp', 'mp')
- grad_expand_bias: float32 [6400], P('mp')
- grad_reduce_weight: float32 [6400, 1600], P('mp', 'dp')
- grad_reduce_bias: float32 [1600], P('mp')
The draws below stay inside these ranges and needn't reach their ends.
All inputs are finite; a program needn't handle non-finite values.
Results may differ from the reference program's by a relative error of at most 0.018.
Values may be sent and summed in bfloat16 or wider, within the bound.
A program may use at most 192 MiB of HBM per device.

```python
import math
import jax
import jax.numpy as jnp
from jax import lax

D = 1600
H = 25
HD = 64
FF = 6400
LEN = 1024
TOKENS = 16384


def draw_stream(key, part):
    key = jax.random.fold_in(key, 11)
    base_key, column_key, row_key = jax.random.split(key, 3)
    columns = jnp.arange(D, dtype=jnp.float32) / D
    column_scale = jnp.exp(jnp.log(3.0) * columns) * jax.random.uniform(column_key, (D,), jnp.float32, 0.7, 1.3)
    row_scale = jnp.exp(jax.random.uniform(row_key, (TOKENS, 1), jnp.float32, jnp.log(0.5), jnp.log(2.5)))
    base = jnp.clip(jax.random.normal(base_key, (TOKENS, D), jnp.float32), -4.0, 4.0)
    return (base * column_scale * row_scale).astype(jnp.float32)


def draw_expand_weight(key, part):
    key = jax.random.fold_in(key, 23)
    noise_key, common_key = jax.random.split(key)
    noise = jnp.clip(jax.random.normal(noise_key, (D, FF), jnp.float32), -4.0, 4.0)
    common = jnp.clip(jax.random.normal(common_key, (1, FF), jnp.float32), -4.0, 4.0)
    return ((noise + common) / math.sqrt(D)).astype(jnp.bfloat16)


def level_of(key, shape, cuts, least, high):
    level = 1.0
    for position, blocks in cuts:
        heights = jax.random.uniform(jax.random.fold_in(jax.random.fold_in(key, 6), position), (blocks,), jnp.float32, least / len(cuts), high / len(cuts))
        level = level * jnp.repeat(jnp.exp(heights), shape[position] // blocks).reshape((-1,) + (1,) * (len(shape) - 1 - position))
    return level


def bell_draw(key, dims, width, most, pieces=(), kind=jnp.bfloat16):
    factor_of = level_of(key, dims, pieces, -0.22, 0.18) if pieces else 1.0
    values = jax.random.normal(key, dims, jnp.float32) * width * factor_of
    return jnp.minimum(jnp.maximum(values, -most), most).astype(kind)


def setup_inputs(seed: int = 0) -> dict:
    arg_keys = jax.random.split(jax.random.key(seed), 15)
    stream = draw_stream(jax.random.fold_in(arg_keys[14], 71), 0)
    first_gain = jnp.clip(1.0 + 0.18 * jax.random.normal(arg_keys[1], (D,), jnp.float32), 0.1, 1.9)
    first_shift = bell_draw(arg_keys[2], (D,), 0.5, 3.0, ((0, 8),), jnp.float32)
    triple_weight = bell_draw(arg_keys[3], (D, 3, D), D ** -0.5, 0.15625, ((2, 8),))
    triple_bias = bell_draw(arg_keys[4], (2, D), 0.5, 3.0, ((1, 8),), jnp.float32)
    mixer_weight = bell_draw(arg_keys[5], (D, D), (max(D // 128, 4)) ** -0.5, 1.75, ((0, 8),))
    mixer_bias = bell_draw(arg_keys[6], (D,), 0.5, 3.0, ((0, 8),), jnp.float32)
    second_gain = jnp.clip(1.0 + 0.18 * jax.random.normal(arg_keys[7], (D,), jnp.float32), 0.1, 1.9)
    second_shift = bell_draw(arg_keys[8], (D,), 0.5, 3.0, ((0, 8),), jnp.float32)
    expand_weight = draw_expand_weight(jax.random.fold_in(arg_keys[14], 71), 0)
    expand_bias = bell_draw(arg_keys[10], (FF,), 0.5, 3.0, ((0, 8),), jnp.float32)
    reduce_weight = bell_draw(arg_keys[11], (FF, D), FF ** -0.5, 0.078125, ((0, 8),))
    reduce_bias = bell_draw(arg_keys[12], (D,), 0.5, 3.0, ((0, 8),), jnp.float32)
    cotangent = bell_draw(arg_keys[13], (TOKENS, D), 1.0, 6.0, ((0, 16), (1, 8)), jnp.float32)
    return {"stream": stream, "first_gain": first_gain, "first_shift": first_shift, "triple_weight": triple_weight, "triple_bias": triple_bias, "mixer_weight": mixer_weight, "mixer_bias": mixer_bias, "second_gain": second_gain, "second_shift": second_shift, "expand_weight": expand_weight, "expand_bias": expand_bias, "reduce_weight": reduce_weight, "reduce_bias": reduce_bias, "cotangent": cotangent}


@jax.custom_vjp
def low(v):
    return lax.optimization_barrier(v.astype(jnp.bfloat16)).astype(jnp.float32)

@jax.custom_vjp
def low_back(v):
    return v

def low_keep(v):
    return (low(v), None)

def low_pass(kept, grad):
    return (grad,)

def back_keep(v):
    return (v, None)

def back_low(kept, grad):
    return (low(grad),)
low.defvjp(low_keep, low_pass)
low_back.defvjp(back_keep, back_low)

def layer_norm(value, gain, shift):
    center = lax.optimization_barrier(jnp.mean(value, -1, keepdims=True))
    spread = lax.optimization_barrier(jnp.mean(jnp.square(value - center), -1, keepdims=True))
    return (value - center) * lax.rsqrt(spread + 1e-05) * gain + shift

def attend(block):
    queries = block[:, 0]
    keys_all = block[:, 1]
    values = block[:, 2]
    scale = 1.0 / math.sqrt(HD)
    scores = low_back(jnp.einsum('qhd,khd->hqk', queries, keys_all, precision=lax.Precision.HIGHEST) * scale)
    places = jnp.arange(LEN)
    allowed = places[None, :] <= places[:, None]
    scores = jnp.where(allowed[None], scores, -1e+30)
    probs = low(jax.nn.softmax(scores, -1))
    return jnp.einsum('hqk,khd->qhd', probs, values, precision=lax.Precision.HIGHEST)

def forward(stream, first_gain, first_shift, triple_weight, triple_bias, mixer_weight, mixer_bias, second_gain, second_shift, expand_weight, expand_bias, reduce_weight, reduce_bias):
    highest = lax.Precision.HIGHEST
    count = stream.shape[0]
    first_low = low(layer_norm(stream, first_gain, first_shift))
    bias_three = jnp.stack([triple_bias[0], jnp.zeros_like(triple_bias[0]), triple_bias[1]])
    triple = jnp.einsum('td,dce->tce', first_low, triple_weight, precision=highest) + bias_three
    triple = low_back(low(triple))
    grouped = triple.reshape(count // LEN, LEN, 3, H, HD)
    mixed = lax.map(jax.checkpoint(attend), grouped)
    mixed = low_back(low(mixed.reshape(count, H * HD)))
    after = stream + low_back(jnp.dot(mixed, mixer_weight, precision=highest)) + mixer_bias
    second_low = low(layer_norm(after, second_gain, second_shift))
    pre = low_back(jnp.dot(second_low, expand_weight, precision=highest)) + expand_bias
    hidden = low(jax.nn.gelu(pre, approximate=True))
    return after + low_back(jnp.dot(hidden, reduce_weight, precision=highest)) + reduce_bias

def reference(stream, first_gain, first_shift, triple_weight, triple_bias, mixer_weight, mixer_bias, second_gain, second_shift, expand_weight, expand_bias, reduce_weight, reduce_bias, cotangent):
    inputs = (stream, first_gain, first_shift, triple_weight.astype(jnp.float32), triple_bias, mixer_weight.astype(jnp.float32), mixer_bias, second_gain, second_shift, expand_weight.astype(jnp.float32), expand_bias, reduce_weight.astype(jnp.float32), reduce_bias)
    result, pullback = jax.vjp(forward, *inputs)
    grads = pullback(cotangent)
    return (result, grads[0], grads[1], grads[2], grads[3], grads[4], grads[5], grads[6], grads[7], grads[8], grads[9], grads[10], grads[11], grads[12])
```

```python
import functools
import math

import jax
import jax.numpy as jnp
from jax import lax
from jax.experimental import pallas as pl
from jax.experimental.pallas import tpu as pltpu
from jax.sharding import PartitionSpec as P

H = 25
HD = 64
LEN = 1024
D = 1600
FF = 6400
PARTS = 8
NARROW = D // PARTS
ROWS = 208
DEEP = 112
WIN = 256
HALF = LEN // 2
EPSILON = 1e-05
MESH = pl.DeviceIdType.MESH
BF = jnp.bfloat16
F32 = jnp.float32
VMEM_LIMIT = 60 * 1024 * 1024


def dot_n(left, right):
    return lax.dot_general(left, right, (((1,), (0,)), ((), ())), preferred_element_type=F32)


def dot_t(left, right):
    return lax.dot_general(left, right, (((1,), (1,)), ((), ())), preferred_element_type=F32)


def dot_f(left, right):
    return lax.dot_general(left, right, (((0,), (0,)), ((), ())), preferred_element_type=F32)


class Place:
    def __init__(self):
        self.me = lax.axis_index("mp")
        self.chip = self.me // 2
        self.core = self.me % 2
        self.right_chip = lax.rem(self.chip + 1, 4)
        self.left_chip = lax.rem(self.chip + 3, 4)
        self.far_chip = lax.rem(self.chip + 2, 4)
        self.right = self.right_chip * 2 + self.core
        self.left = self.left_chip * 2 + self.core
        self.far = self.far_chip * 2 + self.core
        self.twin = self.chip * 2 + 1 - self.core
        self.peers = [lax.rem(self.me + i, PARTS) for i in range(1, PARTS)]
        self.chips = [self.chip, self.left_chip, self.right_chip, self.far_chip]


def greet(place):
    barrier = pltpu.get_barrier_semaphore()
    for peer in place.peers:
        pl.semaphore_signal(barrier, inc=1, device_id={"mp": peer}, device_id_type=MESH)
    pl.semaphore_wait(barrier, len(place.peers))


def remote(source, target, send, receive, device):
    return pltpu.make_async_remote_copy(
        src_ref=source,
        dst_ref=target,
        send_sem=send,
        recv_sem=receive,
        device_id={"mp": device},
        device_id_type=MESH,
    )


class Share:
    def __init__(self, place, tiles, send, receive):
        self.place, self.tiles, self.send, self.receive = place, tiles, send, receive

    def copy(self, step, owner, device):
        tile = self.tiles.at[owner]
        return remote(tile, tile, self.send.at[step], self.receive.at[step], device)

    def start(self):
        for step, peer in enumerate(self.place.peers):
            self.copy(step, self.place.me, peer).start()

    def wait(self):
        me = self.place.me
        for step in range(PARTS - 1):
            owner = lax.rem(me + PARTS - 1 - step, PARTS)
            self.copy(step, owner, me).wait_recv()
        for step, peer in enumerate(self.place.peers):
            self.copy(step, me, peer).wait_send()


class Gather:
    def __init__(self, place, blocks, send, receive):
        self.place, self.blocks, self.send, self.receive = place, blocks, send, receive

    def copy(self, step, owner, half, device):
        if half is None:
            block = self.blocks.at[owner]
        else:
            block = self.blocks.at[owner, :, pl.ds(half * HALF, HALF)]
        return remote(block, block, self.send.at[step], self.receive.at[step], device)

    def other(self, owner):
        return owner + 1 - 2 * self.place.core

    def start(self):
        p = self.place
        self.copy(0, p.me, 0, p.right).start()
        self.copy(3, p.me, 1, p.left).start()
        self.copy(1, p.me, 1, p.right).start()
        self.copy(4, p.me, 0, p.left).start()
        self.copy(6, p.me, None, p.twin).start()

    def near(self):
        p = self.place
        self.copy(0, p.left, 0, p.me).wait_recv()
        self.copy(2, p.left, 0, p.right).start()
        self.copy(7, p.left, 0, p.twin).start()
        self.copy(3, p.right, 1, p.me).wait_recv()
        self.copy(5, p.right, 1, p.left).start()
        self.copy(8, p.right, 1, p.twin).start()
        self.copy(6, p.twin, None, p.me).wait_recv()

    def middle(self):
        p = self.place
        self.copy(1, p.left, 1, p.me).wait_recv()
        self.copy(9, p.left, 1, p.twin).start()
        self.copy(4, p.right, 0, p.me).wait_recv()
        self.copy(10, p.right, 0, p.twin).start()
        self.copy(7, self.other(p.left), 0, p.me).wait_recv()
        self.copy(8, self.other(p.right), 1, p.me).wait_recv()
        self.copy(9, self.other(p.left), 1, p.me).wait_recv()
        self.copy(10, self.other(p.right), 0, p.me).wait_recv()

    def last(self):
        p = self.place
        self.copy(2, p.far, 0, p.me).wait_recv()
        self.copy(11, p.far, 0, p.twin).start()
        self.copy(5, p.far, 1, p.me).wait_recv()
        self.copy(12, p.far, 1, p.twin).start()
        self.copy(11, self.other(p.far), 0, p.me).wait_recv()
        self.copy(12, self.other(p.far), 1, p.me).wait_recv()

    def end(self):
        p = self.place
        for step, owner, half, device in (
            (0, p.me, 0, p.right),
            (1, p.me, 1, p.right),
            (2, p.left, 0, p.right),
            (3, p.me, 1, p.left),
            (4, p.me, 0, p.left),
            (5, p.right, 1, p.left),
            (6, p.me, None, p.twin),
            (7, p.left, 0, p.twin),
            (8, p.right, 1, p.twin),
            (9, p.left, 1, p.twin),
            (10, p.right, 0, p.twin),
            (11, p.far, 0, p.twin),
            (12, p.far, 1, p.twin),
        ):
            self.copy(step, owner, half, device).wait_send()


GATHER_SEMS = 13


def pack(blocks, chip, whole):
    whole[chip, 0:NARROW, :] = blocks[2 * chip, 0:NARROW, :]
    whole[chip, NARROW : 2 * NARROW, :] = blocks[2 * chip + 1, 0:NARROW, :]


def enter_kernel(
    stream, vectors, weight, bias, turned, stats, whole, triple, blocks, tiles, total,
    tile_send, tile_receive, send, receive,
):
    place = Place()
    greet(place)
    values = stream[...].T
    turned[...] = values
    center = jnp.sum(values, 0, keepdims=True) / NARROW
    tiles[place.me, 0:1, :] = center
    tiles[place.me, 1:2, :] = jnp.sum(jnp.square(values - center), 0, keepdims=True)
    share = Share(place, tiles, tile_send, tile_receive)
    share.start()
    share.wait()
    centers = tiles[:, 0, :]
    center = jnp.sum(centers, 0, keepdims=True) / PARTS
    spread = jnp.sum(tiles[:, 1, :], 0, keepdims=True)
    spread += NARROW * jnp.sum(jnp.square(centers - center), 0, keepdims=True)
    scale = lax.rsqrt(spread / D + EPSILON)
    stats[0:1, :] = center
    stats[1:2, :] = scale
    low = (values - center) * scale * vectors[:, 0:1] + vectors[:, 1:2]
    blocks[place.me, 0:NARROW, :] = low.astype(BF)
    blocks[place.me, NARROW:ROWS, :] = jnp.zeros((ROWS - NARROW, LEN), BF)
    gather = Gather(place, blocks, send, receive)
    gather.start()

    def multiply(chip, first):
        pack(blocks, chip, whole)
        rows = pl.ds(pl.multiple_of(chip * 400, 16), 400)
        for tile in range(0, LEN, 256):
            term = dot_f(weight[rows, :], whole[chip, :, tile : tile + 256])
            if first:
                total[:, tile : tile + 256] = term + bias[...]
            else:
                total[:, tile : tile + 256] += term

    gather.near()
    multiply(place.chip, True)
    gather.middle()
    multiply(place.left_chip, False)
    multiply(place.right_chip, False)
    gather.last()
    pack(blocks, place.far_chip, whole)
    rows = pl.ds(pl.multiple_of(place.far_chip * 400, 16), 400)
    for tile in range(0, LEN, 256):
        term = dot_f(weight[rows, :], whole[place.far_chip, :, tile : tile + 256])
        triple[:, tile : tile + 256] = (total[:, tile : tile + 256] + term).astype(BF)
    gather.end()


def vmem(count):
    return [pl.BlockSpec(memory_space=pltpu.VMEM)] * count


def sems(count):
    return pltpu.SemaphoreType.DMA((count,))


def shape(dims, kind):
    return jax.ShapeDtypeStruct(dims, kind)


def params(collective):
    return pltpu.CompilerParams(
        collective_id=collective, has_side_effects=True, vmem_limit_bytes=VMEM_LIMIT
    )


def enter(stream, vectors, weight, bias):
    return pl.pallas_call(
        enter_kernel,
        out_shape=(
            shape((NARROW, LEN), F32),
            shape((8, LEN), F32),
            shape((4, 400, LEN), BF),
            shape((3 * WIN, LEN), BF),
        ),
        in_specs=vmem(4),
        out_specs=tuple(vmem(4)),
        scratch_shapes=[
            pltpu.VMEM((PARTS, ROWS, LEN), BF),
            pltpu.VMEM((PARTS, 8, LEN), F32),
            pltpu.VMEM((3 * WIN, LEN), F32),
            sems(7),
            sems(7),
            sems(GATHER_SEMS),
            sems(GATHER_SEMS),
        ],
        compiler_params=params(1),
        name="enter",
    )(stream, vectors, weight, bias)


class Reduce:
    def __init__(self, place, parts, twin, left_one, right_one, left_two, right_two, send, receive):
        self.place, self.parts, self.twin = place, parts, twin
        self.left_one, self.right_one = left_one, right_one
        self.left_two, self.right_two = left_two, right_two
        self.send, self.receive = send, receive
        self.order = [place.far_chip, place.right_chip, place.left_chip, place.chip]

    def copy(self, step):
        p = self.place
        low, high = pl.ds(0, HALF), pl.ds(HALF, HALF)
        if step < 4:
            chip = self.order[step]
            source = self.parts.at[2 * chip + 1 - p.core]
            target = self.twin.at[chip]
            device = p.twin
        elif step == 4:
            source, target, device = self.parts.at[p.far, :, low], self.left_one, p.right
        elif step == 5:
            source, target, device = self.parts.at[p.far, :, high], self.right_one, p.left
        elif step == 6:
            source, target, device = self.parts.at[p.right, :, high], self.left_two.at[:, high], p.right
        elif step == 7:
            source, target, device = self.parts.at[p.right, :, low], self.left_two.at[:, low], p.right
        elif step == 8:
            source, target, device = self.parts.at[p.left, :, low], self.right_two.at[:, low], p.left
        else:
            source, target, device = self.parts.at[p.left, :, high], self.right_two.at[:, high], p.left
        return remote(source, target, self.send.at[step], self.receive.at[step], device)

    def arrived(self, step):
        p = self.place
        low, high = pl.ds(0, HALF), pl.ds(HALF, HALF)
        if step < 4:
            target = self.twin.at[self.order[step]]
        else:
            target = (
                self.left_one,
                self.right_one,
                self.left_two.at[:, high],
                self.left_two.at[:, low],
                self.right_two.at[:, low],
                self.right_two.at[:, high],
            )[step - 4]
        remote(target, target, self.send.at[step], self.receive.at[step], p.me).wait_recv()

    def give(self, step):
        self.copy(step).start()

    def fold(self, step):
        self.arrived(step)
        chip = self.order[step]
        mine = 2 * chip + self.place.core
        self.parts[mine] = (self.parts[mine].astype(F32) + self.twin[chip].astype(F32)).astype(BF)

    def first(self):
        self.fold(0)
        self.copy(4).start()
        self.copy(5).start()

    def second(self):
        self.fold(1)
        self.copy(6).start()
        self.fold(2)
        self.copy(8).start()

    def third(self):
        p = self.place
        self.arrived(4)
        held = self.parts[p.right, :, 0:HALF].astype(F32)
        self.parts[p.right, :, 0:HALF] = (held + self.left_one[...].astype(F32)).astype(BF)
        self.copy(7).start()
        self.arrived(5)
        held = self.parts[p.left, :, HALF:LEN].astype(F32)
        self.parts[p.left, :, HALF:LEN] = (held + self.right_one[...].astype(F32)).astype(BF)
        self.copy(9).start()
        self.fold(3)

    def result(self):
        for step in range(6, 10):
            self.arrived(step)
        total = self.parts[self.place.me, 0:NARROW, :].astype(F32)
        total += self.left_two[0:NARROW, :].astype(F32)
        return total + self.right_two[0:NARROW, :].astype(F32)

    def end(self):
        for step in range(10):
            self.copy(step).wait_send()


REDUCE_SCRATCH = [
    pltpu.VMEM((PARTS, ROWS, LEN), BF),
    pltpu.VMEM((4, ROWS, LEN), BF),
    pltpu.VMEM((ROWS, HALF), BF),
    pltpu.VMEM((ROWS, HALF), BF),
    pltpu.VMEM((ROWS, LEN), BF),
    pltpu.VMEM((ROWS, LEN), BF),
    pltpu.SemaphoreType.DMA((10,)),
    pltpu.SemaphoreType.DMA((10,)),
]
GATHER_SCRATCH = [
    pltpu.VMEM((PARTS, ROWS, LEN), BF),
    pltpu.SemaphoreType.DMA((GATHER_SEMS,)),
    pltpu.SemaphoreType.DMA((GATHER_SEMS,)),
]
SHARE_SCRATCH = [
    pltpu.VMEM((PARTS, 8, LEN), F32),
    pltpu.SemaphoreType.DMA((7,)),
    pltpu.SemaphoreType.DMA((7,)),
]


def put_block(blocks, index, values):
    blocks[index, 0:NARROW, :] = values.astype(BF)
    blocks[index, NARROW:ROWS, :] = jnp.zeros((ROWS - NARROW, LEN), BF)


def put_parts(parts, chip, lanes, term):
    for core in range(2):
        parts[2 * chip + core, 0:NARROW, lanes] = term[core * NARROW : (core + 1) * NARROW].astype(BF)
        parts[2 * chip + core, NARROW:ROWS, lanes] = jnp.zeros((ROWS - NARROW, term.shape[1]), BF)


def put_grads(grads, index, lanes, term):
    for part in range(4):
        grads[index, part, 0:100, lanes] = term[100 * part : 100 * part + 100].astype(BF)


def head_count(place):
    return jnp.where(place.me == PARTS - 1, 4, 3)


def look_kernel(
    triple, cotangent, mixed, probs, cot_whole, cot_sum,
    blocks, send, receive,
):
    place = Place()
    greet(place)
    cot = cotangent[...].T
    cot_sum[...] = jnp.broadcast_to(jnp.sum(cot, 1, keepdims=True), (NARROW, 128))
    put_block(blocks, place.me, cot)
    gather = Gather(place, blocks, send, receive)
    gather.start()
    mixed[3 * HD : WIN, :] = jnp.zeros((HD, LEN), BF)

    def head(h, carry):
        at = pl.multiple_of(h * HD, HD)
        queries = triple[pl.ds(at, HD), :] * jnp.asarray(1 / math.sqrt(HD), BF)
        keys = triple[pl.ds(WIN + at, HD), :]
        values = triple[pl.ds(2 * WIN + at, HD), :]
        for tile in range(0, LEN, 256):
            reach = tile + 256
            scores = dot_f(keys[:, :reach], queries[:, tile:reach])
            key_place = lax.broadcasted_iota(jnp.int32, (reach, 256), 0)
            query_place = tile + lax.broadcasted_iota(jnp.int32, (reach, 256), 1)
            scores = jnp.where(key_place <= query_place, scores, -1e30)
            top = jnp.max(scores, 0, keepdims=True)
            weights = jnp.exp(scores - top)
            total = jnp.sum(weights, 0, keepdims=True)
            chances = (weights * (1.0 / total)).astype(BF)
            probs[h, 0:reach, tile:reach] = chances
            mixed[pl.ds(at, HD), tile:reach] = dot_n(values[:, :reach], chances).astype(BF)

        @pl.when(h == 0)
        def _():
            gather.near()
            pack(blocks, place.chip, cot_whole)

        @pl.when(h == 1)
        def _():
            gather.middle()
            pack(blocks, place.left_chip, cot_whole)
            pack(blocks, place.right_chip, cot_whole)

        return carry

    lax.fori_loop(0, head_count(place), head, 0)
    gather.last()
    pack(blocks, place.far_chip, cot_whole)
    gather.end()


def look(triple, cotangent):
    return pl.pallas_call(
        look_kernel,
        out_shape=(
            shape((WIN, LEN), BF),
            shape((4, LEN, LEN), BF),
            shape((4, 400, LEN), BF),
            shape((NARROW, 128), F32),
        ),
        in_specs=vmem(2),
        out_specs=tuple(vmem(4)),
        scratch_shapes=GATHER_SCRATCH,
        compiler_params=params(2),
        name="look",
    )(triple, cotangent)


def expand_kernel(
    mixed, mixer, turned, vectors, weight, bias,
    after, stats, whole, hidden, slope,
    total, *scratch,
):
    place = Place()
    greet(place)
    reduce = Reduce(place, *scratch[0:8])
    blocks, send, receive = scratch[8:11]
    tiles, tile_send, tile_receive = scratch[11:14]
    for step, chip in enumerate(reduce.order):
        rows = pl.ds(pl.multiple_of(chip * 400, 16), 400)
        put_parts(reduce.parts, chip, slice(0, LEN), dot_n(mixer[rows, :], mixed[...]))
        reduce.give(step)
    reduce.first()
    reduce.second()
    reduce.third()
    values = reduce.result() + turned[...] + vectors[:, 2:3]
    after[...] = values
    center = jnp.sum(values, 0, keepdims=True) / NARROW
    tiles[place.me, 0:1, :] = center
    tiles[place.me, 1:2, :] = jnp.sum(jnp.square(values - center), 0, keepdims=True)
    share = Share(place, tiles, tile_send, tile_receive)
    share.start()
    reduce.end()
    share.wait()
    centers = tiles[:, 0, :]
    center = jnp.sum(centers, 0, keepdims=True) / PARTS
    spread = jnp.sum(tiles[:, 1, :], 0, keepdims=True)
    spread += NARROW * jnp.sum(jnp.square(centers - center), 0, keepdims=True)
    scale = lax.rsqrt(spread / D + EPSILON)
    stats[0:1, :] = center
    stats[1:2, :] = scale
    put_block(blocks, place.me, (values - center) * scale * vectors[:, 3:4] + vectors[:, 4:5])
    gather = Gather(place, blocks, send, receive)
    gather.start()

    def multiply(chip, first):
        pack(blocks, chip, whole)
        rows = pl.ds(pl.multiple_of(chip * 400, 16), 400)
        for tile in range(0, LEN, 256):
            term = dot_f(weight[rows, :], whole[chip, :, tile : tile + 256])
            if first:
                total[:, tile : tile + 256] = term + bias[...]
            else:
                total[:, tile : tile + 256] += term

    gather.near()
    multiply(place.chip, True)
    gather.middle()
    multiply(place.left_chip, False)
    multiply(place.right_chip, False)
    gather.last()
    multiply(place.far_chip, False)
    gather.end()
    root = math.sqrt(2 / math.pi)
    for tile in range(0, LEN, 256):
        pre = total[:, tile : tile + 256]
        square = pre * pre
        bend = jnp.tanh(root * pre * (1 + 0.044715 * square))
        half = 0.5 * (1 + bend)
        hidden[:, tile : tile + 256] = (pre * half).astype(BF)
        curve = 0.5 * pre * (1 - bend * bend) * (root * (1 + 3 * 0.044715 * square))
        slope[:, tile : tile + 256] = (half + curve).astype(BF)


def expand(mixed, mixer, turned, vectors, weight, bias):
    return pl.pallas_call(
        expand_kernel,
        out_shape=(
            shape((NARROW, LEN), F32),
            shape((8, LEN), F32),
            shape((4, 400, LEN), BF),
            shape((FF // PARTS, LEN), BF),
            shape((FF // PARTS, LEN), BF),
        ),
        in_specs=vmem(6),
        out_specs=tuple(vmem(5)),
        scratch_shapes=[pltpu.VMEM((FF // PARTS, LEN), F32)]
        + REDUCE_SCRATCH
        + GATHER_SCRATCH
        + SHARE_SCRATCH,
        compiler_params=params(3),
        name="expand",
    )(mixed, mixer, turned, vectors, weight, bias)


def back_kernel(
    cot_whole, cotangent, hidden, slope, reducer, expander, second, after, stats, vectors, mixer,
    grad_after, after_whole, grad_mixed, grad_expand, grad_reduce, sums, expand_sum,
    low, total, *scratch,
):
    place = Place()
    greet(place)
    reduce = Reduce(place, *scratch[0:8])
    blocks, send, receive = scratch[8:11]
    tiles, tile_send, tile_receive = scratch[11:14]
    for tile in range(0, LEN, 256):
        lanes = slice(tile, tile + 256)
        grad_hidden = dot_n(reducer[...], cot_whole[:, :, lanes].reshape(D, 256))
        grad_pre = grad_hidden * slope[:, lanes].astype(F32)
        part = jnp.sum(grad_pre, 1, keepdims=True)
        if tile == 0:
            expand_sum[...] = jnp.broadcast_to(part, (FF // PARTS, 128))
        else:
            expand_sum[...] += jnp.broadcast_to(part, (FF // PARTS, 128))
        low[:, lanes] = grad_pre.astype(BF)
    for step, chip in enumerate(reduce.order):
        rows = pl.ds(pl.multiple_of(chip * 400, 16), 400)
        put_parts(reduce.parts, chip, slice(0, LEN), dot_n(expander[rows, :], low[...]))
        reduce.give(step)
        if step == 1:
            reduce.first()
    reduce.second()
    for chip in range(4):
        put_grads(grad_expand, chip, slice(0, 800), dot_t(second[chip], low[...]))
    reduce.third()
    for chip in range(4):
        put_grads(grad_reduce, chip, slice(0, 800), dot_t(cot_whole[chip], hidden[...]))
    grad = reduce.result()
    normed = (after[...] - stats[0:1, :]) * stats[1:2, :]
    scaled = grad * vectors[:, 3:4]
    tiles[place.me, 0:1, :] = jnp.sum(scaled, 0, keepdims=True)
    tiles[place.me, 1:2, :] = jnp.sum(scaled * normed, 0, keepdims=True)
    share = Share(place, tiles, tile_send, tile_receive)
    share.start()
    reduce.end()
    gain_sum = jnp.sum(grad * normed, 1, keepdims=True)
    shift_sum = jnp.sum(grad, 1, keepdims=True)
    share.wait()
    mean = jnp.sum(tiles[:, 0, :], 0, keepdims=True) / D
    along = jnp.sum(tiles[:, 1, :], 0, keepdims=True) / D
    back = stats[1:2, :] * (scaled - mean - normed * along) + cotangent[...].T
    grad_after[...] = back
    put_block(blocks, place.me, back)
    gather = Gather(place, blocks, send, receive)
    gather.start()
    sums[:, 0:1] = gain_sum
    sums[:, 1:2] = shift_sum
    sums[:, 2:3] = jnp.sum(back, 1, keepdims=True)

    def multiply(chip, first):
        pack(blocks, chip, after_whole)
        rows = pl.ds(pl.multiple_of(chip * 400, 16), 400)
        term = dot_f(mixer[rows, :], after_whole[chip])
        if first:
            total[...] = term
        else:
            total[...] += term

    gather.near()
    multiply(place.chip, True)
    gather.middle()
    multiply(place.left_chip, False)
    multiply(place.right_chip, False)
    gather.last()
    pack(blocks, place.far_chip, after_whole)
    rows = pl.ds(pl.multiple_of(place.far_chip * 400, 16), 400)
    grad_mixed[...] = (total[...] + dot_f(mixer[rows, :], after_whole[place.far_chip])).astype(BF)
    gather.end()


def back(cot_whole, cotangent, hidden, slope, reducer, expander, second, after, stats, vectors, mixer):
    return pl.pallas_call(
        back_kernel,
        out_shape=(
            shape((NARROW, LEN), F32),
            shape((4, 400, LEN), BF),
            shape((WIN, LEN), BF),
            shape((4, 4, DEEP, 800), BF),
            shape((4, 4, DEEP, 800), BF),
            shape((NARROW, 128), F32),
            shape((FF // PARTS, 128), F32),
        ),
        in_specs=vmem(11),
        out_specs=tuple(vmem(7)),
        scratch_shapes=[pltpu.VMEM((FF // PARTS, LEN), BF), pltpu.VMEM((WIN, LEN), F32)]
        + REDUCE_SCRATCH
        + GATHER_SCRATCH
        + SHARE_SCRATCH,
        compiler_params=params(4),
        name="back",
    )(cot_whole, cotangent, hidden, slope, reducer, expander, second, after, stats, vectors, mixer)


def attend_kernel(
    triple, probs, grad_mixed, mixed, reducer, hidden, after, vectors,
    result, grad_triple, own, sums,
    wide, edge, edge_in, keys_total, edge_send, edge_receive, *scratch,
):
    place = Place()
    greet(place)
    reduce = Reduce(place, *scratch[0:8])
    edge[3] = mixed[0:HD, :]
    previous = lax.rem(place.me + PARTS - 1, PARTS)
    following = lax.rem(place.me + 1, PARTS)

    def edge_copy(step, device):
        return remote(edge.at[step], edge_in.at[step], edge_send.at[step], edge_receive.at[step], device)

    edge_copy(3, previous).start()
    for tile in range(0, LEN, 256):
        lanes = slice(tile, tile + 256)
        term = dot_f(reducer[...], hidden[:, lanes])
        for chip in range(4):
            put_parts(reduce.parts, chip, lanes, term[400 * chip : 400 * chip + 400])
    for step in range(4):
        reduce.give(step)
    grad_triple[...] = jnp.zeros((3 * WIN, LEN), BF)
    root = jnp.asarray(1 / math.sqrt(HD), BF)

    def head(h, carry):
        at = pl.multiple_of(h * HD, HD)
        queries = triple[pl.ds(at, HD), :] * root
        keys = triple[pl.ds(WIN + at, HD), :]
        values = triple[pl.ds(2 * WIN + at, HD), :]
        grad_out = grad_mixed[pl.ds(at, HD), :]
        delta = jnp.sum(
            grad_out.astype(F32) * mixed[pl.ds(at, HD), :].astype(F32), 0, keepdims=True
        )
        for tile in range(LEN - 256, -1, -256):
            reach = tile + 256
            lanes = slice(tile, reach)
            chances = probs[h, 0:reach, lanes]
            grad_probs = dot_f(values[:, :reach], grad_out[:, lanes])
            grad_scores = (chances.astype(F32) * (grad_probs - delta[:, lanes])).astype(BF)
            grad_triple[pl.ds(at, HD), lanes] = (
                dot_n(keys[:, :reach], grad_scores) * (1 / math.sqrt(HD))
            ).astype(BF)
            key_term = dot_t(queries[:, lanes], grad_scores)
            value_term = dot_t(grad_out[:, lanes], chances)
            if reach == LEN:
                keys_total[0] = key_term
                keys_total[1] = value_term
            else:
                keys_total[0, :, 0:reach] += key_term
                keys_total[1, :, 0:reach] += value_term
        grad_triple[pl.ds(WIN + at, HD), :] = keys_total[0].astype(BF)
        grad_triple[pl.ds(2 * WIN + at, HD), :] = keys_total[1].astype(BF)

        @pl.when(h == 0)
        def _():
            for part in range(3):
                edge[part] = grad_triple[part * WIN : part * WIN + HD, :]
                edge_copy(part, previous).start()
            reduce.first()
            reduce.second()

        @pl.when(h == 1)
        def _():
            reduce.third()

        return carry

    lax.fori_loop(0, head_count(place), head, 0)
    total = reduce.result()
    reduce.end()
    for step in range(4):
        edge_copy(step, following).wait_recv()
        edge_copy(step, previous).wait_send()
    last = place.me == PARTS - 1
    for part in range(4):
        if part < 3:
            piece = grad_triple[part * WIN : (part + 1) * WIN, :].astype(F32)
        else:
            piece = mixed[...].astype(F32)
        wide[0 : 3 * HD, :] = piece[0 : 3 * HD]
        wide[3 * HD : WIN, :] = jnp.where(last, piece[3 * HD : WIN], edge_in[part].astype(F32))
        shifted = wide[pl.ds(pl.multiple_of(8 * place.me, 8), NARROW), :]
        own[part, 0:NARROW, :] = shifted.astype(BF)
        own[part, NARROW:ROWS, :] = jnp.zeros((ROWS - NARROW, LEN), BF)
        sums[:, part : part + 1] = jnp.sum(shifted, 1, keepdims=True)
    result[...] = (total + after[...] + vectors[:, 5:6]).T


def attend(triple, probs, grad_mixed, mixed, reducer, hidden, after, vectors):
    return pl.pallas_call(
        attend_kernel,
        out_shape=(
            shape((LEN, NARROW), F32),
            shape((3 * WIN, LEN), BF),
            shape((4, ROWS, LEN), BF),
            shape((NARROW, 128), F32),
        ),
        in_specs=vmem(8),
        out_specs=tuple(vmem(4)),
        scratch_shapes=[
            pltpu.VMEM((WIN, LEN), F32),
            pltpu.VMEM((4, HD, LEN), BF),
            pltpu.VMEM((4, HD, LEN), BF),
            pltpu.VMEM((2, HD, LEN), F32),
            sems(4),
            sems(4),
        ]
        + REDUCE_SCRATCH,
        compiler_params=params(5),
        name="attend",
    )(triple, probs, grad_mixed, mixed, reducer, hidden, after, vectors)


def leave_kernel(
    grad_triple, own, weight, first_whole, after_whole, turned, stats, grad_after, vectors,
    grad_stream, grad_weights, sums, *scratch,
):
    place = Place()
    greet(place)
    reduce = Reduce(place, *scratch[0:8])
    tiles, tile_send, tile_receive = scratch[8:11]
    for step, chip in enumerate(reduce.order):
        rows = pl.ds(pl.multiple_of(chip * 400, 16), 400)
        put_parts(reduce.parts, chip, slice(0, LEN), dot_n(weight[rows, :], grad_triple[...]))
        reduce.give(step)
        if step == 1:
            reduce.first()
    reduce.second()

    def weigh(chip):
        for part in range(4):
            acts = first_whole[chip] if part < 3 else after_whole[chip]
            term = dot_t(acts, own[part, 0:NARROW, :])
            put_grads(grad_weights, chip, slice(part * NARROW, (part + 1) * NARROW), term)

    weigh(0)
    weigh(1)
    reduce.third()
    weigh(2)
    weigh(3)
    grad = reduce.result()
    normed = (turned[...] - stats[0:1, :]) * stats[1:2, :]
    scaled = grad * vectors[:, 0:1]
    tiles[place.me, 0:1, :] = jnp.sum(scaled, 0, keepdims=True)
    tiles[place.me, 1:2, :] = jnp.sum(scaled * normed, 0, keepdims=True)
    share = Share(place, tiles, tile_send, tile_receive)
    share.start()
    reduce.end()
    sums[:, 0:1] = jnp.sum(grad * normed, 1, keepdims=True)
    sums[:, 1:2] = jnp.sum(grad, 1, keepdims=True)
    share.wait()
    mean = jnp.sum(tiles[:, 0, :], 0, keepdims=True) / D
    along = jnp.sum(tiles[:, 1, :], 0, keepdims=True) / D
    total = stats[1:2, :] * (scaled - mean - normed * along) + grad_after[...]
    grad_stream[...] = total.T


def leave(grad_triple, own, weight, first_whole, after_whole, turned, stats, grad_after, vectors):
    return pl.pallas_call(
        leave_kernel,
        out_shape=(
            shape((LEN, NARROW), F32),
            shape((4, 4, DEEP, 800), BF),
            shape((NARROW, 128), F32),
        ),
        in_specs=vmem(9),
        out_specs=tuple(vmem(3)),
        scratch_shapes=REDUCE_SCRATCH + SHARE_SCRATCH,
        compiler_params=params(6),
        name="leave",
    )(grad_triple, own, weight, first_whole, after_whole, turned, stats, grad_after, vectors)


class Spread:
    def __init__(self, grads, middle, first_in, second_in, first_axis, places, send, receive):
        self.grads, self.middle = grads, middle
        self.first_in, self.second_in = first_in, second_in
        self.first_axis, self.places = first_axis, places
        self.send, self.receive = send, receive

    def peer(self, axis, step):
        at = lax.rem(self.places[axis] + step, 4)
        z, y = (at, self.places["y"]) if axis == "z" else (self.places["z"], at)
        return at, z * 4 + y

    def copy(self, phase, step):
        axis = self.first_axis if phase == 0 else "zy".replace(self.first_axis, "")
        at, device = self.peer(axis, step)
        if phase == 1:
            source, target = self.middle.at[at], self.second_in.at[step - 1]
        else:
            source = self.grads.at[at] if axis == "z" else self.grads.at[:, at]
            target = self.first_in.at[step - 1]
        slot = 3 * phase + step - 1
        return pltpu.make_async_remote_copy(
            src_ref=source,
            dst_ref=target,
            send_sem=self.send.at[slot],
            recv_sem=self.receive.at[slot],
            device_id={"dp": device},
            device_id_type=MESH,
        )

    def start(self):
        for step in range(1, 4):
            self.copy(0, step).start()

    def turn(self):
        for step in range(1, 4):
            self.copy(0, step).wait_recv()
        at = self.places[self.first_axis]
        for part in range(4):
            if self.first_axis == "z":
                total = self.grads[at, part].astype(F32)
            else:
                total = self.grads[part, at].astype(F32)
            for step in range(3):
                total += self.first_in[step, part].astype(F32)
            self.middle[part] = total.astype(BF)
        for step in range(1, 4):
            self.copy(1, step).start()

    def result(self):
        for step in range(1, 4):
            self.copy(1, step).wait_recv()
        other = "zy".replace(self.first_axis, "")
        total = self.middle[self.places[other]].astype(F32)
        for step in range(3):
            total += self.second_in[step].astype(F32)
        return total[0:100]

    def end(self):
        for phase in range(2):
            for step in range(1, 4):
                self.copy(phase, step).wait_send()


def spread_scratch(width):
    return [
        pltpu.VMEM((4, DEEP, width), BF),
        pltpu.VMEM((3, 4, DEEP, width), BF),
        pltpu.VMEM((3, DEEP, width), BF),
        pltpu.SemaphoreType.DMA((6,)),
        pltpu.SemaphoreType.DMA((6,)),
    ]


def weights_kernel(
    grad_expand, grad_reduce, grad_rest, first_sums, second_sums, own_sums, expand_sum, cot_sum,
    out_triple, out_mixer, out_expand, out_reduce, out_vectors,
    table, table_send, table_receive, *scratch,
):
    group = lax.axis_index("dp")
    places = {"z": group // 4, "y": group % 4}
    barrier = pltpu.get_barrier_semaphore()
    peers = [lax.rem(group + i, 16) for i in range(1, 16)]
    for peer in peers:
        pl.semaphore_signal(barrier, inc=1, device_id={"dp": peer}, device_id_type=MESH)
    pl.semaphore_wait(barrier, 15)
    spreads = []
    for i, (grads, axis) in enumerate(((grad_expand, "z"), (grad_reduce, "y"), (grad_rest, "z"))):
        pieces = scratch[5 * i : 5 * i + 5]
        spreads.append(Spread(grads, *pieces[0:3], axis, places, *pieces[3:5]))
        spreads[-1].start()
    columns = [first_sums[:, 0:1], first_sums[:, 1:2], own_sums[:, 0:1], own_sums[:, 2:3],
               second_sums[:, 2:3], second_sums[:, 0:1], second_sums[:, 1:2], cot_sum[:, 0:1]]
    columns += [expand_sum[200 * i : 200 * i + 200, 0:1] for i in range(4)]
    place = lax.broadcasted_iota(jnp.int32, (NARROW, 128), 1)
    packed = jnp.zeros((NARROW, 128), F32)
    for i, column in enumerate(columns):
        packed = jnp.where(place == i, column, packed)
    table[group] = packed.T[0:16]

    def table_copy(step, owner, device):
        return pltpu.make_async_remote_copy(
            src_ref=table.at[owner],
            dst_ref=table.at[owner],
            send_sem=table_send.at[step],
            recv_sem=table_receive.at[step],
            device_id={"dp": device},
            device_id_type=MESH,
        )

    for step, peer in enumerate(peers):
        table_copy(step, group, peer).start()
    for spread in spreads:
        spread.turn()
    for step in range(15):
        table_copy(step, lax.rem(group + 15 - step, 16), group).wait_recv()
    out_vectors[...] = jnp.sum(table[...], 0)
    out_expand[...] = spreads[0].result()
    out_reduce[...] = spreads[1].result().T
    rest = spreads[2].result()
    for part in range(3):
        out_triple[part] = rest[:, part * NARROW : (part + 1) * NARROW]
    out_mixer[...] = rest[:, 3 * NARROW :].T
    for spread in spreads:
        spread.end()
    for step, peer in enumerate(peers):
        table_copy(step, group, peer).wait_send()


def weights(*sources):
    return pl.pallas_call(
        weights_kernel,
        out_shape=(
            shape((3, 100, NARROW), F32),
            shape((NARROW, 100), F32),
            shape((100, 800), F32),
            shape((800, 100), F32),
            shape((16, NARROW), F32),
        ),
        in_specs=vmem(8),
        out_specs=tuple(vmem(5)),
        scratch_shapes=[pltpu.VMEM((16, 16, NARROW), F32), sems(15), sems(15)]
        + spread_scratch(800) * 3,
        compiler_params=params(7),
        name="weights",
    )(*sources)


def shards(
    stream, first_gain, first_shift, triple_weight, triple_bias, mixer_weight, mixer_bias,
    second_gain, second_shift, expand_weight, expand_bias, reduce_weight, reduce_bias, cotangent,
):
    rank = lax.axis_index("mp")
    ring = [(i, (i + 1) % PARTS) for i in range(PARTS)]
    spare = WIN - NARROW
    bias_three = jnp.stack([triple_bias[0], jnp.zeros_like(triple_bias[0]), triple_bias[1]])
    tail_weight = lax.ppermute(triple_weight[:, :, NARROW - spare :].reshape(D, 3 * spare), "mp", ring)
    tail_bias = lax.ppermute(bias_three[:, NARROW - spare :], "mp", ring)
    tail_mixer = lax.ppermute(mixer_weight[NARROW - spare :], "mp", ring)
    begin = spare - 8 * rank

    def window(tail, own, axis):
        pads = [(0, 0)] * own.ndim
        pads[axis] = (0, spare)
        whole = jnp.pad(jnp.concatenate([tail, own], axis), pads)
        return lax.dynamic_slice_in_dim(whole, begin, WIN, axis)

    weight = window(tail_weight.reshape(D, 3, spare), triple_weight, 2).reshape(D, 3 * WIN)
    bias = window(tail_bias, bias_three, 1).reshape(3 * WIN, 1)
    mixer = window(tail_mixer, mixer_weight, 0).T
    vectors = jnp.stack(
        [first_gain, first_shift, mixer_bias, second_gain, second_shift, reduce_bias], 1
    )
    turned, first_stats, first_whole, triple = enter(stream, vectors, weight, bias)
    mixed, probs, cot_whole, cot_sum = look(triple, cotangent)
    after, second_stats, second_whole, hidden, slope = expand(
        mixed, mixer, turned, vectors, expand_weight, expand_bias.reshape(FF // PARTS, 1)
    )
    grad_after, after_whole, grad_mixed, grad_expand, grad_reduce, second_sums, expand_sum = back(
        cot_whole, cotangent, hidden, slope, reduce_weight, expand_weight, second_whole,
        after, second_stats, vectors, mixer,
    )
    result, grad_triple, own, own_sums = attend(
        triple, probs, grad_mixed, mixed, reduce_weight, hidden, after, vectors
    )
    grad_stream, grad_rest, first_sums = leave(
        grad_triple, own, weight, first_whole, after_whole, turned, first_stats, grad_after, vectors
    )
    out_triple, out_mixer, out_expand, out_reduce, sums = weights(
        grad_expand, grad_reduce, grad_rest, first_sums, second_sums, own_sums, expand_sum, cot_sum
    )
    return (
        result,
        grad_stream,
        sums[0],
        sums[1],
        out_triple.transpose(1, 0, 2),
        sums[2:4],
        out_mixer,
        sums[4],
        sums[5],
        sums[6],
        out_expand,
        sums[8:12].reshape(FF // PARTS),
        out_reduce,
        sums[7],
    )


def solution(mesh):
    placed = (
        P("dp", "mp"),
        P("mp"),
        P("mp"),
        P(None, None, "mp"),
        P(None, "mp"),
        P("mp", None),
        P("mp"),
        P("mp"),
        P("mp"),
        P(None, "mp"),
        P("mp"),
        P("mp", None),
        P("mp"),
        P("dp", "mp"),
    )
    return jax.shard_map(
        shards,
        mesh=mesh,
        in_specs=placed,
        out_specs=(
            P("dp", "mp"),
            P("dp", "mp"),
            P("mp"),
            P("mp"),
            P("dp", None, "mp"),
            P(None, "mp"),
            P("mp", "dp"),
            P("mp"),
            P("mp"),
            P("mp"),
            P("dp", "mp"),
            P("mp"),
            P("mp", "dp"),
            P("mp"),
        ),
        check_vma=False,
    )
```

```python
import math

import jax
import jax.numpy as jnp
from jax import lax
from jax.experimental import pallas as pl
from jax.experimental.pallas import tpu as pltpu
from jax.sharding import PartitionSpec as P

HD = 64
LEN = 1024
D = 1600
PARTS = 8
NARROW = D // PARTS
HIDDEN = 800
CHIP = 400
ROWS = 208
DEEP = 112
WIN = 256
TAIL = WIN - NARROW
HALF = LEN // 2
TILE = 256
EPSILON = 1e-05
ROOT = 1 / math.sqrt(HD)
MESH = pl.DeviceIdType.MESH
BF = jnp.bfloat16
F32 = jnp.float32
VMEM_LIMIT = 62 * 1024 * 1024


def dot_n(left, right):
    return lax.dot_general(left, right, (((1,), (0,)), ((), ())), preferred_element_type=F32)


def dot_t(left, right):
    return lax.dot_general(left, right, (((1,), (1,)), ((), ())), preferred_element_type=F32)


def dot_f(left, right):
    return lax.dot_general(left, right, (((0,), (0,)), ((), ())), preferred_element_type=F32)


class Place:
    def __init__(self):
        self.me = lax.axis_index("mp")
        self.chip = self.me // 2
        self.core = self.me % 2
        self.right_chip = lax.rem(self.chip + 1, 4)
        self.left_chip = lax.rem(self.chip + 3, 4)
        self.far_chip = lax.rem(self.chip + 2, 4)
        self.right = self.right_chip * 2 + self.core
        self.left = self.left_chip * 2 + self.core
        self.far = self.far_chip * 2 + self.core
        self.twin = self.chip * 2 + 1 - self.core
        self.peers = [lax.rem(self.me + i, PARTS) for i in range(1, PARTS)]
        self.previous = lax.rem(self.me + PARTS - 1, PARTS)
        self.following = lax.rem(self.me + 1, PARTS)
        self.last = self.me == PARTS - 1
        self.group = lax.axis_index("dp")
        self.at = {"z": self.group // 4, "y": self.group % 4}

    def along(self, axis, step):
        at = lax.rem(self.at[axis] + step, 4)
        z, y = (at, self.at["y"]) if axis == "z" else (self.at["z"], at)
        return at, z * 4 + y


def greet(devices):
    barrier = pltpu.get_barrier_semaphore()
    for device in devices:
        pl.semaphore_signal(barrier, inc=1, device_id=device, device_id_type=MESH)
    pl.semaphore_wait(barrier, len(devices))


def remote(source, target, sems, step, device, axis="mp"):
    send, receive = sems
    return pltpu.make_async_remote_copy(
        src_ref=source,
        dst_ref=target,
        send_sem=send.at[step],
        recv_sem=receive.at[step],
        device_id={axis: device},
        device_id_type=MESH,
    )


class Share:
    def __init__(self, place, tiles, sems, offset):
        self.place, self.tiles, self.sems, self.offset = place, tiles, sems, offset

    def copy(self, step, owner, device):
        tile = self.tiles.at[owner]
        return remote(tile, tile, self.sems, self.offset + step, device)

    def start(self, *vectors):
        rows = HALF // 128
        for i, vector in enumerate(vectors):
            for j in range(rows):
                piece = vector[:, 128 * j : 128 * j + 128]
                self.tiles[self.place.me, rows * i + j : rows * i + j + 1, :] = piece
        for step, peer in enumerate(self.place.peers):
            self.copy(step, self.place.me, peer).start()

    def wait(self):
        me = self.place.me
        for step in range(PARTS - 1):
            owner = lax.rem(me + PARTS - 1 - step, PARTS)
            self.copy(step, owner, me).wait_recv()
        for step, peer in enumerate(self.place.peers):
            self.copy(step, me, peer).wait_send()

    def read(self, index):
        rows = HALF // 128
        return jnp.concatenate([self.tiles[:, rows * index + j, :] for j in range(rows)], 1)


class Gather:
    COUNT = 13

    def __init__(self, place, blocks, half, sems, offset):
        self.place, self.blocks, self.base = place, blocks, half * HALF
        self.sems, self.offset = sems, offset

    def copy(self, step, owner, side, device):
        if side is None:
            lanes = pl.ds(self.base, HALF)
        else:
            lanes = pl.ds(self.base + side * TILE, TILE)
        block = self.blocks.at[owner, :, lanes]
        return remote(block, block, self.sems, self.offset + step, device)

    def other(self, owner):
        return owner + 1 - 2 * self.place.core

    def start(self):
        p = self.place
        self.copy(0, p.me, 0, p.right).start()
        self.copy(3, p.me, 1, p.left).start()
        self.copy(1, p.me, 1, p.right).start()
        self.copy(4, p.me, 0, p.left).start()
        self.copy(6, p.me, None, p.twin).start()

    def near(self):
        p = self.place
        self.copy(0, p.left, 0, p.me).wait_recv()
        self.copy(2, p.left, 0, p.right).start()
        self.copy(7, p.left, 0, p.twin).start()
        self.copy(3, p.right, 1, p.me).wait_recv()
        self.copy(5, p.right, 1, p.left).start()
        self.copy(8, p.right, 1, p.twin).start()
        self.copy(6, p.twin, None, p.me).wait_recv()

    def middle(self):
        p = self.place
        self.copy(1, p.left, 1, p.me).wait_recv()
        self.copy(9, p.left, 1, p.twin).start()
        self.copy(4, p.right, 0, p.me).wait_recv()
        self.copy(10, p.right, 0, p.twin).start()
        self.copy(7, self.other(p.left), 0, p.me).wait_recv()
        self.copy(8, self.other(p.right), 1, p.me).wait_recv()
        self.copy(9, self.other(p.left), 1, p.me).wait_recv()
        self.copy(10, self.other(p.right), 0, p.me).wait_recv()

    def far(self):
        p = self.place
        self.copy(2, p.far, 0, p.me).wait_recv()
        self.copy(11, p.far, 0, p.twin).start()
        self.copy(5, p.far, 1, p.me).wait_recv()
        self.copy(12, p.far, 1, p.twin).start()

    def last(self):
        p = self.place
        self.copy(11, self.other(p.far), 0, p.me).wait_recv()
        self.copy(12, self.other(p.far), 1, p.me).wait_recv()

    def end(self):
        p = self.place
        for step, owner, side, device in (
            (0, p.me, 0, p.right),
            (1, p.me, 1, p.right),
            (2, p.left, 0, p.right),
            (3, p.me, 1, p.left),
            (4, p.me, 0, p.left),
            (5, p.right, 1, p.left),
            (6, p.me, None, p.twin),
            (7, p.left, 0, p.twin),
            (8, p.right, 1, p.twin),
            (9, p.left, 1, p.twin),
            (10, p.right, 0, p.twin),
            (11, p.far, 0, p.twin),
            (12, p.far, 1, p.twin),
        ):
            self.copy(step, owner, side, device).wait_send()


class Reduce:
    COUNT = 10

    def __init__(self, place, buffers, half, sems, offset):
        self.place, self.base = place, half * HALF
        self.parts, self.twin, self.left_one, self.left_two, self.right_two = buffers
        self.right_one = self.left_one
        self.sems, self.offset = sems, offset
        self.order = [place.far_chip, place.right_chip, place.left_chip, place.chip]
        self.lanes = slice(self.base, self.base + HALF)
        self.low = slice(self.base, self.base + TILE)
        self.high = slice(self.base + TILE, self.base + HALF)

    def copy(self, step):
        p = self.place
        both, low, high = pl.ds(self.base, HALF), pl.ds(self.base, TILE), pl.ds(self.base + TILE, TILE)
        if step < 4:
            chip = self.order[step]
            source = self.parts.at[2 * chip + 1 - p.core, :, both]
            target = self.twin.at[chip, :, both]
            device = p.twin
        elif step == 4:
            source, target, device = self.parts.at[p.far, :, low], self.left_one.at[:, low], p.right
        elif step == 5:
            source, target, device = self.parts.at[p.far, :, high], self.right_one.at[:, high], p.left
        elif step == 6:
            source, target, device = self.parts.at[p.right, :, high], self.left_two.at[:, high], p.right
        elif step == 7:
            source, target, device = self.parts.at[p.right, :, low], self.left_two.at[:, low], p.right
        elif step == 8:
            source, target, device = self.parts.at[p.left, :, low], self.right_two.at[:, low], p.left
        else:
            source, target, device = self.parts.at[p.left, :, high], self.right_two.at[:, high], p.left
        return remote(source, target, self.sems, self.offset + step, device)

    def arrived(self, step):
        both, low, high = pl.ds(self.base, HALF), pl.ds(self.base, TILE), pl.ds(self.base + TILE, TILE)
        if step < 4:
            target = self.twin.at[self.order[step], :, both]
        else:
            target = (
                self.left_one.at[:, low],
                self.right_one.at[:, high],
                self.left_two.at[:, high],
                self.left_two.at[:, low],
                self.right_two.at[:, low],
                self.right_two.at[:, high],
            )[step - 4]
        remote(target, target, self.sems, self.offset + step, self.place.me).wait_recv()

    def put(self, chip, term):
        for core in range(2):
            rows = term[core * NARROW : (core + 1) * NARROW]
            self.parts[2 * chip + core, 0:NARROW, self.lanes] = rows.astype(BF)

    def give(self, step):
        self.copy(step).start()

    def fold(self, step):
        self.arrived(step)
        chip = self.order[step]
        mine = 2 * chip + self.place.core
        total = self.parts[mine, :, self.lanes].astype(F32) + self.twin[chip, :, self.lanes].astype(F32)
        self.parts[mine, :, self.lanes] = total.astype(BF)

    def first(self):
        self.fold(0)
        self.copy(4).start()
        self.copy(5).start()

    def second(self):
        self.fold(1)
        self.copy(6).start()
        self.fold(2)
        self.copy(8).start()

    def third(self):
        p = self.place
        self.arrived(4)
        held = self.parts[p.right, :, self.low].astype(F32)
        self.parts[p.right, :, self.low] = (held + self.left_one[:, self.low].astype(F32)).astype(BF)
        self.copy(7).start()
        self.arrived(5)
        held = self.parts[p.left, :, self.high].astype(F32)
        self.parts[p.left, :, self.high] = (held + self.right_one[:, self.high].astype(F32)).astype(BF)
        self.copy(9).start()
        self.fold(3)

    def result(self):
        for step in range(6, 10):
            self.arrived(step)
        total = self.parts[self.place.me, 0:NARROW, self.lanes].astype(F32)
        total += self.left_two[0:NARROW, self.lanes].astype(F32)
        return total + self.right_two[0:NARROW, self.lanes].astype(F32)

    def end(self):
        for step in range(10):
            self.copy(step).wait_send()


REDUCE_BUFFERS = [
    pltpu.VMEM((PARTS, ROWS, LEN), BF),
    pltpu.VMEM((4, ROWS, LEN), BF),
    pltpu.VMEM((ROWS, LEN), BF),
    pltpu.VMEM((ROWS, LEN), BF),
    pltpu.VMEM((ROWS, LEN), BF),
]


class Spread:
    COUNT = 6

    def __init__(self, place, grads, first_in, middle, second_in, axis, sems, offset):
        self.place, self.grads, self.first_in = place, grads, first_in
        self.middle, self.second_in = middle, second_in
        self.axis, self.other = axis, "zy".replace(axis, "")
        self.sems, self.offset = sems, offset

    def copy(self, phase, step):
        at, device = self.place.along(self.other if phase else self.axis, step)
        if phase == 1:
            source, target = self.middle.at[at], self.second_in.at[step - 1]
        else:
            source = self.grads.at[at] if self.axis == "z" else self.grads.at[:, at]
            target = self.first_in.at[step - 1]
        return remote(source, target, self.sems, self.offset + 3 * phase + step - 1, device, "dp")

    def start(self, phase):
        for step in range(1, 4):
            self.copy(phase, step).start()

    def arrive(self, phase):
        for step in range(1, 4):
            self.copy(phase, step).wait_recv()

    def leave(self, phase):
        for step in range(1, 4):
            self.copy(phase, step).wait_send()

    def turn(self, own):
        for part in range(4):
            total = own(part).astype(F32)
            for step in range(3):
                total += self.first_in[step, part].astype(F32)
            self.middle[part] = total.astype(BF)
        self.start(1)

    def result(self):
        self.arrive(1)
        total = self.middle[self.place.at[self.other]].astype(F32)
        for step in range(3):
            total += self.second_in[step].astype(F32)
        return total[0:100]


def pack(blocks, chip, whole, lanes):
    whole[chip, 0:NARROW, lanes] = blocks[2 * chip, 0:NARROW, lanes]
    whole[chip, NARROW:CHIP, lanes] = blocks[2 * chip + 1, 0:NARROW, lanes]


def put_grads(grads, index, lanes, term):
    for part in range(4):
        grads[index, part, 0:100, lanes] = term[100 * part : 100 * part + 100].astype(BF)


def column(vector, count):
    return jnp.broadcast_to(vector.reshape(1, count), (8, count)).T[:, 0:1]


def vmem(count):
    return [pl.BlockSpec(memory_space=pltpu.VMEM)] * count


def hbm(count):
    return [pl.BlockSpec(memory_space=pl.ANY)] * count


def sems(count):
    return pltpu.SemaphoreType.DMA((count,))


def shape(dims, kind):
    return jax.ShapeDtypeStruct(dims, kind)


def params(collective):
    return pltpu.CompilerParams(
        collective_id=collective, has_side_effects=True, vmem_limit_bytes=VMEM_LIMIT
    )


HALVES = (slice(0, HALF), slice(HALF, LEN))


def forward_kernel(
    stream, cot, first_gain, first_shift, triple_bias, mixer_bias, second_gain, second_shift, expand_bias,
    triple_weight, mixer_weight, expand_weight, reduce_weight,
    triple_out, probs_out, mixed_out, first_out, after_whole_out, parts_out, weight_out,
    in_expand, in_reduce, own_expand, own_reduce,
    after, grad_after, grad_mixed, stats, sums, expand_sum,
    triple_raw, mixer_raw, expand_raw, weight, mixer, expander,
    edge, edge_in, mixer_edge, mixer_edge_in, wide, land_one, land_two, whole, second_whole,
    total, triple, mixed, stage, hidden, low, grads_expand, grads_reduce, tiles,
    parts, twin, one_in, left_two, right_two,
    local, gather_send, gather_receive, reduce_send, reduce_receive, share_send, share_receive,
    edge_send, edge_receive, spread_send, spread_receive,
):
    place = Place()
    me = place.me

    def load(source, target, slot):
        copy = pltpu.make_async_copy(source, target, local.at[slot])
        copy.start()
        return copy

    mixer_load = load(mixer_weight, mixer_raw, 0)
    triple_load = load(triple_weight, triple_raw, 1)
    expand_load = load(expand_weight, expand_raw, 2)
    greet(
        [{"mp": peer} for peer in place.peers]
        + [{"dp": place.along(axis, step)[1]} for axis in "zy" for step in range(1, 4)]
    )
    gather_sems = (gather_send, gather_receive)
    edge_sems = (edge_send, edge_receive)
    shares = [Share(place, tiles.at[half], (share_send, share_receive), 7 * half) for half in range(2)]
    firsts = [Gather(place, land_one, half, gather_sems, 13 * half) for half in range(2)]
    cots = [Gather(place, land_two, half, gather_sems, 26 + 13 * half) for half in range(2)]
    buffers = (parts, twin, one_in, left_two, right_two)
    reduces = [Reduce(place, buffers, half, (reduce_send, reduce_receive), 10 * half) for half in range(2)]
    cot_whole = second_whole

    def send_center(half, values):
        center = jnp.sum(values, 0, keepdims=True) / NARROW
        shares[half].start(center, jnp.sum(jnp.square(values - center), 0, keepdims=True))

    def normal(half, values, gain, shift, row):
        share = shares[half]
        share.wait()
        centers, spreads = share.read(0), share.read(1)
        center = jnp.sum(centers, 0, keepdims=True) / PARTS
        spread = jnp.sum(spreads, 0, keepdims=True)
        spread += NARROW * jnp.sum(jnp.square(centers - center), 0, keepdims=True)
        scale = lax.rsqrt(spread / D + EPSILON)
        stats[row : row + 1, HALVES[half]] = center
        stats[row + 1 : row + 2, HALVES[half]] = scale
        low_values = (values - center) * scale * gain + shift
        land_one[me, 0:NARROW, HALVES[half]] = low_values.astype(BF)

    for half in range(2):
        send_center(half, stream[:, HALVES[half]])
    land_two[me, 0:NARROW, :] = cot[...].astype(BF)
    cots[0].start()
    mixer_load.wait()
    mixer_edge[0:TAIL, :] = mixer_raw[NARROW - TAIL : NARROW, :]
    mixer_edge_copy = remote(mixer_edge, mixer_edge_in, edge_sems, 2, place.following)
    mixer_edge_copy.start()
    gain, shift = column(first_gain[...], NARROW), column(first_shift[...], NARROW)
    normal(0, stream[:, HALVES[0]], gain, shift, 0)
    firsts[0].start()
    normal(1, stream[:, HALVES[1]], gain, shift, 0)
    sums[:, 3:4] = jnp.sum(cot[...], 1, keepdims=True)
    triple_load.wait()
    for chip in range(4):
        for part in range(3):
            weight[chip, part * NARROW : (part + 1) * NARROW, :] = triple_raw[
                part, :, chip * CHIP : (chip + 1) * CHIP
            ]
    weight_copy = load(weight, weight_out, 1)
    mixed[3 * HD : WIN, :] = jnp.zeros((HD, LEN), BF)

    def grow(lands, half, chip, target, factor, rows, first):
        pack(lands, chip, target, HALVES[half])
        term = dot_n(factor[chip], target[chip, :, HALVES[half]])
        if first:
            total[0:rows, HALVES[half]] = term
        else:
            total[0:rows, HALVES[half]] += term

    def grow_first(half, chip, first=False):
        grow(land_one, half, chip, whole, weight, 3 * NARROW, first)

    def edge_copy(half):
        lanes = pl.ds(half * HALF, HALF)
        return remote(edge.at[:, :, lanes], edge_in.at[:, :, lanes], edge_sems, half, place.following)

    biases = [column(triple_bias[0:1, :], NARROW), None, column(triple_bias[1:2, :], NARROW)]

    def place_triple(half):
        lanes = HALVES[half]
        for part in range(3):
            values = total[part * NARROW : (part + 1) * NARROW, lanes]
            if part != 1:
                values = values + biases[part]
            values = values.astype(BF)
            edge[part, 0:TAIL, lanes] = values[NARROW - TAIL : NARROW]
            wide[part, pl.ds(pl.multiple_of(TAIL + 8 * me, 8), NARROW), lanes] = values.astype(F32)
        edge_copy(half).start()
        for part in range(3):
            rows = slice(part * WIN + HD, (part + 1) * WIN)
            triple[rows, lanes] = wide[part, TAIL + HD : TAIL + WIN, lanes].astype(BF)

    def place_tail(half):
        lanes = HALVES[half]
        edge_copy(half).wait_recv()
        for part in range(3):
            tail = edge_in[part, 0:TAIL, lanes].astype(F32)
            wide[part, pl.ds(pl.multiple_of(8 * me, 8), TAIL), lanes] = tail
            rows = slice(part * WIN, part * WIN + HD)
            triple[rows, lanes] = wide[part, TAIL : TAIL + HD, lanes].astype(BF)

    pending = {}

    def look(half, h):
        for tile in (half * HALF, half * HALF + TILE):
            reach = tile + TILE
            lanes = slice(tile, reach)
            queries = triple[HD * h : HD * h + HD, lanes] * jnp.asarray(ROOT, BF)
            keys = triple[WIN + HD * h : WIN + HD * h + HD, 0:reach]
            values = triple[2 * WIN + HD * h : 2 * WIN + HD * h + HD, 0:reach]
            scores = dot_f(keys, queries)
            key_place = lax.broadcasted_iota(jnp.int32, (TILE, TILE), 0)
            query_place = lax.broadcasted_iota(jnp.int32, (TILE, TILE), 1)
            edge_scores = jnp.where(key_place <= query_place, scores[tile:reach], -1e30)
            top = jnp.max(edge_scores, 0, keepdims=True)
            if tile:
                top = jnp.maximum(top, jnp.max(scores[0:tile], 0, keepdims=True))
            edge_weights = jnp.exp(edge_scores - top)
            norm = jnp.sum(edge_weights, 0, keepdims=True)
            if tile:
                weights = jnp.exp(scores[0:tile] - top)
                norm += jnp.sum(weights, 0, keepdims=True)
            slot = 2 if h == 3 else (tile // TILE) % 2
            if slot in pending and h < 3:
                pending.pop(slot).wait()
            inverse = 1.0 / norm
            if tile:
                stage[slot, 0:tile, :] = (weights * inverse).astype(BF)
            stage[slot, tile:reach, :] = (edge_weights * inverse).astype(BF)
            copy = pltpu.make_async_copy(
                stage.at[slot, pl.ds(0, reach), :],
                probs_out.at[h, pl.ds(0, reach), pl.ds(tile, TILE)],
                local.at[4 + slot],
            )
            copy.start()
            mixed[HD * h : HD * h + HD, lanes] = dot_n(values, stage[slot, 0:reach, :]).astype(BF)
            if h == 3:
                copy.wait()
            else:
                pending[slot] = copy

    def look_last(half):
        @pl.when(place.last)
        def _():
            look(half, 3)

    def mix(half):
        for step, chip in enumerate(reduces[half].order):
            reduces[half].put(chip, dot_f(mixer[chip], mixed[:, HALVES[half]]))
            reduces[half].give(step)

    mixer_edge_copy.wait_recv()
    for chip in range(4):
        lanes = slice(chip * CHIP, (chip + 1) * CHIP)
        wide[0, :, 0:CHIP] = jnp.zeros((WIN + TAIL, CHIP), F32)
        wide[0, pl.ds(pl.multiple_of(8 * me, 8), TAIL), 0:CHIP] = mixer_edge_in[0:TAIL, lanes].astype(F32)
        rows = pl.ds(pl.multiple_of(TAIL + 8 * me, 8), NARROW)
        wide[0, rows, 0:CHIP] = mixer_raw[:, lanes].astype(F32)
        mixer[chip] = wide[0, TAIL : TAIL + WIN, 0:CHIP].astype(BF)

    firsts[0].near()
    firsts[1].start()
    cots[0].near()
    grow_first(0, place.chip, True)
    firsts[0].middle()
    grow_first(0, place.left_chip)
    grow_first(0, place.right_chip)
    firsts[0].far()
    firsts[1].near()
    firsts[0].last()
    grow_first(0, place.far_chip)
    place_triple(0)
    cots[0].middle()
    grow_first(1, place.chip, True)
    look(0, 1)
    firsts[1].middle()
    grow_first(1, place.left_chip)
    grow_first(1, place.right_chip)
    cots[0].far()
    look(0, 2)
    firsts[1].far()
    place_tail(0)
    look(0, 0)
    look_last(0)
    firsts[1].last()
    grow_first(1, place.far_chip)
    place_triple(1)
    mix(0)
    cots[1].start()
    first_copy = load(whole, first_out, 7)
    cots[0].last()
    look(1, 1)
    reduces[0].first()
    look(1, 2)
    reduces[0].second()
    cots[1].near()
    place_tail(1)
    look(1, 0)
    reduces[0].third()
    look_last(1)
    mix(1)
    expand_load.wait()
    for chip in range(4):
        expander[chip] = expand_raw[:, chip * CHIP : (chip + 1) * CHIP]
    reducer = expand_raw
    reduce_load = load(reduce_weight, reducer, 3)
    cots[1].middle()
    for chip in range(4):
        pack(land_two, chip, cot_whole, HALVES[0])
    triple_copy = load(triple, triple_out, 8)
    mixed_copy = load(mixed, mixed_out, 9)

    mixer_shift = column(mixer_bias[...], NARROW)
    gain, shift = column(second_gain[...], NARROW), column(second_shift[...], NARROW)

    def add_mixed(half):
        values = reduces[half].result() + stream[:, HALVES[half]] + mixer_shift
        after[:, HALVES[half]] = values
        send_center(half, values)

    def grow_second(half, chip, first=False):
        grow(land_one, half, chip, whole, expander, HIDDEN, first)

    def pull(half):
        grad = dot_n(reducer[...], cot_whole[:, :, HALVES[half]].reshape(D, HALF))
        low[:, HALVES[half]] = grad.astype(BF)

    bias_column = column(expand_bias[...], HIDDEN)
    bend_root = math.sqrt(2 / math.pi)

    def bend(half):
        for tile in (half * HALF, half * HALF + TILE):
            lanes = slice(tile, tile + TILE)
            pre = total[:, lanes] + bias_column
            square = pre * pre
            curve = jnp.tanh(bend_root * pre * (1 + 0.044715 * square))
            middle = 0.5 * (1 + curve)
            hidden[:, lanes] = (pre * middle).astype(BF)
            slope = middle + 0.5 * pre * (1 - curve * curve) * (bend_root * (1 + 3 * 0.044715 * square))
            grad_pre = low[:, lanes].astype(F32) * slope
            row_sums = jnp.broadcast_to(jnp.sum(grad_pre, 1, keepdims=True), (HIDDEN, 128))
            if tile:
                expand_sum[...] += row_sums
            else:
                expand_sum[...] = row_sums
            low[:, lanes] = grad_pre.astype(BF)

    def fall(half):
        for step, chip in enumerate(reduces[half].order):
            reduces[half].put(chip, dot_f(expander[chip], low[:, HALVES[half]]))
            reduces[half].give(step)
            if step == 1:
                reduces[half].first()

    firsts[0].end()
    add_mixed(0)
    reduces[1].first()
    reduces[1].second()
    cots[1].far()
    normal(0, after[:, HALVES[0]], gain, shift, 2)
    firsts[0].start()
    reduces[1].third()
    first_copy.wait()
    cots[1].last()
    for chip in range(4):
        pack(land_two, chip, cot_whole, HALVES[1])
    reduce_load.wait()
    pull(0)
    firsts[0].near()
    firsts[1].end()
    add_mixed(1)
    grow_second(0, place.chip, True)
    normal(1, after[:, HALVES[1]], gain, shift, 2)
    firsts[1].start()
    firsts[0].middle()
    grow_second(0, place.left_chip)
    grow_second(0, place.right_chip)
    firsts[0].far()
    pull(1)
    firsts[0].last()
    grow_second(0, place.far_chip)
    reduces[0].end()
    bend(0)
    firsts[1].near()
    fall(0)
    grow_second(1, place.chip, True)
    firsts[1].middle()
    reduces[0].second()
    grow_second(1, place.left_chip)
    grow_second(1, place.right_chip)
    firsts[1].far()
    reduces[0].third()
    firsts[1].last()
    grow_second(1, place.far_chip)
    reduces[1].end()
    bend(1)
    fall(1)

    spread_sems = (spread_send, spread_receive)
    spread_expand = Spread(place, grads_expand, in_expand, None, None, "z", spread_sems, 0)
    spread_reduce = Spread(place, grads_reduce, in_reduce, None, None, "y", spread_sems, 3)
    second_whole_now = whole

    for chip in range(2):
        put_grads(grads_reduce, chip, slice(0, HIDDEN), dot_t(cot_whole[chip], hidden[...]))
    reduces[1].second()

    def back_start(half):
        lanes = HALVES[half]
        grad = reduces[half].result()
        normed = (after[:, lanes] - stats[2:3, lanes]) * stats[3:4, lanes]
        scaled = grad * gain
        shares[half].start(jnp.sum(scaled, 0, keepdims=True), jnp.sum(scaled * normed, 0, keepdims=True))
        gain_sum = jnp.sum(grad * normed, 1, keepdims=True)
        shift_sum = jnp.sum(grad, 1, keepdims=True)
        if half:
            sums[:, 0:1] += gain_sum
            sums[:, 1:2] += shift_sum
        else:
            sums[:, 0:1] = gain_sum
            sums[:, 1:2] = shift_sum
        grad_after[:, lanes] = scaled

    def back_end(half):
        lanes = HALVES[half]
        share = shares[half]
        share.wait()
        mean = jnp.sum(share.read(0), 0, keepdims=True) / D
        along = jnp.sum(share.read(1), 0, keepdims=True) / D
        normed = (after[:, lanes] - stats[2:3, lanes]) * stats[3:4, lanes]
        grad = stats[3:4, lanes] * (grad_after[:, lanes] - mean - normed * along) + cot[:, lanes]
        grad_after[:, lanes] = grad
        land_two[me, 0:NARROW, lanes] = grad.astype(BF)
        total_sum = jnp.sum(grad, 1, keepdims=True)
        if half:
            sums[:, 2:3] += total_sum
        else:
            sums[:, 2:3] = total_sum

    for chip in range(2, 4):
        put_grads(grads_reduce, chip, slice(0, HIDDEN), dot_t(cot_whole[chip], hidden[...]))
    spread_reduce.start(0)
    cots[0].end()
    back_start(0)
    reduces[1].third()
    back_end(0)
    cots[0].start()
    for chip in range(4):
        put_grads(grads_expand, chip, slice(0, HIDDEN), dot_t(second_whole_now[chip], low[...]))
    spread_expand.start(0)
    cots[0].near()
    cots[1].end()
    back_start(1)
    back_end(1)
    cots[1].start()
    reduces[0].end()
    reduces[1].end()
    after_whole = second_whole

    def grow_mixed(half, chip, first=False, last=False):
        lanes = HALVES[half]
        pack(land_two, chip, after_whole, lanes)
        term = dot_n(mixer[chip], after_whole[chip, :, lanes])
        if first:
            total[0:WIN, lanes] = term
        elif last:
            grad_mixed[:, lanes] = (total[0:WIN, lanes] + term).astype(BF)
        else:
            total[0:WIN, lanes] += term

    def back_result(half):
        for tile in (half * HALF, half * HALF + TILE):
            term = dot_f(reducer[...], hidden[:, tile : tile + TILE])
            for index in range(PARTS):
                rows = slice(index * NARROW, (index + 1) * NARROW)
                parts[index, 0:NARROW, tile : tile + TILE] = term[rows].astype(BF)

    own_at = {"z": place.at["z"], "y": place.at["y"]}
    grow_mixed(0, place.chip, True)
    cots[0].middle()
    grow_mixed(0, place.left_chip)
    grow_mixed(0, place.right_chip)
    cots[0].far()
    back_result(0)
    cots[1].near()
    cots[0].last()
    grow_mixed(0, place.far_chip, False, True)
    grow_mixed(1, place.chip, True)
    back_result(1)
    parts_copy = load(parts, parts_out, 10)
    cots[1].middle()
    grow_mixed(1, place.left_chip)
    grow_mixed(1, place.right_chip)
    own_copies = [
        load(grads_expand.at[own_at["z"]], own_expand, 0),
        load(grads_reduce.at[:, own_at["y"]], own_reduce, 2),
    ]
    cots[1].far()
    cots[1].last()
    grow_mixed(1, place.far_chip, False, True)
    after_copy = load(after_whole, after_whole_out, 3)
    for gather in firsts + cots:
        gather.end()
    mixer_edge_copy.wait_send()
    for half in range(2):
        edge_copy(half).wait_send()
    for spread in (spread_reduce, spread_expand):
        spread.arrive(0)
        spread.leave(0)
    for copy in (weight_copy, triple_copy, mixed_copy, parts_copy, *own_copies, after_copy, *pending.values()):
        copy.wait()


def forward(*arguments):
    wide_rows = WIN + TAIL
    return pl.pallas_call(
        forward_kernel,
        out_shape=(
            shape((3 * WIN, LEN), BF),
            shape((4, LEN, LEN), BF),
            shape((WIN, LEN), BF),
            shape((4, CHIP, LEN), BF),
            shape((4, CHIP, LEN), BF),
            shape((PARTS, ROWS, LEN), BF),
            shape((4, 3 * NARROW, CHIP), BF),
            shape((3, 4, DEEP, HIDDEN), BF),
            shape((3, 4, DEEP, HIDDEN), BF),
            shape((4, DEEP, HIDDEN), BF),
            shape((4, DEEP, HIDDEN), BF),
            shape((NARROW, LEN), F32),
            shape((NARROW, LEN), F32),
            shape((WIN, LEN), BF),
            shape((8, LEN), F32),
            shape((NARROW, 128), F32),
            shape((HIDDEN, 128), F32),
        ),
        in_specs=vmem(9) + hbm(4),
        out_specs=tuple(hbm(11) + vmem(6)),
        scratch_shapes=[
            pltpu.VMEM((3, NARROW, D), BF),
            pltpu.VMEM((NARROW, D), BF),
            pltpu.VMEM((HIDDEN, D), BF),
            pltpu.VMEM((4, 3 * NARROW, CHIP), BF),
            pltpu.VMEM((4, WIN, CHIP), BF),
            pltpu.VMEM((4, HIDDEN, CHIP), BF),
            pltpu.VMEM((3, HD, LEN), BF),
            pltpu.VMEM((3, HD, LEN), BF),
            pltpu.VMEM((HD, D), BF),
            pltpu.VMEM((HD, D), BF),
            pltpu.VMEM((3, WIN + TAIL, LEN), F32),
            pltpu.VMEM((PARTS, ROWS, LEN), BF),
            pltpu.VMEM((PARTS, ROWS, LEN), BF),
            pltpu.VMEM((4, CHIP, LEN), BF),
            pltpu.VMEM((4, CHIP, LEN), BF),
            pltpu.VMEM((HIDDEN, LEN), F32),
            pltpu.VMEM((3 * WIN, LEN), BF),
            pltpu.VMEM((WIN, LEN), BF),
            pltpu.VMEM((3, LEN, TILE), BF),
            pltpu.VMEM((HIDDEN, LEN), BF),
            pltpu.VMEM((HIDDEN, LEN), BF),
            pltpu.VMEM((4, 4, DEEP, HIDDEN), BF),
            pltpu.VMEM((4, 4, DEEP, HIDDEN), BF),
            pltpu.VMEM((2, PARTS, 8, 128), F32),
            *REDUCE_BUFFERS,
            sems(11),
            sems(52),
            sems(52),
            sems(20),
            sems(20),
            sems(14),
            sems(14),
            sems(3),
            sems(3),
            sems(6),
            sems(6),
        ],
        compiler_params=params(1),
        name="forward",
    )(*arguments)


VECTORS = 12


def backward_kernel(
    stream, after, grad_after, stats, first_gain, reduce_bias, second_sums, expand_sum,
    triple_in, probs_in, mixed_in, grad_mixed_in, first_in, after_in, parts_in, weight_in,
    in_expand, in_reduce, own_expand, own_reduce,
    result, grad_stream, out_triple, out_mixer, out_expand, out_reduce,
    out_gain, out_shift, out_bias, out_mixer_bias, out_second_gain, out_second_shift, out_expand_bias,
    out_reduce_bias,
    triple, probs, mixed, grad_mixed, first_whole, after_whole, weight,
    grad_triple, own, wide, edge, edge_in, keys_total, grads, tiles, sums, table,
    parts_one, twin_one, one_in, left_two, right_two,
    parts_two, twin_two, two_in, left_four, right_four,
    expand_first, expand_own, expand_middle, expand_second,
    reduce_first, reduce_own, reduce_middle, reduce_second,
    rest_first, rest_middle, rest_second,
    local, probs_sems, reduce_send, reduce_receive, share_send, share_receive, edge_send, edge_receive,
    spread_send, spread_receive, table_send, table_receive,
):
    place = Place()
    me = place.me
    group = place.group

    def load(source, target, slot):
        copy = pltpu.make_async_copy(source, target, local.at[slot])
        copy.start()
        return copy

    triple_load = load(triple_in, triple, 0)
    grad_mixed_load = load(grad_mixed_in, grad_mixed, 1)
    mixed_load = load(mixed_in, mixed, 2)

    def probs_copy(h, tile):
        reach = tile + TILE
        return pltpu.make_async_copy(
            probs_in.at[h, pl.ds(0, reach), pl.ds(tile, TILE)],
            probs.at[h, pl.ds(0, reach), pl.ds(tile, TILE)],
            probs_sems.at[4 * h + tile // TILE],
        )

    tiles_of = ((TILE, 0), (3 * TILE, 2 * TILE))

    def probs_load(half, h):
        for tile in tiles_of[half]:
            probs_copy(h, tile).start()

    probs_load(1, 0)
    parts_load = load(parts_in, parts_one, 3)
    probs_load(1, 1)
    probs_load(1, 2)

    @pl.when(place.last)
    def _():
        probs_load(1, 3)

    weight_load = load(weight_in, weight, 4)
    for h in range(3):
        probs_load(0, h)

    @pl.when(place.last)
    def _():
        probs_load(0, 3)

    spread_loads = [
        load(in_reduce, reduce_first, 5),
        load(own_reduce, reduce_own, 6),
        load(in_expand, expand_first, 7),
        load(own_expand, expand_own, 8),
    ]
    first_load = load(first_in, first_whole, 9)
    after_load = load(after_in, after_whole, 10)
    others = [lax.rem(group + i, 16) for i in range(1, 16)]
    greet([{"mp": peer} for peer in place.peers] + [{"dp": other} for other in others])
    reduce_sems = (reduce_send, reduce_receive)
    edge_sems = (edge_send, edge_receive)
    spread_sems = (spread_send, spread_receive)
    shares = [Share(place, tiles.at[half], (share_send, share_receive), 7 * half) for half in range(2)]
    one = (parts_one, twin_one, one_in, left_two, right_two)
    two = (parts_two, twin_two, two_in, left_four, right_four)
    outs = [Reduce(place, one, half, reduce_sems, 10 * half) for half in range(2)]
    reduces = [Reduce(place, two, half, reduce_sems, 20 + 10 * half) for half in range(2)]
    spread_expand = Spread(
        place, None, expand_first, expand_middle, expand_second, "z", spread_sems, 0
    )
    spread_reduce = Spread(
        place, None, reduce_first, reduce_middle, reduce_second, "y", spread_sems, 6
    )
    spread_rest = Spread(place, grads, rest_first, rest_middle, rest_second, "z", spread_sems, 12)

    def edge_copy(step):
        if step == 2:
            piece, target = edge.at[3], edge_in.at[3]
        else:
            lanes = pl.ds(step * HALF, HALF)
            piece, target = edge.at[0:3, :, lanes], edge_in.at[0:3, :, lanes]
        return remote(piece, target, edge_sems, step, place.previous)

    mixed_load.wait()
    edge[3] = mixed[0:HD, :]
    edge_copy(2).start()
    grad_triple[...] = jnp.zeros((3 * WIN, LEN), BF)
    triple_load.wait()
    grad_mixed_load.wait()

    def attend(half, h):
        row = HD * h
        keys = triple[WIN + row : WIN + row + HD, :]
        values = triple[2 * WIN + row : 2 * WIN + row + HD, :]
        for tile in reversed(tiles_of[half]) if half == 0 else tiles_of[half]:
            probs_copy(h, tile).wait()
        for tile in tiles_of[half]:
            reach = tile + TILE
            lanes = slice(tile, reach)
            queries = triple[row : row + HD, lanes] * jnp.asarray(ROOT, BF)
            grad_out = grad_mixed[row : row + HD, lanes]
            delta = jnp.sum(
                grad_out.astype(F32) * mixed[row : row + HD, lanes].astype(F32), 0, keepdims=True
            )
            chances = probs[h, 0:reach, lanes]
            grad_probs = dot_f(values[:, 0:reach], grad_out)
            grad_scores = (chances.astype(F32) * (grad_probs - delta)).astype(BF)
            grad_queries = dot_n(keys[:, 0:reach], grad_scores) * ROOT
            grad_triple[row : row + HD, lanes] = grad_queries.astype(BF)
            key_term = dot_t(queries, grad_scores)
            value_term = dot_t(grad_out, chances)
            if reach == LEN:
                keys_total[h, 0] = key_term
                keys_total[h, 1] = value_term
            else:
                keys_total[h, 0, :, 0:reach] += key_term
                keys_total[h, 1, :, 0:reach] += value_term
        lanes = HALVES[half]
        grad_triple[WIN + row : WIN + row + HD, lanes] = keys_total[h, 0, :, lanes].astype(BF)
        grad_triple[2 * WIN + row : 2 * WIN + row + HD, lanes] = keys_total[h, 1, :, lanes].astype(BF)

    def attend_last(half):
        @pl.when(place.last)
        def _():
            attend(half, 3)

    def send_edge(half):
        for part in range(3):
            edge[part, :, HALVES[half]] = grad_triple[part * WIN : part * WIN + HD, HALVES[half]]
        edge_copy(half).start()

    def place_own(part, lanes):
        if part < 3:
            piece = grad_triple[part * WIN : (part + 1) * WIN, lanes]
        else:
            piece = mixed[:, lanes]
        piece = piece.astype(F32)
        wide[0 : 3 * HD, lanes] = piece[0 : 3 * HD]
        neighbour = edge_in[part, :, lanes].astype(F32)
        wide[3 * HD : WIN, lanes] = jnp.where(place.last, piece[3 * HD : WIN], neighbour)
        values = wide[pl.ds(pl.multiple_of(8 * me, 8), NARROW), lanes]
        own[part * NARROW : (part + 1) * NARROW, lanes] = values.astype(BF)
        return jnp.sum(values, 1, keepdims=True)

    def fall(half):
        edge_copy(half).wait_recv()
        for part in range(3):
            total = place_own(part, HALVES[half])
            if half == 1:
                sums[:, 2 + part : 3 + part] = total
            else:
                sums[:, 2 + part : 3 + part] += total
        for step, chip in enumerate(reduces[half].order):
            reduces[half].put(chip, dot_f(weight[chip], own[0 : 3 * NARROW, HALVES[half]]))
            reduces[half].give(step)
            if step == 1:
                reduces[half].first()

    parts_load.wait()
    for half in range(2):
        for step in range(4):
            outs[half].give(step)
    attend(1, 0)
    send_edge(1)
    outs[1].first()
    outs[0].first()
    outs[1].second()
    outs[0].second()
    attend(1, 1)
    outs[1].third()
    outs[0].third()
    attend(1, 2)
    attend_last(1)
    weight_load.wait()
    fall(1)
    for copy in spread_loads:
        copy.wait()
    spread_reduce.turn(lambda part: reduce_own[part])
    spread_expand.turn(lambda part: expand_own[part])
    reduces[1].second()
    attend(0, 0)
    send_edge(0)
    attend(0, 1)
    reduces[1].third()
    attend(0, 2)
    attend_last(0)
    fall(0)
    edge_copy(2).wait_recv()
    place_own(3, slice(0, LEN))
    first_load.wait()
    after_load.wait()

    def weigh(chip):
        for part in range(4):
            acts = first_whole[chip] if part < 3 else after_whole[chip]
            rows = slice(part * NARROW, (part + 1) * NARROW)
            put_grads(grads, chip, rows, dot_t(acts, own[rows, :]))

    weigh(0)
    reduces[0].second()
    weigh(1)
    weigh(2)
    reduces[0].third()
    weigh(3)
    spread_rest.start(0)
    gain = column(first_gain[...], NARROW)
    shift = column(reduce_bias[...], NARROW)

    def back_start(half):
        lanes = HALVES[half]
        grad = reduces[half].result()
        normed = (stream[:, lanes] - stats[0:1, lanes]) * stats[1:2, lanes]
        scaled = grad * gain
        shares[half].start(jnp.sum(scaled, 0, keepdims=True), jnp.sum(scaled * normed, 0, keepdims=True))
        gain_sum = jnp.sum(grad * normed, 1, keepdims=True)
        shift_sum = jnp.sum(grad, 1, keepdims=True)
        if half == 1:
            sums[:, 0:1] = gain_sum
            sums[:, 1:2] = shift_sum
        else:
            sums[:, 0:1] += gain_sum
            sums[:, 1:2] += shift_sum
        grad_stream[:, lanes] = scaled

    def back_end(half):
        lanes = HALVES[half]
        share = shares[half]
        share.wait()
        mean = jnp.sum(share.read(0), 0, keepdims=True) / D
        along = jnp.sum(share.read(1), 0, keepdims=True) / D
        normed = (stream[:, lanes] - stats[0:1, lanes]) * stats[1:2, lanes]
        back = stats[1:2, lanes] * (grad_stream[:, lanes] - mean - normed * along)
        grad_stream[:, lanes] = back + grad_after[:, lanes]

    back_start(1)
    for half in range(2):
        result[:, HALVES[half]] = outs[half].result() + after[:, HALVES[half]] + shift
    out_expand[...] = spread_expand.result()
    out_reduce[...] = spread_reduce.result()
    back_end(1)
    back_start(0)
    columns = [
        sums[:, 0:1], sums[:, 1:2], sums[:, 2:3], sums[:, 4:5],
        second_sums[:, 2:3], second_sums[:, 0:1], second_sums[:, 1:2], second_sums[:, 3:4],
    ]
    columns += [expand_sum[NARROW * i : NARROW * (i + 1), 0:1] for i in range(4)]
    spot = lax.broadcasted_iota(jnp.int32, (NARROW, 128), 1)
    packed = jnp.zeros((NARROW, 128), F32)
    for i, values in enumerate(columns):
        packed = jnp.where(spot == i, values, packed)
    table[group] = packed.T[0:16]

    def table_copy(step, owner, device):
        return remote(table.at[owner], table.at[owner], (table_send, table_receive), step, device, "dp")

    for step, other in enumerate(others):
        table_copy(step, group, other).start()
    back_end(0)
    spread_rest.arrive(0)
    spread_rest.turn(lambda part: grads[place.at["z"], part])
    for step in range(15):
        table_copy(step, lax.rem(group + 15 - step, 16), group).wait_recv()
    vectors = jnp.sum(table[...], 0)
    out_gain[...] = vectors[0:1].reshape(NARROW)
    out_shift[...] = vectors[1:2].reshape(NARROW)
    out_bias[...] = vectors[2:4]
    out_mixer_bias[...] = vectors[4:5].reshape(NARROW)
    out_second_gain[...] = vectors[5:6].reshape(NARROW)
    out_second_shift[...] = vectors[6:7].reshape(NARROW)
    out_reduce_bias[...] = vectors[7:8].reshape(NARROW)
    out_expand_bias[...] = vectors[8:12]
    rest = spread_rest.result()
    for part in range(3):
        out_triple[part] = rest[:, part * NARROW : (part + 1) * NARROW].T
    out_mixer[...] = rest[:, 3 * NARROW :].T
    for reduce in outs + reduces:
        reduce.end()
    for step in range(3):
        edge_copy(step).wait_send()
    for spread in (spread_expand, spread_reduce, spread_rest):
        spread.leave(1)
    spread_rest.leave(0)
    for step, other in enumerate(others):
        table_copy(step, group, other).wait_send()


def backward(*arguments):
    width = 4 * NARROW
    return pl.pallas_call(
        backward_kernel,
        out_shape=(
            shape((NARROW, LEN), F32),
            shape((NARROW, LEN), F32),
            shape((3, NARROW, 100), F32),
            shape((NARROW, 100), F32),
            shape((100, HIDDEN), F32),
            shape((100, HIDDEN), F32),
            shape((NARROW,), F32),
            shape((NARROW,), F32),
            shape((2, NARROW), F32),
            shape((NARROW,), F32),
            shape((NARROW,), F32),
            shape((NARROW,), F32),
            shape((4, NARROW), F32),
            shape((NARROW,), F32),
        ),
        in_specs=vmem(8) + hbm(12),
        out_specs=tuple(vmem(14)),
        scratch_shapes=[
            pltpu.VMEM((3 * WIN, LEN), BF),
            pltpu.VMEM((4, LEN, LEN), BF),
            pltpu.VMEM((WIN, LEN), BF),
            pltpu.VMEM((WIN, LEN), BF),
            pltpu.VMEM((4, CHIP, LEN), BF),
            pltpu.VMEM((4, CHIP, LEN), BF),
            pltpu.VMEM((4, 3 * NARROW, CHIP), BF),
            pltpu.VMEM((3 * WIN, LEN), BF),
            pltpu.VMEM((width, LEN), BF),
            pltpu.VMEM((WIN, LEN), F32),
            pltpu.VMEM((4, HD, LEN), BF),
            pltpu.VMEM((4, HD, LEN), BF),
            pltpu.VMEM((4, 2, HD, LEN), F32),
            pltpu.VMEM((4, 4, DEEP, width), BF),
            pltpu.VMEM((2, PARTS, 8, 128), F32),
            pltpu.VMEM((NARROW, 128), F32),
            pltpu.VMEM((16, 16, NARROW), F32),
            *REDUCE_BUFFERS,
            *REDUCE_BUFFERS,
            pltpu.VMEM((3, 4, DEEP, HIDDEN), BF),
            pltpu.VMEM((4, DEEP, HIDDEN), BF),
            pltpu.VMEM((4, DEEP, HIDDEN), BF),
            pltpu.VMEM((3, DEEP, HIDDEN), BF),
            pltpu.VMEM((3, 4, DEEP, HIDDEN), BF),
            pltpu.VMEM((4, DEEP, HIDDEN), BF),
            pltpu.VMEM((4, DEEP, HIDDEN), BF),
            pltpu.VMEM((3, DEEP, HIDDEN), BF),
            pltpu.VMEM((3, 4, DEEP, width), BF),
            pltpu.VMEM((4, DEEP, width), BF),
            pltpu.VMEM((3, DEEP, width), BF),
            sems(11),
            sems(16),
            sems(40),
            sems(40),
            sems(14),
            sems(14),
            sems(3),
            sems(3),
            sems(18),
            sems(18),
            sems(15),
            sems(15),
        ],
        compiler_params=params(2),
        name="backward",
    )(*arguments)


def shards(
    stream, first_gain, first_shift, triple_weight, triple_bias, mixer_weight, mixer_bias,
    second_gain, second_shift, expand_weight, expand_bias, reduce_weight, reduce_bias, cotangent,
):
    turned = stream.T
    (
        triple, probs, mixed, first_whole, after_whole, parts, weight,
        in_expand, in_reduce, own_expand, own_reduce,
        after, grad_after, grad_mixed, stats, sums, expand_sum,
    ) = forward(
        turned, cotangent.T, first_gain, first_shift, triple_bias, mixer_bias, second_gain, second_shift,
        expand_bias, triple_weight.transpose(1, 2, 0), mixer_weight, expand_weight.T, reduce_weight,
    )
    (
        result, grad_stream, out_triple, out_mixer, out_expand, out_reduce,
        out_gain, out_shift, out_bias, out_mixer_bias, out_second_gain, out_second_shift, out_expand_bias,
        out_reduce_bias,
    ) = backward(
        turned, after, grad_after, stats, first_gain, reduce_bias, sums, expand_sum,
        triple, probs, mixed, grad_mixed, first_whole, after_whole, parts, weight,
        in_expand, in_reduce, own_expand, own_reduce,
    )
    return (
        result.T,
        grad_stream.T,
        out_gain,
        out_shift,
        out_triple.transpose(2, 0, 1),
        out_bias,
        out_mixer,
        out_mixer_bias,
        out_second_gain,
        out_second_shift,
        out_expand,
        out_expand_bias.reshape(HIDDEN),
        out_reduce.T,
        out_reduce_bias,
    )


def solution(mesh):
    placed = (
        P("dp", "mp"),
        P("mp"),
        P("mp"),
        P(None, None, "mp"),
        P(None, "mp"),
        P("mp", None),
        P("mp"),
        P("mp"),
        P("mp"),
        P(None, "mp"),
        P("mp"),
        P("mp", None),
        P("mp"),
        P("dp", "mp"),
    )
    return jax.shard_map(
        shards,
        mesh=mesh,
        in_specs=placed,
        out_specs=(
            P("dp", "mp"),
            P("dp", "mp"),
            P("mp"),
            P("mp"),
            P("dp", None, "mp"),
            P(None, "mp"),
            P("mp", "dp"),
            P("mp"),
            P("mp"),
            P("mp"),
            P("dp", "mp"),
            P("mp"),
            P("mp", "dp"),
            P("mp"),
        ),
        check_vma=False,
    )
```

```python
import math

import jax
import jax.numpy as jnp
from jax import lax
from jax.experimental import pallas as pl
from jax.experimental.pallas import tpu as pltpu
from jax.sharding import PartitionSpec as P

HD = 64
LEN = 1024
D = 1600
PARTS = 8
NARROW = D // PARTS
HIDDEN = 800
CHIP = 400
ROWS = 208
DEEP = 112
SPLIT = 208
WIN = 256
TAIL = WIN - NARROW
HALF = LEN // 2
TILE = 256
EPSILON = 1e-05
ROOT = 1 / math.sqrt(HD)
MESH = pl.DeviceIdType.MESH
BF = jnp.bfloat16
F32 = jnp.float32
VMEM_LIMIT = 62 * 1024 * 1024


def dot_n(left, right):
    return lax.dot_general(left, right, (((1,), (0,)), ((), ())), preferred_element_type=F32)


def dot_t(left, right):
    return lax.dot_general(left, right, (((1,), (1,)), ((), ())), preferred_element_type=F32)


def dot_f(left, right):
    return lax.dot_general(left, right, (((0,), (0,)), ((), ())), preferred_element_type=F32)


class Place:
    def __init__(self):
        self.me = lax.axis_index("mp")
        self.chip = self.me // 2
        self.core = self.me % 2
        self.right_chip = lax.rem(self.chip + 1, 4)
        self.left_chip = lax.rem(self.chip + 3, 4)
        self.far_chip = lax.rem(self.chip + 2, 4)
        self.right = self.right_chip * 2 + self.core
        self.left = self.left_chip * 2 + self.core
        self.far = self.far_chip * 2 + self.core
        self.twin = self.chip * 2 + 1 - self.core
        self.peers = [lax.rem(self.me + i, PARTS) for i in range(1, PARTS)]
        self.previous = lax.rem(self.me + PARTS - 1, PARTS)
        self.following = lax.rem(self.me + 1, PARTS)
        self.last = self.me == PARTS - 1
        self.group = lax.axis_index("dp")
        self.at = {"z": self.group // 4, "y": self.group % 4}

    def along(self, axis, step):
        at = lax.rem(self.at[axis] + step, 4)
        z, y = (at, self.at["y"]) if axis == "z" else (self.at["z"], at)
        return at, z * 4 + y


def greet(devices):
    barrier = pltpu.get_barrier_semaphore()
    for device in devices:
        pl.semaphore_signal(barrier, inc=1, device_id=device, device_id_type=MESH)
    pl.semaphore_wait(barrier, len(devices))


def remote(source, target, sems, step, device, axis="mp"):
    send, receive = sems
    return pltpu.make_async_remote_copy(
        src_ref=source,
        dst_ref=target,
        send_sem=send.at[step],
        recv_sem=receive.at[step],
        device_id={axis: device},
        device_id_type=MESH,
    )


class Share:
    def __init__(self, place, tiles, sems, offset):
        self.place, self.tiles, self.sems, self.offset = place, tiles, sems, offset

    def copy(self, step, owner, device):
        tile = self.tiles.at[owner]
        return remote(tile, tile, self.sems, self.offset + step, device)

    def start(self, *vectors):
        rows = HALF // 128
        for i, vector in enumerate(vectors):
            for j in range(rows):
                piece = vector[:, 128 * j : 128 * j + 128]
                self.tiles[self.place.me, rows * i + j : rows * i + j + 1, :] = piece
        for step, peer in enumerate(self.place.peers):
            self.copy(step, self.place.me, peer).start()

    def wait(self):
        me = self.place.me
        for step in range(PARTS - 1):
            owner = lax.rem(me + PARTS - 1 - step, PARTS)
            self.copy(step, owner, me).wait_recv()
        for step, peer in enumerate(self.place.peers):
            self.copy(step, me, peer).wait_send()

    def read(self, index):
        rows = HALF // 128
        return jnp.concatenate([self.tiles[:, rows * index + j, :] for j in range(rows)], 1)


class Gather:
    COUNT = 13

    def __init__(self, place, blocks, half, sems, offset):
        self.place, self.blocks, self.base = place, blocks, half * HALF
        self.sems, self.offset = sems, offset

    def copy(self, step, owner, side, device):
        if side is None:
            lanes = pl.ds(self.base, HALF)
        else:
            lanes = pl.ds(self.base + side * TILE, TILE)
        block = self.blocks.at[owner, :, lanes]
        return remote(block, block, self.sems, self.offset + step, device)

    def other(self, owner):
        return owner + 1 - 2 * self.place.core

    def start(self):
        p = self.place
        self.copy(0, p.me, 0, p.right).start()
        self.copy(3, p.me, 1, p.left).start()
        self.copy(1, p.me, 1, p.right).start()
        self.copy(4, p.me, 0, p.left).start()
        self.copy(6, p.me, None, p.twin).start()

    def near(self):
        p = self.place
        self.copy(0, p.left, 0, p.me).wait_recv()
        self.copy(2, p.left, 0, p.right).start()
        self.copy(7, p.left, 0, p.twin).start()
        self.copy(3, p.right, 1, p.me).wait_recv()
        self.copy(5, p.right, 1, p.left).start()
        self.copy(8, p.right, 1, p.twin).start()
        self.copy(6, p.twin, None, p.me).wait_recv()

    def middle(self):
        p = self.place
        self.copy(1, p.left, 1, p.me).wait_recv()
        self.copy(9, p.left, 1, p.twin).start()
        self.copy(4, p.right, 0, p.me).wait_recv()
        self.copy(10, p.right, 0, p.twin).start()
        self.copy(7, self.other(p.left), 0, p.me).wait_recv()
        self.copy(8, self.other(p.right), 1, p.me).wait_recv()
        self.copy(9, self.other(p.left), 1, p.me).wait_recv()
        self.copy(10, self.other(p.right), 0, p.me).wait_recv()

    def far(self):
        p = self.place
        self.copy(2, p.far, 0, p.me).wait_recv()
        self.copy(11, p.far, 0, p.twin).start()
        self.copy(5, p.far, 1, p.me).wait_recv()
        self.copy(12, p.far, 1, p.twin).start()

    def last(self):
        p = self.place
        self.copy(11, self.other(p.far), 0, p.me).wait_recv()
        self.copy(12, self.other(p.far), 1, p.me).wait_recv()

    def end(self):
        p = self.place
        for step, owner, side, device in (
            (0, p.me, 0, p.right),
            (1, p.me, 1, p.right),
            (2, p.left, 0, p.right),
            (3, p.me, 1, p.left),
            (4, p.me, 0, p.left),
            (5, p.right, 1, p.left),
            (6, p.me, None, p.twin),
            (7, p.left, 0, p.twin),
            (8, p.right, 1, p.twin),
            (9, p.left, 1, p.twin),
            (10, p.right, 0, p.twin),
            (11, p.far, 0, p.twin),
            (12, p.far, 1, p.twin),
        ):
            self.copy(step, owner, side, device).wait_send()


class Reduce:
    COUNT = 10

    def __init__(self, place, buffers, half, sems, offset):
        self.place, self.base = place, half * HALF
        self.parts, self.twin, self.left_one, self.left_two, self.right_two = buffers
        self.right_one = self.left_one
        self.sems, self.offset = sems, offset
        self.order = [place.far_chip, place.right_chip, place.left_chip, place.chip]
        self.lanes = slice(self.base, self.base + HALF)
        self.low = slice(self.base, self.base + TILE)
        self.high = slice(self.base + TILE, self.base + HALF)

    def copy(self, step):
        p = self.place
        both, low, high = pl.ds(self.base, HALF), pl.ds(self.base, TILE), pl.ds(self.base + TILE, TILE)
        if step < 4:
            chip = self.order[step]
            source = self.parts.at[2 * chip + 1 - p.core, :, both]
            target = self.twin.at[chip, :, both]
            device = p.twin
        elif step == 4:
            source, target, device = self.parts.at[p.far, :, low], self.left_one.at[:, low], p.right
        elif step == 5:
            source, target, device = self.parts.at[p.far, :, high], self.right_one.at[:, high], p.left
        elif step == 6:
            source, target, device = self.parts.at[p.right, :, high], self.left_two.at[:, high], p.right
        elif step == 7:
            source, target, device = self.parts.at[p.right, :, low], self.left_two.at[:, low], p.right
        elif step == 8:
            source, target, device = self.parts.at[p.left, :, low], self.right_two.at[:, low], p.left
        else:
            source, target, device = self.parts.at[p.left, :, high], self.right_two.at[:, high], p.left
        return remote(source, target, self.sems, self.offset + step, device)

    def arrived(self, step):
        both, low, high = pl.ds(self.base, HALF), pl.ds(self.base, TILE), pl.ds(self.base + TILE, TILE)
        if step < 4:
            target = self.twin.at[self.order[step], :, both]
        else:
            target = (
                self.left_one.at[:, low],
                self.right_one.at[:, high],
                self.left_two.at[:, high],
                self.left_two.at[:, low],
                self.right_two.at[:, low],
                self.right_two.at[:, high],
            )[step - 4]
        remote(target, target, self.sems, self.offset + step, self.place.me).wait_recv()

    def put(self, chip, term):
        for core in range(2):
            rows = term[core * NARROW : (core + 1) * NARROW]
            self.parts[2 * chip + core, 0:NARROW, self.lanes] = rows.astype(BF)

    def give(self, step):
        self.copy(step).start()

    def fold(self, step):
        self.arrived(step)
        chip = self.order[step]
        mine = 2 * chip + self.place.core
        total = self.parts[mine, :, self.lanes].astype(F32) + self.twin[chip, :, self.lanes].astype(F32)
        self.parts[mine, :, self.lanes] = total.astype(BF)

    def first(self):
        self.fold(0)
        self.copy(4).start()
        self.copy(5).start()

    def second(self):
        self.fold(1)
        self.copy(6).start()
        self.fold(2)
        self.copy(8).start()

    def third(self):
        p = self.place
        self.arrived(4)
        held = self.parts[p.right, :, self.low].astype(F32)
        self.parts[p.right, :, self.low] = (held + self.left_one[:, self.low].astype(F32)).astype(BF)
        self.copy(7).start()
        self.arrived(5)
        held = self.parts[p.left, :, self.high].astype(F32)
        self.parts[p.left, :, self.high] = (held + self.right_one[:, self.high].astype(F32)).astype(BF)
        self.copy(9).start()
        self.fold(3)

    def result(self):
        for step in range(6, 10):
            self.arrived(step)
        total = self.parts[self.place.me, 0:NARROW, self.lanes].astype(F32)
        total += self.left_two[0:NARROW, self.lanes].astype(F32)
        return total + self.right_two[0:NARROW, self.lanes].astype(F32)

    def end(self):
        for step in range(10):
            self.copy(step).wait_send()


REDUCE_BUFFERS = [
    pltpu.VMEM((PARTS, ROWS, LEN), BF),
    pltpu.VMEM((4, ROWS, LEN), BF),
    pltpu.VMEM((ROWS, LEN), BF),
    pltpu.VMEM((ROWS, LEN), BF),
    pltpu.VMEM((ROWS, LEN), BF),
]


class Spread:
    COUNT = 9

    def __init__(self, place, axis, grads, passing, up, down, middle, second_in, sems, offset):
        self.place, self.axis, self.other = place, axis, "zy".replace(axis, "")
        self.grads, self.passing, self.up, self.down = grads, passing, up, down
        self.middle, self.second_in = middle, second_in
        self.sems, self.offset = sems, offset

    def copy(self, step):
        low, high = pl.ds(0, SPLIT), pl.ds(SPLIT, CHIP - SPLIT)
        if step < 6:
            away, rows, target, way = (
                (2, low, self.passing, 1),
                (2, high, self.passing, 3),
                (1, high, self.up, 1),
                (3, low, self.down, 3),
                (1, low, self.up, 1),
                (3, high, self.down, 3),
            )[step]
            source = self.grads.at[self.place.along(self.axis, away)[0], rows]
            device = self.place.along(self.axis, way)[1]
            target = target.at[rows]
        else:
            at, device = self.place.along(self.other, step - 5)
            source, target = self.middle.at[at], self.second_in.at[step - 6]
        return remote(source, target, self.sems, self.offset + step, device, "dp")

    def start(self):
        for step in range(4):
            self.copy(step).start()

    def pass_on(self):
        for step, away, rows in ((0, 1, slice(0, SPLIT)), (1, 3, slice(SPLIT, CHIP))):
            self.copy(step).wait_recv()
            block = self.place.along(self.axis, away)[0]
            total = self.grads[block, rows].astype(F32) + self.passing[rows].astype(F32)
            self.grads[block, rows] = total.astype(BF)
            self.copy(step + 4).start()

    def arrive(self):
        for step in range(2, 6):
            self.copy(step).wait_recv()

    def turn(self, own):
        total = own.astype(F32) + self.up[...].astype(F32) + self.down[...].astype(F32)
        for part in range(4):
            self.middle[part, 0:100] = total[100 * part : 100 * part + 100].astype(BF)
        for step in range(6, 9):
            self.copy(step).start()

    def result(self):
        for step in range(6, 9):
            self.copy(step).wait_recv()
        total = self.middle[self.place.at[self.other], 0:100].astype(F32)
        for step in range(3):
            total += self.second_in[step, 0:100].astype(F32)
        return total

    def leave(self, steps):
        for step in steps:
            self.copy(step).wait_send()


def pack(blocks, chip, whole, lanes):
    whole[chip, 0:NARROW, lanes] = blocks[2 * chip, 0:NARROW, lanes]
    whole[chip, NARROW:CHIP, lanes] = blocks[2 * chip + 1, 0:NARROW, lanes]


def put_grads(grads, axis, chip, term):
    if axis == "z":
        grads[chip] = term.astype(BF)
    else:
        for part in range(4):
            grads[part, 100 * chip : 100 * chip + 100] = term[100 * part : 100 * part + 100].astype(BF)


def column(vector, count):
    return jnp.broadcast_to(vector.reshape(1, count), (8, count)).T[:, 0:1]


def vmem(count):
    return [pl.BlockSpec(memory_space=pltpu.VMEM)] * count


def hbm(count):
    return [pl.BlockSpec(memory_space=pl.ANY)] * count


def sems(count):
    return pltpu.SemaphoreType.DMA((count,))


def shape(dims, kind):
    return jax.ShapeDtypeStruct(dims, kind)


def params(collective):
    return pltpu.CompilerParams(
        collective_id=collective, has_side_effects=True, vmem_limit_bytes=VMEM_LIMIT
    )


HALVES = (slice(0, HALF), slice(HALF, LEN))


def forward_kernel(
    stream, cot, first_gain, first_shift, triple_bias, mixer_bias, second_gain, second_shift, expand_bias,
    triple_weight, mixer_weight, expand_weight, reduce_weight,
    triple_out, probs_out, mixed_out, first_out, after_whole_out, parts_out, weight_out,
    own_expand, up_expand, down_expand, own_reduce, up_reduce, down_reduce,
    after, grad_after, grad_mixed, stats, sums, expand_sum,
    triple_raw, mixer_raw, expand_raw, weight, mixer, expander,
    edge, edge_in, mixer_edge, mixer_edge_in, wide, land_one, land_two, whole, second_whole,
    total, triple, mixed, stage, hidden, low, grads_expand, grads_reduce, passing_expand, passing_reduce, tiles,
    parts, twin, one_in, left_two, right_two,
    local, gather_send, gather_receive, reduce_send, reduce_receive, share_send, share_receive,
    edge_send, edge_receive, spread_send, spread_receive,
):
    place = Place()
    me = place.me

    def load(source, target, slot):
        copy = pltpu.make_async_copy(source, target, local.at[slot])
        copy.start()
        return copy

    mixer_load = load(mixer_weight, mixer_raw, 0)
    triple_load = load(triple_weight, triple_raw, 1)
    expand_load = load(expand_weight, expand_raw, 2)
    greet(
        [{"mp": peer} for peer in place.peers]
        + [{"dp": place.along(axis, step)[1]} for axis in "zy" for step in range(1, 4)]
    )
    gather_sems = (gather_send, gather_receive)
    edge_sems = (edge_send, edge_receive)
    shares = [Share(place, tiles.at[half], (share_send, share_receive), 7 * half) for half in range(2)]
    firsts = [Gather(place, land_one, half, gather_sems, 13 * half) for half in range(2)]
    cots = [Gather(place, land_two, half, gather_sems, 26 + 13 * half) for half in range(2)]
    buffers = (parts, twin, one_in, left_two, right_two)
    reduces = [Reduce(place, buffers, half, (reduce_send, reduce_receive), 10 * half) for half in range(2)]
    cot_whole = second_whole

    def send_center(half, values):
        center = jnp.sum(values, 0, keepdims=True) / NARROW
        shares[half].start(center, jnp.sum(jnp.square(values - center), 0, keepdims=True))

    def normal(half, values, gain, shift, row):
        share = shares[half]
        share.wait()
        centers, spreads = share.read(0), share.read(1)
        center = jnp.sum(centers, 0, keepdims=True) / PARTS
        spread = jnp.sum(spreads, 0, keepdims=True)
        spread += NARROW * jnp.sum(jnp.square(centers - center), 0, keepdims=True)
        scale = lax.rsqrt(spread / D + EPSILON)
        stats[row : row + 1, HALVES[half]] = center
        stats[row + 1 : row + 2, HALVES[half]] = scale
        low_values = (values - center) * scale * gain + shift
        land_one[me, 0:NARROW, HALVES[half]] = low_values.astype(BF)

    for half in range(2):
        send_center(half, stream[:, HALVES[half]])
    land_two[me, 0:NARROW, :] = cot[...].astype(BF)
    cots[0].start()
    mixer_load.wait()
    mixer_edge[0:TAIL, :] = mixer_raw[NARROW - TAIL : NARROW, :]
    mixer_edge_copy = remote(mixer_edge, mixer_edge_in, edge_sems, 2, place.following)
    mixer_edge_copy.start()
    gain, shift = column(first_gain[...], NARROW), column(first_shift[...], NARROW)
    normal(0, stream[:, HALVES[0]], gain, shift, 0)
    firsts[0].start()
    normal(1, stream[:, HALVES[1]], gain, shift, 0)
    sums[:, 3:4] = jnp.sum(cot[...], 1, keepdims=True)
    triple_load.wait()
    for chip in range(4):
        for part in range(3):
            weight[chip, part * NARROW : (part + 1) * NARROW, :] = triple_raw[
                part, :, chip * CHIP : (chip + 1) * CHIP
            ]
    weight_copy = load(weight, weight_out, 1)
    mixed[3 * HD : WIN, :] = jnp.zeros((HD, LEN), BF)

    def grow(lands, half, chip, target, factor, rows, first):
        pack(lands, chip, target, HALVES[half])
        term = dot_n(factor[chip], target[chip, :, HALVES[half]])
        if first:
            total[0:rows, HALVES[half]] = term
        else:
            total[0:rows, HALVES[half]] += term

    def grow_first(half, chip, first=False):
        grow(land_one, half, chip, whole, weight, 3 * NARROW, first)

    def edge_copy(half):
        lanes = pl.ds(half * HALF, HALF)
        return remote(edge.at[:, :, lanes], edge_in.at[:, :, lanes], edge_sems, half, place.following)

    biases = [column(triple_bias[0:1, :], NARROW), None, column(triple_bias[1:2, :], NARROW)]

    def place_triple(half):
        lanes = HALVES[half]
        for part in range(3):
            values = total[part * NARROW : (part + 1) * NARROW, lanes]
            if part != 1:
                values = values + biases[part]
            values = values.astype(BF)
            edge[part, 0:TAIL, lanes] = values[NARROW - TAIL : NARROW]
            wide[part, pl.ds(pl.multiple_of(TAIL + 8 * me, 8), NARROW), lanes] = values.astype(F32)
        edge_copy(half).start()
        for part in range(3):
            rows = slice(part * WIN + HD, (part + 1) * WIN)
            triple[rows, lanes] = wide[part, TAIL + HD : TAIL + WIN, lanes].astype(BF)

    def place_tail(half):
        lanes = HALVES[half]
        edge_copy(half).wait_recv()
        for part in range(3):
            tail = edge_in[part, 0:TAIL, lanes].astype(F32)
            wide[part, pl.ds(pl.multiple_of(8 * me, 8), TAIL), lanes] = tail
            rows = slice(part * WIN, part * WIN + HD)
            triple[rows, lanes] = wide[part, TAIL : TAIL + HD, lanes].astype(BF)

    pending = {}

    def look(half, h):
        for tile in (half * HALF, half * HALF + TILE):
            reach = tile + TILE
            lanes = slice(tile, reach)
            queries = triple[HD * h : HD * h + HD, lanes] * jnp.asarray(ROOT, BF)
            keys = triple[WIN + HD * h : WIN + HD * h + HD, 0:reach]
            values = triple[2 * WIN + HD * h : 2 * WIN + HD * h + HD, 0:reach]
            scores = dot_f(keys, queries)
            key_place = lax.broadcasted_iota(jnp.int32, (TILE, TILE), 0)
            query_place = lax.broadcasted_iota(jnp.int32, (TILE, TILE), 1)
            edge_scores = jnp.where(key_place <= query_place, scores[tile:reach], -1e30)
            top = jnp.max(edge_scores, 0, keepdims=True)
            if tile:
                top = jnp.maximum(top, jnp.max(scores[0:tile], 0, keepdims=True))
            edge_weights = jnp.exp(edge_scores - top)
            norm = jnp.sum(edge_weights, 0, keepdims=True)
            if tile:
                weights = jnp.exp(scores[0:tile] - top)
                norm += jnp.sum(weights, 0, keepdims=True)
            slot = 2 if h == 3 else (tile // TILE) % 2
            if slot in pending and h < 3:
                pending.pop(slot).wait()
            inverse = 1.0 / norm
            if tile:
                stage[slot, 0:tile, :] = (weights * inverse).astype(BF)
            stage[slot, tile:reach, :] = (edge_weights * inverse).astype(BF)
            copy = pltpu.make_async_copy(
                stage.at[slot, pl.ds(0, reach), :],
                probs_out.at[h, pl.ds(0, reach), pl.ds(tile, TILE)],
                local.at[4 + slot],
            )
            copy.start()
            mixed[HD * h : HD * h + HD, lanes] = dot_n(values, stage[slot, 0:reach, :]).astype(BF)
            if h == 3:
                copy.wait()
            else:
                pending[slot] = copy

    def look_last(half):
        @pl.when(place.last)
        def _():
            look(half, 3)

    def mix(half):
        for step, chip in enumerate(reduces[half].order):
            reduces[half].put(chip, dot_f(mixer[chip], mixed[:, HALVES[half]]))
            reduces[half].give(step)

    mixer_edge_copy.wait_recv()
    for chip in range(4):
        lanes = slice(chip * CHIP, (chip + 1) * CHIP)
        wide[0, :, 0:CHIP] = jnp.zeros((WIN + TAIL, CHIP), F32)
        wide[0, pl.ds(pl.multiple_of(8 * me, 8), TAIL), 0:CHIP] = mixer_edge_in[0:TAIL, lanes].astype(F32)
        rows = pl.ds(pl.multiple_of(TAIL + 8 * me, 8), NARROW)
        wide[0, rows, 0:CHIP] = mixer_raw[:, lanes].astype(F32)
        mixer[chip] = wide[0, TAIL : TAIL + WIN, 0:CHIP].astype(BF)

    firsts[0].near()
    firsts[1].start()
    cots[0].near()
    grow_first(0, place.chip, True)
    firsts[0].middle()
    grow_first(0, place.left_chip)
    grow_first(0, place.right_chip)
    firsts[0].far()
    firsts[1].near()
    firsts[0].last()
    grow_first(0, place.far_chip)
    place_triple(0)
    cots[0].middle()
    grow_first(1, place.chip, True)
    look(0, 1)
    firsts[1].middle()
    grow_first(1, place.left_chip)
    grow_first(1, place.right_chip)
    cots[0].far()
    look(0, 2)
    firsts[1].far()
    place_tail(0)
    look(0, 0)
    look_last(0)
    firsts[1].last()
    grow_first(1, place.far_chip)
    place_triple(1)
    mix(0)
    cots[1].start()
    first_copy = load(whole, first_out, 7)
    cots[0].last()
    look(1, 1)
    reduces[0].first()
    look(1, 2)
    reduces[0].second()
    cots[1].near()
    place_tail(1)
    look(1, 0)
    reduces[0].third()
    look_last(1)
    mix(1)
    expand_load.wait()
    for chip in range(4):
        expander[chip] = expand_raw[:, chip * CHIP : (chip + 1) * CHIP]
    reducer = expand_raw
    reduce_load = load(reduce_weight, reducer, 3)
    cots[1].middle()
    for chip in range(4):
        pack(land_two, chip, cot_whole, HALVES[0])
    triple_copy = load(triple, triple_out, 8)
    mixed_copy = load(mixed, mixed_out, 9)

    mixer_shift = column(mixer_bias[...], NARROW)
    gain, shift = column(second_gain[...], NARROW), column(second_shift[...], NARROW)

    def add_mixed(half):
        values = reduces[half].result() + stream[:, HALVES[half]] + mixer_shift
        after[:, HALVES[half]] = values
        send_center(half, values)

    def grow_second(half, chip, first=False):
        grow(land_one, half, chip, whole, expander, HIDDEN, first)

    def pull(half):
        grad = dot_n(reducer[...], cot_whole[:, :, HALVES[half]].reshape(D, HALF))
        low[:, HALVES[half]] = grad.astype(BF)

    bias_column = column(expand_bias[...], HIDDEN)
    bend_root = math.sqrt(2 / math.pi)

    def bend(half):
        for tile in (half * HALF, half * HALF + TILE):
            lanes = slice(tile, tile + TILE)
            pre = total[:, lanes] + bias_column
            square = pre * pre
            curve = jnp.tanh(bend_root * pre * (1 + 0.044715 * square))
            middle = 0.5 * (1 + curve)
            hidden[:, lanes] = (pre * middle).astype(BF)
            slope = middle + 0.5 * pre * (1 - curve * curve) * (bend_root * (1 + 3 * 0.044715 * square))
            grad_pre = low[:, lanes].astype(F32) * slope
            row_sums = jnp.broadcast_to(jnp.sum(grad_pre, 1, keepdims=True), (HIDDEN, 128))
            if tile:
                expand_sum[...] += row_sums
            else:
                expand_sum[...] = row_sums
            low[:, lanes] = grad_pre.astype(BF)

    def fall(half):
        for step, chip in enumerate(reduces[half].order):
            reduces[half].put(chip, dot_f(expander[chip], low[:, HALVES[half]]))
            reduces[half].give(step)
            if step == 1:
                reduces[half].first()

    firsts[0].end()
    add_mixed(0)
    reduces[1].first()
    reduces[1].second()
    cots[1].far()
    normal(0, after[:, HALVES[0]], gain, shift, 2)
    firsts[0].start()
    reduces[1].third()
    first_copy.wait()
    cots[1].last()
    for chip in range(4):
        pack(land_two, chip, cot_whole, HALVES[1])
    reduce_load.wait()
    pull(0)
    firsts[0].near()
    firsts[1].end()
    add_mixed(1)
    grow_second(0, place.chip, True)
    normal(1, after[:, HALVES[1]], gain, shift, 2)
    firsts[1].start()
    firsts[0].middle()
    grow_second(0, place.left_chip)
    grow_second(0, place.right_chip)
    firsts[0].far()
    pull(1)
    firsts[0].last()
    grow_second(0, place.far_chip)
    reduces[0].end()
    bend(0)
    firsts[1].near()
    fall(0)
    grow_second(1, place.chip, True)
    firsts[1].middle()
    reduces[0].second()
    grow_second(1, place.left_chip)
    grow_second(1, place.right_chip)
    firsts[1].far()
    reduces[0].third()
    firsts[1].last()
    grow_second(1, place.far_chip)
    reduces[1].end()
    bend(1)
    fall(1)

    spread_sems = (spread_send, spread_receive)
    spread_expand = Spread(
        place, "z", grads_expand, passing_expand, up_expand, down_expand, None, None, spread_sems, 0
    )
    spread_reduce = Spread(
        place, "y", grads_reduce, passing_reduce, up_reduce, down_reduce, None, None, spread_sems, 6
    )
    second_whole_now = whole

    for chip in range(2):
        put_grads(grads_reduce, "y", chip, dot_t(cot_whole[chip], hidden[...]))
    reduces[1].second()

    def back_start(half):
        lanes = HALVES[half]
        grad = reduces[half].result()
        normed = (after[:, lanes] - stats[2:3, lanes]) * stats[3:4, lanes]
        scaled = grad * gain
        shares[half].start(jnp.sum(scaled, 0, keepdims=True), jnp.sum(scaled * normed, 0, keepdims=True))
        gain_sum = jnp.sum(grad * normed, 1, keepdims=True)
        shift_sum = jnp.sum(grad, 1, keepdims=True)
        if half:
            sums[:, 0:1] += gain_sum
            sums[:, 1:2] += shift_sum
        else:
            sums[:, 0:1] = gain_sum
            sums[:, 1:2] = shift_sum
        grad_after[:, lanes] = scaled

    def back_end(half):
        lanes = HALVES[half]
        share = shares[half]
        share.wait()
        mean = jnp.sum(share.read(0), 0, keepdims=True) / D
        along = jnp.sum(share.read(1), 0, keepdims=True) / D
        normed = (after[:, lanes] - stats[2:3, lanes]) * stats[3:4, lanes]
        grad = stats[3:4, lanes] * (grad_after[:, lanes] - mean - normed * along) + cot[:, lanes]
        grad_after[:, lanes] = grad
        land_two[me, 0:NARROW, lanes] = grad.astype(BF)
        total_sum = jnp.sum(grad, 1, keepdims=True)
        if half:
            sums[:, 2:3] += total_sum
        else:
            sums[:, 2:3] = total_sum

    for chip in range(2, 4):
        put_grads(grads_reduce, "y", chip, dot_t(cot_whole[chip], hidden[...]))
    spread_reduce.start()
    cots[0].end()
    back_start(0)
    reduces[1].third()
    back_end(0)
    cots[0].start()
    for chip in range(4):
        put_grads(grads_expand, "z", chip, dot_t(second_whole_now[chip], low[...]))
    spread_expand.start()
    cots[0].near()
    cots[1].end()
    back_start(1)
    back_end(1)
    cots[1].start()
    reduces[0].end()
    reduces[1].end()
    after_whole = second_whole

    def grow_mixed(half, chip, first=False, last=False):
        lanes = HALVES[half]
        pack(land_two, chip, after_whole, lanes)
        term = dot_n(mixer[chip], after_whole[chip, :, lanes])
        if first:
            total[0:WIN, lanes] = term
        elif last:
            grad_mixed[:, lanes] = (total[0:WIN, lanes] + term).astype(BF)
        else:
            total[0:WIN, lanes] += term

    def back_result(half):
        for tile in (half * HALF, half * HALF + TILE):
            term = dot_f(reducer[...], hidden[:, tile : tile + TILE])
            for index in range(PARTS):
                rows = slice(index * NARROW, (index + 1) * NARROW)
                parts[index, 0:NARROW, tile : tile + TILE] = term[rows].astype(BF)

    own_at = {"z": place.at["z"], "y": place.at["y"]}
    grow_mixed(0, place.chip, True)
    cots[0].middle()
    grow_mixed(0, place.left_chip)
    grow_mixed(0, place.right_chip)
    cots[0].far()
    back_result(0)
    cots[1].near()
    cots[0].last()
    grow_mixed(0, place.far_chip, False, True)
    spread_reduce.pass_on()
    grow_mixed(1, place.chip, True)
    back_result(1)
    spread_expand.pass_on()
    parts_copy = load(parts, parts_out, 10)
    cots[1].middle()
    grow_mixed(1, place.left_chip)
    grow_mixed(1, place.right_chip)
    own_copies = [
        load(grads_expand.at[own_at["z"]], own_expand, 0),
        load(grads_reduce.at[own_at["y"]], own_reduce, 2),
    ]
    cots[1].far()
    cots[1].last()
    grow_mixed(1, place.far_chip, False, True)
    after_copy = load(after_whole, after_whole_out, 3)
    for gather in firsts + cots:
        gather.end()
    mixer_edge_copy.wait_send()
    for half in range(2):
        edge_copy(half).wait_send()
    for spread in (spread_reduce, spread_expand):
        spread.arrive()
        spread.leave(range(6))
    for copy in (weight_copy, triple_copy, mixed_copy, parts_copy, *own_copies, after_copy, *pending.values()):
        copy.wait()


def forward(*arguments):
    wide_rows = WIN + TAIL
    return pl.pallas_call(
        forward_kernel,
        out_shape=(
            shape((3 * WIN, LEN), BF),
            shape((4, LEN, LEN), BF),
            shape((WIN, LEN), BF),
            shape((4, CHIP, LEN), BF),
            shape((4, CHIP, LEN), BF),
            shape((PARTS, ROWS, LEN), BF),
            shape((4, 3 * NARROW, CHIP), BF),
            *[shape((CHIP, HIDDEN), BF)] * 6,
            shape((NARROW, LEN), F32),
            shape((NARROW, LEN), F32),
            shape((WIN, LEN), BF),
            shape((8, LEN), F32),
            shape((NARROW, 128), F32),
            shape((HIDDEN, 128), F32),
        ),
        in_specs=vmem(9) + hbm(4),
        out_specs=tuple(hbm(13) + vmem(6)),
        scratch_shapes=[
            pltpu.VMEM((3, NARROW, D), BF),
            pltpu.VMEM((NARROW, D), BF),
            pltpu.VMEM((HIDDEN, D), BF),
            pltpu.VMEM((4, 3 * NARROW, CHIP), BF),
            pltpu.VMEM((4, WIN, CHIP), BF),
            pltpu.VMEM((4, HIDDEN, CHIP), BF),
            pltpu.VMEM((3, HD, LEN), BF),
            pltpu.VMEM((3, HD, LEN), BF),
            pltpu.VMEM((HD, D), BF),
            pltpu.VMEM((HD, D), BF),
            pltpu.VMEM((3, WIN + TAIL, LEN), F32),
            pltpu.VMEM((PARTS, ROWS, LEN), BF),
            pltpu.VMEM((PARTS, ROWS, LEN), BF),
            pltpu.VMEM((4, CHIP, LEN), BF),
            pltpu.VMEM((4, CHIP, LEN), BF),
            pltpu.VMEM((HIDDEN, LEN), F32),
            pltpu.VMEM((3 * WIN, LEN), BF),
            pltpu.VMEM((WIN, LEN), BF),
            pltpu.VMEM((3, LEN, TILE), BF),
            pltpu.VMEM((HIDDEN, LEN), BF),
            pltpu.VMEM((HIDDEN, LEN), BF),
            pltpu.VMEM((4, CHIP, HIDDEN), BF),
            pltpu.VMEM((4, CHIP, HIDDEN), BF),
            pltpu.VMEM((CHIP, HIDDEN), BF),
            pltpu.VMEM((CHIP, HIDDEN), BF),
            pltpu.VMEM((2, PARTS, 8, 128), F32),
            *REDUCE_BUFFERS,
            sems(11),
            sems(52),
            sems(52),
            sems(20),
            sems(20),
            sems(14),
            sems(14),
            sems(3),
            sems(3),
            sems(12),
            sems(12),
        ],
        compiler_params=params(1),
        name="forward",
    )(*arguments)


VECTORS = 12


def backward_kernel(
    stream, after, grad_after, stats, first_gain, reduce_bias, second_sums, expand_sum,
    triple_in, probs_in, mixed_in, grad_mixed_in, first_in, after_in, parts_in, weight_in,
    own_expand_in, up_expand_in, down_expand_in, own_reduce_in, up_reduce_in, down_reduce_in,
    result, grad_stream, out_triple, out_mixer, out_expand, out_reduce,
    out_gain, out_shift, out_bias, out_mixer_bias, out_second_gain, out_second_shift, out_expand_bias,
    out_reduce_bias,
    triple, probs, mixed, grad_mixed, first_whole, after_whole, weight,
    grad_triple, own, wide, edge, edge_in, keys_total, tiles, sums, table,
    parts_one, twin_one, one_in, left_two, right_two,
    parts_two, twin_two, two_in, left_four, right_four,
    own_expand, up_expand, down_expand, middle_expand, second_expand,
    own_reduce, up_reduce, down_reduce, middle_reduce, second_reduce,
    grads_mixer, passing_mixer, up_mixer, down_mixer, middle_mixer, second_mixer,
    grads_z, passing_z, up_z, down_z, middle_z, second_z,
    grads_y, passing_y, up_y, down_y, middle_y, second_y,
    local, probs_sems, reduce_send, reduce_receive, share_send, share_receive, edge_send, edge_receive,
    spread_send, spread_receive, table_send, table_receive,
):
    place = Place()
    me = place.me
    group = place.group

    def load(source, target, slot):
        copy = pltpu.make_async_copy(source, target, local.at[slot])
        copy.start()
        return copy

    triple_load = load(triple_in, triple, 0)
    grad_mixed_load = load(grad_mixed_in, grad_mixed, 1)
    mixed_load = load(mixed_in, mixed, 2)

    def probs_copy(h, tile):
        reach = tile + TILE
        return pltpu.make_async_copy(
            probs_in.at[h, pl.ds(0, reach), pl.ds(tile, TILE)],
            probs.at[h, pl.ds(0, reach), pl.ds(tile, TILE)],
            probs_sems.at[4 * h + tile // TILE],
        )

    tiles_of = ((TILE, 0), (3 * TILE, 2 * TILE))

    def probs_load(half, h):
        for tile in tiles_of[half]:
            probs_copy(h, tile).start()

    probs_load(1, 0)
    parts_load = load(parts_in, parts_one, 3)
    probs_load(1, 1)
    probs_load(1, 2)

    @pl.when(place.last)
    def _():
        probs_load(1, 3)

    weight_load = load(weight_in, weight, 4)
    for h in range(3):
        probs_load(0, h)

    @pl.when(place.last)
    def _():
        probs_load(0, 3)

    spread_loads = [
        load(own_reduce_in, own_reduce, 5),
        load(up_reduce_in, up_reduce, 6),
        load(down_reduce_in, down_reduce, 7),
        load(own_expand_in, own_expand, 8),
        load(up_expand_in, up_expand, 9),
        load(down_expand_in, down_expand, 10),
    ]
    after_load = load(after_in, after_whole, 11)
    first_load = load(first_in, first_whole, 12)
    others = [lax.rem(group + i, 16) for i in range(1, 16)]
    greet([{"mp": peer} for peer in place.peers] + [{"dp": other} for other in others])
    reduce_sems = (reduce_send, reduce_receive)
    edge_sems = (edge_send, edge_receive)
    spread_sems = (spread_send, spread_receive)
    shares = [Share(place, tiles.at[half], (share_send, share_receive), 7 * half) for half in range(2)]
    one = (parts_one, twin_one, one_in, left_two, right_two)
    two = (parts_two, twin_two, two_in, left_four, right_four)
    outs = [Reduce(place, one, half, reduce_sems, 10 * half) for half in range(2)]
    reduces = [Reduce(place, two, half, reduce_sems, 20 + 10 * half) for half in range(2)]
    spread_expand = Spread(
        place, "z", None, None, up_expand, down_expand, middle_expand, second_expand, spread_sems, 0
    )
    spread_reduce = Spread(
        place, "y", None, None, up_reduce, down_reduce, middle_reduce, second_reduce, spread_sems, 9
    )
    spread_mixer = Spread(
        place, "z", grads_mixer, passing_mixer, up_mixer, down_mixer, middle_mixer, second_mixer, spread_sems, 18
    )
    spread_z = Spread(place, "z", grads_z, passing_z, up_z, down_z, middle_z, second_z, spread_sems, 27)
    spread_y = Spread(place, "y", grads_y, passing_y, up_y, down_y, middle_y, second_y, spread_sems, 36)

    def edge_copy(step):
        if step == 2:
            piece, target = edge.at[3], edge_in.at[3]
        else:
            lanes = pl.ds(step * HALF, HALF)
            piece, target = edge.at[0:3, :, lanes], edge_in.at[0:3, :, lanes]
        return remote(piece, target, edge_sems, step, place.previous)

    mixed_load.wait()
    edge[3] = mixed[0:HD, :]
    edge_copy(2).start()
    grad_triple[...] = jnp.zeros((3 * WIN, LEN), BF)
    triple_load.wait()
    grad_mixed_load.wait()

    def attend(half, h):
        row = HD * h
        keys = triple[WIN + row : WIN + row + HD, :]
        values = triple[2 * WIN + row : 2 * WIN + row + HD, :]
        for tile in reversed(tiles_of[half]) if half == 0 else tiles_of[half]:
            probs_copy(h, tile).wait()
        for tile in tiles_of[half]:
            reach = tile + TILE
            lanes = slice(tile, reach)
            queries = triple[row : row + HD, lanes] * jnp.asarray(ROOT, BF)
            grad_out = grad_mixed[row : row + HD, lanes]
            delta = jnp.sum(
                grad_out.astype(F32) * mixed[row : row + HD, lanes].astype(F32), 0, keepdims=True
            )
            chances = probs[h, 0:reach, lanes]
            grad_probs = dot_f(values[:, 0:reach], grad_out)
            grad_scores = (chances.astype(F32) * (grad_probs - delta)).astype(BF)
            grad_queries = dot_n(keys[:, 0:reach], grad_scores) * ROOT
            grad_triple[row : row + HD, lanes] = grad_queries.astype(BF)
            key_term = dot_t(queries, grad_scores)
            value_term = dot_t(grad_out, chances)
            if reach == LEN:
                keys_total[h, 0] = key_term
                keys_total[h, 1] = value_term
            else:
                keys_total[h, 0, :, 0:reach] += key_term
                keys_total[h, 1, :, 0:reach] += value_term
        lanes = HALVES[half]
        grad_triple[WIN + row : WIN + row + HD, lanes] = keys_total[h, 0, :, lanes].astype(BF)
        grad_triple[2 * WIN + row : 2 * WIN + row + HD, lanes] = keys_total[h, 1, :, lanes].astype(BF)

    def attend_last(half):
        @pl.when(place.last)
        def _():
            attend(half, 3)

    def send_edge(half):
        for part in range(3):
            edge[part, :, HALVES[half]] = grad_triple[part * WIN : part * WIN + HD, HALVES[half]]
        edge_copy(half).start()

    def place_own(part, lanes):
        if part < 3:
            piece = grad_triple[part * WIN : (part + 1) * WIN, lanes]
        else:
            piece = mixed[:, lanes]
        piece = piece.astype(F32)
        wide[0 : 3 * HD, lanes] = piece[0 : 3 * HD]
        neighbour = edge_in[part, :, lanes].astype(F32)
        wide[3 * HD : WIN, lanes] = jnp.where(place.last, piece[3 * HD : WIN], neighbour)
        values = wide[pl.ds(pl.multiple_of(8 * me, 8), NARROW), lanes]
        own[part * NARROW : (part + 1) * NARROW, lanes] = values.astype(BF)
        return jnp.sum(values, 1, keepdims=True)

    def place_rows(half):
        edge_copy(half).wait_recv()
        for part in range(3):
            total = place_own(part, HALVES[half])
            if half == 1:
                sums[:, 2 + part : 3 + part] = total
            else:
                sums[:, 2 + part : 3 + part] += total

    def fall(half, rows=True):
        if rows:
            place_rows(half)
        for step, chip in enumerate(reduces[half].order):
            reduces[half].put(chip, dot_f(weight[chip], own[0 : 3 * NARROW, HALVES[half]]))
            reduces[half].give(step)
            if step == 1:
                reduces[half].first()

    def weigh(axis, grads, whole, rows):
        for chip in range(4):
            put_grads(grads, axis, chip, dot_t(whole[chip], own[rows, :]))

    parts_load.wait()
    for half in range(2):
        for step in range(4):
            outs[half].give(step)
    attend(1, 0)
    send_edge(1)
    outs[1].first()
    outs[0].first()
    for copy in spread_loads:
        copy.wait()
    spread_reduce.turn(own_reduce[...])
    spread_expand.turn(own_expand[...])
    outs[1].second()
    outs[0].second()
    attend(1, 1)
    outs[1].third()
    outs[0].third()
    edge_copy(2).wait_recv()
    place_own(3, slice(0, LEN))
    after_load.wait()
    weigh("z", grads_mixer, after_whole, slice(3 * NARROW, 4 * NARROW))
    spread_mixer.start()
    attend(1, 2)
    attend_last(1)
    weight_load.wait()
    fall(1)
    attend(0, 0)
    send_edge(0)
    reduces[1].second()
    spread_mixer.pass_on()
    attend(0, 1)
    reduces[1].third()
    attend(0, 2)
    attend_last(0)
    first_load.wait()
    place_rows(0)
    weigh("y", grads_y, first_whole, slice(WIN, 3 * NARROW))
    spread_y.start()
    weigh("z", grads_z, first_whole, slice(0, WIN))
    spread_z.start()
    fall(0, False)
    spread_mixer.arrive()
    spread_mixer.turn(grads_mixer[place.at["z"]])
    reduces[0].second()
    spread_z.pass_on()
    spread_y.pass_on()
    reduces[0].third()
    gain = column(first_gain[...], NARROW)
    shift = column(reduce_bias[...], NARROW)

    def back_start(half):
        lanes = HALVES[half]
        grad = reduces[half].result()
        normed = (stream[:, lanes] - stats[0:1, lanes]) * stats[1:2, lanes]
        scaled = grad * gain
        shares[half].start(jnp.sum(scaled, 0, keepdims=True), jnp.sum(scaled * normed, 0, keepdims=True))
        gain_sum = jnp.sum(grad * normed, 1, keepdims=True)
        shift_sum = jnp.sum(grad, 1, keepdims=True)
        if half == 1:
            sums[:, 0:1] = gain_sum
            sums[:, 1:2] = shift_sum
        else:
            sums[:, 0:1] += gain_sum
            sums[:, 1:2] += shift_sum
        grad_stream[:, lanes] = scaled

    def back_end(half):
        lanes = HALVES[half]
        share = shares[half]
        share.wait()
        mean = jnp.sum(share.read(0), 0, keepdims=True) / D
        along = jnp.sum(share.read(1), 0, keepdims=True) / D
        normed = (stream[:, lanes] - stats[0:1, lanes]) * stats[1:2, lanes]
        back = stats[1:2, lanes] * (grad_stream[:, lanes] - mean - normed * along)
        grad_stream[:, lanes] = back + grad_after[:, lanes]

    back_start(1)
    for half in range(2):
        result[:, HALVES[half]] = outs[half].result() + after[:, HALVES[half]] + shift
    out_expand[...] = spread_expand.result()
    out_reduce[...] = spread_reduce.result()
    back_end(1)
    back_start(0)
    columns = [
        sums[:, 0:1], sums[:, 1:2], sums[:, 2:3], sums[:, 4:5],
        second_sums[:, 2:3], second_sums[:, 0:1], second_sums[:, 1:2], second_sums[:, 3:4],
    ]
    columns += [expand_sum[NARROW * i : NARROW * (i + 1), 0:1] for i in range(4)]
    spot = lax.broadcasted_iota(jnp.int32, (NARROW, 128), 1)
    packed = jnp.zeros((NARROW, 128), F32)
    for i, values in enumerate(columns):
        packed = jnp.where(spot == i, values, packed)
    table[group] = packed.T[0:16]

    def table_copy(step, owner, device):
        return remote(table.at[owner], table.at[owner], (table_send, table_receive), step, device, "dp")

    for step, other in enumerate(others):
        table_copy(step, group, other).start()
    back_end(0)
    spread_z.arrive()
    spread_z.turn(grads_z[place.at["z"]])
    spread_y.arrive()
    spread_y.turn(grads_y[place.at["y"]])
    for step in range(15):
        table_copy(step, lax.rem(group + 15 - step, 16), group).wait_recv()
    vectors = jnp.sum(table[...], 0)
    out_gain[...] = vectors[0:1].reshape(NARROW)
    out_shift[...] = vectors[1:2].reshape(NARROW)
    out_bias[...] = vectors[2:4]
    out_mixer_bias[...] = vectors[4:5].reshape(NARROW)
    out_second_gain[...] = vectors[5:6].reshape(NARROW)
    out_second_shift[...] = vectors[6:7].reshape(NARROW)
    out_reduce_bias[...] = vectors[7:8].reshape(NARROW)
    out_expand_bias[...] = vectors[8:12]
    out_mixer[...] = spread_mixer.result().T
    rest = jnp.concatenate([spread_z.result(), spread_y.result()], 1)
    for part in range(3):
        out_triple[part] = rest[:, part * NARROW : (part + 1) * NARROW].T
    for reduce in outs + reduces:
        reduce.end()
    for step in range(3):
        edge_copy(step).wait_send()
    for spread in (spread_expand, spread_reduce):
        spread.leave(range(6, 9))
    for spread in (spread_mixer, spread_z, spread_y):
        spread.leave(range(9))
    for step, other in enumerate(others):
        table_copy(step, group, other).wait_send()


def spread_scratch(lanes, whole):
    one = [pltpu.VMEM((CHIP, lanes), BF)]
    ends = [pltpu.VMEM((4, DEEP, lanes), BF), pltpu.VMEM((3, DEEP, lanes), BF)]
    return ([pltpu.VMEM((4, CHIP, lanes), BF)] if whole else []) + one * 3 + ends


def backward(*arguments):
    width = 4 * NARROW
    return pl.pallas_call(
        backward_kernel,
        out_shape=(
            shape((NARROW, LEN), F32),
            shape((NARROW, LEN), F32),
            shape((3, NARROW, 100), F32),
            shape((NARROW, 100), F32),
            shape((100, HIDDEN), F32),
            shape((100, HIDDEN), F32),
            shape((NARROW,), F32),
            shape((NARROW,), F32),
            shape((2, NARROW), F32),
            shape((NARROW,), F32),
            shape((NARROW,), F32),
            shape((NARROW,), F32),
            shape((4, NARROW), F32),
            shape((NARROW,), F32),
        ),
        in_specs=vmem(8) + hbm(14),
        out_specs=tuple(vmem(14)),
        scratch_shapes=[
            pltpu.VMEM((3 * WIN, LEN), BF),
            pltpu.VMEM((4, LEN, LEN), BF),
            pltpu.VMEM((WIN, LEN), BF),
            pltpu.VMEM((WIN, LEN), BF),
            pltpu.VMEM((4, CHIP, LEN), BF),
            pltpu.VMEM((4, CHIP, LEN), BF),
            pltpu.VMEM((4, 3 * NARROW, CHIP), BF),
            pltpu.VMEM((3 * WIN, LEN), BF),
            pltpu.VMEM((width, LEN), BF),
            pltpu.VMEM((WIN, LEN), F32),
            pltpu.VMEM((4, HD, LEN), BF),
            pltpu.VMEM((4, HD, LEN), BF),
            pltpu.VMEM((4, 2, HD, LEN), F32),
            pltpu.VMEM((2, PARTS, 8, 128), F32),
            pltpu.VMEM((NARROW, 128), F32),
            pltpu.VMEM((16, 16, NARROW), F32),
            *REDUCE_BUFFERS,
            *REDUCE_BUFFERS,
            *spread_scratch(HIDDEN, False),
            *spread_scratch(HIDDEN, False),
            *spread_scratch(NARROW, True),
            *spread_scratch(WIN, True),
            *spread_scratch(3 * NARROW - WIN, True),
            sems(13),
            sems(16),
            sems(40),
            sems(40),
            sems(14),
            sems(14),
            sems(3),
            sems(3),
            sems(45),
            sems(45),
            sems(15),
            sems(15),
        ],
        compiler_params=params(2),
        name="backward",
    )(*arguments)


def hand_over_kernel(*refs):
    count = len(refs) // 2
    for source, target in zip(refs[:count], refs[count:]):
        if source.shape == target.shape:
            target[...] = source[...]
        else:
            rows = [source[i : i + 1, :] for i in range(source.shape[0])]
            target[...] = jnp.concatenate(rows, 1).reshape(target.shape)


def hand_over(*arrays):
    count = len(arrays)
    return pl.pallas_call(
        hand_over_kernel,
        out_shape=tuple(
            shape((HIDDEN,) if array.shape == (4, NARROW) else array.shape, array.dtype) for array in arrays
        ),
        in_specs=vmem(count),
        out_specs=tuple(vmem(count)),
        compiler_params=pltpu.CompilerParams(vmem_limit_bytes=VMEM_LIMIT),
        name="hand_over",
    )(*arrays)


def shards(
    stream, first_gain, first_shift, triple_weight, triple_bias, mixer_weight, mixer_bias,
    second_gain, second_shift, expand_weight, expand_bias, reduce_weight, reduce_bias, cotangent,
):
    turned = stream.T
    (
        triple, probs, mixed, first_whole, after_whole, parts, weight,
        *spreads,
        after, grad_after, grad_mixed, stats, sums, expand_sum,
    ) = forward(
        turned, cotangent.T, first_gain, first_shift, triple_bias, mixer_bias, second_gain, second_shift,
        expand_bias, triple_weight.transpose(1, 2, 0), mixer_weight, expand_weight.T, reduce_weight,
    )
    (
        result, grad_stream, out_triple, out_mixer, out_expand, out_reduce,
        out_gain, out_shift, out_bias, out_mixer_bias, out_second_gain, out_second_shift, out_expand_bias,
        out_reduce_bias,
    ) = hand_over(*backward(
        turned, after, grad_after, stats, first_gain, reduce_bias, sums, expand_sum,
        triple, probs, mixed, grad_mixed, first_whole, after_whole, parts, weight, *spreads,
    ))
    return (
        result.T,
        grad_stream.T,
        out_gain,
        out_shift,
        out_triple.transpose(2, 0, 1),
        out_bias,
        out_mixer,
        out_mixer_bias,
        out_second_gain,
        out_second_shift,
        out_expand,
        out_expand_bias,
        out_reduce.T,
        out_reduce_bias,
    )


def solution(mesh):
    placed = (
        P("dp", "mp"),
        P("mp"),
        P("mp"),
        P(None, None, "mp"),
        P(None, "mp"),
        P("mp", None),
        P("mp"),
        P("mp"),
        P("mp"),
        P(None, "mp"),
        P("mp"),
        P("mp", None),
        P("mp"),
        P("dp", "mp"),
    )
    return jax.shard_map(
        shards,
        mesh=mesh,
        in_specs=placed,
        out_specs=(
            P("dp", "mp"),
            P("dp", "mp"),
            P("mp"),
            P("mp"),
            P("dp", None, "mp"),
            P(None, "mp"),
            P("mp", "dp"),
            P("mp"),
            P("mp"),
            P("mp"),
            P("dp", "mp"),
            P("mp"),
            P("mp", "dp"),
            P("mp"),
        ),
        check_vma=False,
    )
```

```python
import math

import jax
import jax.numpy as jnp
from jax import lax
from jax.experimental import pallas as pl
from jax.experimental.pallas import tpu as pltpu
from jax.sharding import PartitionSpec as P

HD = 64
LEN = 1024
D = 1600
PARTS = 8
NARROW = D // PARTS
HIDDEN = 800
CHIP = 400
ROWS = 208
DEEP = 112
SPLIT = 208
WIN = 256
TAIL = WIN - NARROW
HALF = LEN // 2
TILE = 256
EPSILON = 1e-05
ROOT = 1 / math.sqrt(HD)
MESH = pl.DeviceIdType.MESH
BF = jnp.bfloat16
F32 = jnp.float32
VMEM_LIMIT = 62 * 1024 * 1024


def dot_n(left, right):
    return lax.dot_general(left, right, (((1,), (0,)), ((), ())), preferred_element_type=F32)


def dot_t(left, right):
    return lax.dot_general(left, right, (((1,), (1,)), ((), ())), preferred_element_type=F32)


def dot_f(left, right):
    return lax.dot_general(left, right, (((0,), (0,)), ((), ())), preferred_element_type=F32)


class Place:
    def __init__(self):
        self.me = lax.axis_index("mp")
        self.chip = self.me // 2
        self.core = self.me % 2
        self.right_chip = lax.rem(self.chip + 1, 4)
        self.left_chip = lax.rem(self.chip + 3, 4)
        self.far_chip = lax.rem(self.chip + 2, 4)
        self.right = self.right_chip * 2 + self.core
        self.left = self.left_chip * 2 + self.core
        self.far = self.far_chip * 2 + self.core
        self.twin = self.chip * 2 + 1 - self.core
        self.peers = [lax.rem(self.me + i, PARTS) for i in range(1, PARTS)]
        self.previous = lax.rem(self.me + PARTS - 1, PARTS)
        self.following = lax.rem(self.me + 1, PARTS)
        self.last = self.me == PARTS - 1
        self.group = lax.axis_index("dp")
        self.at = {"z": self.group // 4, "y": self.group % 4}

    def along(self, axis, step):
        at = lax.rem(self.at[axis] + step, 4)
        z, y = (at, self.at["y"]) if axis == "z" else (self.at["z"], at)
        return at, z * 4 + y


def greet(devices):
    barrier = pltpu.get_barrier_semaphore()
    for device in devices:
        pl.semaphore_signal(barrier, inc=1, device_id=device, device_id_type=MESH)
    pl.semaphore_wait(barrier, len(devices))


def remote(source, target, sems, step, device, axis="mp"):
    send, receive = sems
    return pltpu.make_async_remote_copy(
        src_ref=source,
        dst_ref=target,
        send_sem=send.at[step],
        recv_sem=receive.at[step],
        device_id={axis: device},
        device_id_type=MESH,
    )


class Share:
    def __init__(self, place, tiles, sems, offset):
        self.place, self.tiles, self.sems, self.offset = place, tiles, sems, offset

    def copy(self, step, owner, device):
        tile = self.tiles.at[owner]
        return remote(tile, tile, self.sems, self.offset + step, device)

    def start(self, *vectors):
        rows = HALF // 128
        for i, vector in enumerate(vectors):
            for j in range(rows):
                piece = vector[:, 128 * j : 128 * j + 128]
                self.tiles[self.place.me, rows * i + j : rows * i + j + 1, :] = piece
        for step, peer in enumerate(self.place.peers):
            self.copy(step, self.place.me, peer).start()

    def wait(self):
        me = self.place.me
        for step in range(PARTS - 1):
            owner = lax.rem(me + PARTS - 1 - step, PARTS)
            self.copy(step, owner, me).wait_recv()
        for step, peer in enumerate(self.place.peers):
            self.copy(step, me, peer).wait_send()

    def read(self, index):
        rows = HALF // 128
        return jnp.concatenate([self.tiles[:, rows * index + j, :] for j in range(rows)], 1)


class Gather:
    COUNT = 13

    def __init__(self, place, blocks, half, sems, offset):
        self.place, self.blocks, self.base = place, blocks, half * HALF
        self.sems, self.offset = sems, offset

    def copy(self, step, owner, side, device):
        if side is None:
            lanes = pl.ds(self.base, HALF)
        else:
            lanes = pl.ds(self.base + side * TILE, TILE)
        block = self.blocks.at[owner, :, lanes]
        return remote(block, block, self.sems, self.offset + step, device)

    def other(self, owner):
        return owner + 1 - 2 * self.place.core

    def start(self):
        self.start_first()
        self.start_rest()

    def start_first(self):
        p = self.place
        self.copy(0, p.me, 0, p.right).start()
        self.copy(3, p.me, 1, p.left).start()

    def start_rest(self):
        p = self.place
        self.copy(1, p.me, 1, p.right).start()
        self.copy(4, p.me, 0, p.left).start()
        self.copy(6, p.me, None, p.twin).start()

    def near(self):
        p = self.place
        self.copy(0, p.left, 0, p.me).wait_recv()
        self.copy(2, p.left, 0, p.right).start()
        self.copy(7, p.left, 0, p.twin).start()
        self.copy(3, p.right, 1, p.me).wait_recv()
        self.copy(5, p.right, 1, p.left).start()
        self.copy(8, p.right, 1, p.twin).start()
        self.copy(6, p.twin, None, p.me).wait_recv()

    def middle(self):
        p = self.place
        self.copy(1, p.left, 1, p.me).wait_recv()
        self.copy(9, p.left, 1, p.twin).start()
        self.copy(4, p.right, 0, p.me).wait_recv()
        self.copy(10, p.right, 0, p.twin).start()
        self.copy(7, self.other(p.left), 0, p.me).wait_recv()
        self.copy(8, self.other(p.right), 1, p.me).wait_recv()
        self.copy(9, self.other(p.left), 1, p.me).wait_recv()
        self.copy(10, self.other(p.right), 0, p.me).wait_recv()

    def far(self):
        p = self.place
        self.copy(2, p.far, 0, p.me).wait_recv()
        self.copy(11, p.far, 0, p.twin).start()
        self.copy(5, p.far, 1, p.me).wait_recv()
        self.copy(12, p.far, 1, p.twin).start()

    def last(self):
        p = self.place
        self.copy(11, self.other(p.far), 0, p.me).wait_recv()
        self.copy(12, self.other(p.far), 1, p.me).wait_recv()

    def end(self):
        p = self.place
        for step, owner, side, device in (
            (0, p.me, 0, p.right),
            (1, p.me, 1, p.right),
            (2, p.left, 0, p.right),
            (3, p.me, 1, p.left),
            (4, p.me, 0, p.left),
            (5, p.right, 1, p.left),
            (6, p.me, None, p.twin),
            (7, p.left, 0, p.twin),
            (8, p.right, 1, p.twin),
            (9, p.left, 1, p.twin),
            (10, p.right, 0, p.twin),
            (11, p.far, 0, p.twin),
            (12, p.far, 1, p.twin),
        ):
            self.copy(step, owner, side, device).wait_send()


class Reduce:
    COUNT = 10

    def __init__(self, place, buffers, half, sems, offset):
        self.place, self.base = place, half * HALF
        self.parts, self.twin, self.left_one, self.left_two, self.right_two = buffers
        self.right_one = self.left_one
        self.sems, self.offset = sems, offset
        self.order = [place.far_chip, place.right_chip, place.left_chip, place.chip]
        self.lanes = slice(self.base, self.base + HALF)
        self.low = slice(self.base, self.base + TILE)
        self.high = slice(self.base + TILE, self.base + HALF)

    def copy(self, step):
        p = self.place
        both, low, high = pl.ds(self.base, HALF), pl.ds(self.base, TILE), pl.ds(self.base + TILE, TILE)
        if step < 4:
            chip = self.order[step]
            source = self.parts.at[2 * chip + 1 - p.core, :, both]
            target = self.twin.at[chip, :, both]
            device = p.twin
        elif step == 4:
            source, target, device = self.parts.at[p.far, :, low], self.left_one.at[:, low], p.right
        elif step == 5:
            source, target, device = self.parts.at[p.far, :, high], self.right_one.at[:, high], p.left
        elif step == 6:
            source, target, device = self.parts.at[p.right, :, high], self.left_two.at[:, high], p.right
        elif step == 7:
            source, target, device = self.parts.at[p.right, :, low], self.left_two.at[:, low], p.right
        elif step == 8:
            source, target, device = self.parts.at[p.left, :, low], self.right_two.at[:, low], p.left
        else:
            source, target, device = self.parts.at[p.left, :, high], self.right_two.at[:, high], p.left
        return remote(source, target, self.sems, self.offset + step, device)

    def arrived(self, step):
        both, low, high = pl.ds(self.base, HALF), pl.ds(self.base, TILE), pl.ds(self.base + TILE, TILE)
        if step < 4:
            target = self.twin.at[self.order[step], :, both]
        else:
            target = (
                self.left_one.at[:, low],
                self.right_one.at[:, high],
                self.left_two.at[:, high],
                self.left_two.at[:, low],
                self.right_two.at[:, low],
                self.right_two.at[:, high],
            )[step - 4]
        remote(target, target, self.sems, self.offset + step, self.place.me).wait_recv()

    def put(self, chip, term):
        for core in range(2):
            rows = term[core * NARROW : (core + 1) * NARROW]
            self.parts[2 * chip + core, 0:NARROW, self.lanes] = rows.astype(BF)

    def give(self, step):
        self.copy(step).start()

    def fold(self, step):
        self.arrived(step)
        chip = self.order[step]
        mine = 2 * chip + self.place.core
        total = self.parts[mine, :, self.lanes].astype(F32) + self.twin[chip, :, self.lanes].astype(F32)
        self.parts[mine, :, self.lanes] = total.astype(BF)

    def first(self):
        self.fold(0)
        self.copy(4).start()
        self.copy(5).start()

    def second(self):
        self.fold(1)
        self.copy(6).start()
        self.fold(2)
        self.copy(8).start()

    def third(self):
        p = self.place
        self.arrived(4)
        held = self.parts[p.right, :, self.low].astype(F32)
        self.parts[p.right, :, self.low] = (held + self.left_one[:, self.low].astype(F32)).astype(BF)
        self.copy(7).start()
        self.arrived(5)
        held = self.parts[p.left, :, self.high].astype(F32)
        self.parts[p.left, :, self.high] = (held + self.right_one[:, self.high].astype(F32)).astype(BF)
        self.copy(9).start()
        self.fold(3)

    def result(self):
        for step in range(6, 10):
            self.arrived(step)
        total = self.parts[self.place.me, 0:NARROW, self.lanes].astype(F32)
        total += self.left_two[0:NARROW, self.lanes].astype(F32)
        return total + self.right_two[0:NARROW, self.lanes].astype(F32)

    def end(self):
        for step in range(10):
            self.copy(step).wait_send()


REDUCE_BUFFERS = [
    pltpu.VMEM((PARTS, ROWS, LEN), BF),
    pltpu.VMEM((4, ROWS, LEN), BF),
    pltpu.VMEM((ROWS, LEN), BF),
    pltpu.VMEM((ROWS, LEN), BF),
    pltpu.VMEM((ROWS, LEN), BF),
]


class Spread:
    COUNT = 9
    LOW, HIGH = slice(0, SPLIT), slice(SPLIT, CHIP)

    def __init__(self, place, axis, grads, passing, early, onward, late, middle, second_in, sems, offset):
        self.place, self.axis, self.other = place, axis, "zy".replace(axis, "")
        self.grads, self.passing, self.early = grads, passing, early
        self.onward, self.late = onward, late
        self.middle, self.second_in = middle, second_in
        self.sems, self.offset = sems, offset

    def block(self, away):
        return self.place.along(self.axis, away)[0]

    def copy(self, step):
        low, high = pl.ds(0, SPLIT), pl.ds(SPLIT, CHIP - SPLIT)
        if step < 6:
            away, rows, target, way = (
                (2, low, self.passing, 1),
                (2, high, self.passing, 3),
                (1, high, self.early, 1),
                (3, low, self.early, 3),
                (None, low, self.late, 1),
                (None, high, self.late, 3),
            )[step]
            source = self.onward.at[rows] if away is None else self.grads.at[self.block(away), rows]
            device = self.place.along(self.axis, way)[1]
            target = target.at[rows]
        else:
            at, device = self.place.along(self.other, step - 5)
            source, target = self.middle.at[at], self.second_in.at[step - 6]
        return remote(source, target, self.sems, self.offset + step, device, "dp")

    def start(self):
        for step in range(4):
            self.copy(step).start()

    def arrive(self, steps):
        for step in steps:
            self.copy(step).wait_recv()

    def pass_on(self, held):
        for step, rows in ((4, self.LOW), (5, self.HIGH)):
            self.onward[rows] = (held(rows).astype(F32) + self.passing[rows].astype(F32)).astype(BF)
            self.copy(step).start()

    def mine(self, rows):
        return self.grads[self.block(1 if rows == self.LOW else 3), rows]

    def turn(self, own):
        total = own.astype(F32) + self.early[...].astype(F32) + self.late[...].astype(F32)
        for part in range(4):
            self.middle[part, 0:100] = total[100 * part : 100 * part + 100].astype(BF)
        for step in range(6, 9):
            self.copy(step).start()

    def result(self):
        self.arrive(range(6, 9))
        total = self.middle[self.place.at[self.other], 0:100].astype(F32)
        for step in range(3):
            total += self.second_in[step, 0:100].astype(F32)
        return total

    def leave(self, steps):
        for step in steps:
            self.copy(step).wait_send()


def pack(blocks, chip, whole, lanes):
    whole[chip, 0:NARROW, lanes] = blocks[2 * chip, 0:NARROW, lanes]
    whole[chip, NARROW:CHIP, lanes] = blocks[2 * chip + 1, 0:NARROW, lanes]


def put_grads(grads, axis, chip, term, add=False):
    if axis == "z":
        places = [(chip, slice(0, CHIP), slice(0, CHIP))]
    else:
        rows = slice(100 * chip, 100 * chip + 100)
        places = [(part, rows, slice(100 * part, 100 * part + 100)) for part in range(4)]
    for block, rows, source in places:
        values = term[source]
        if add:
            values += grads[block, rows].astype(F32)
        grads[block, rows] = values.astype(BF)


def column(vector, count):
    return jnp.broadcast_to(vector.reshape(1, count), (8, count)).T[:, 0:1]


def vmem(count):
    return [pl.BlockSpec(memory_space=pltpu.VMEM)] * count


def hbm(count):
    return [pl.BlockSpec(memory_space=pl.ANY)] * count


def sems(count):
    return pltpu.SemaphoreType.DMA((count,))


def shape(dims, kind):
    return jax.ShapeDtypeStruct(dims, kind)


def params(collective):
    return pltpu.CompilerParams(
        collective_id=collective, has_side_effects=True, vmem_limit_bytes=VMEM_LIMIT
    )


HALVES = (slice(0, HALF), slice(HALF, LEN))


def forward_kernel(
    first_gain, first_shift, triple_bias, mixer_bias, second_gain, second_shift, expand_bias,
    stream_in, cot_in, triple_weight, mixer_weight, expand_weight, reduce_weight,
    triple_out, probs_out, mixed_out, first_out, after_whole_out, parts_out, weight_out,
    own_expand, passing_expand, early_expand, onward_expand, own_reduce, passing_reduce, early_reduce,
    onward_reduce,
    after_out, grad_after_out, grad_mixed_out,
    stats, sums, expand_sum,
    stream, cot, after, grad_after, grad_mixed,
    triple_raw, mixer_raw, expand_raw, weight, mixer, expander,
    edge, edge_in, mixer_edge, mixer_edge_in, wide, land_one, land_two, whole, second_whole,
    total, triple, mixed, stage, hidden, low, grads_expand, grads_reduce, tiles,
    parts, twin, one_in, left_two, right_two,
    local, gather_send, gather_receive, reduce_send, reduce_receive, share_send, share_receive,
    edge_send, edge_receive, spread_send, spread_receive,
):
    place = Place()
    me = place.me

    def load(source, target, slot):
        copy = pltpu.make_async_copy(source, target, local.at[slot])
        copy.start()
        return copy

    stream_load = load(stream_in, stream, 11)
    triple_load = load(triple_weight, triple_raw, 1)
    cot_load = load(cot_in, cot, 12)
    mixer_load = load(mixer_weight, mixer_raw, 0)
    expand_load = load(expand_weight, expand_raw, 2)
    greet(
        [{"mp": peer} for peer in place.peers]
        + [{"dp": place.along(axis, step)[1]} for axis in "zy" for step in range(1, 4)]
    )
    gather_sems = (gather_send, gather_receive)
    edge_sems = (edge_send, edge_receive)
    shares = [Share(place, tiles.at[half], (share_send, share_receive), 7 * half) for half in range(2)]
    firsts = [Gather(place, land_one, half, gather_sems, 13 * half) for half in range(2)]
    cots = [Gather(place, land_two, half, gather_sems, 26 + 13 * half) for half in range(2)]
    buffers = (parts, twin, one_in, left_two, right_two)
    reduces = [Reduce(place, buffers, half, (reduce_send, reduce_receive), 10 * half) for half in range(2)]
    cot_whole = second_whole
    after_whole = second_whole
    reducer = expand_raw

    def send_center(half, values):
        center = jnp.sum(values, 0, keepdims=True) / NARROW
        shares[half].start(center, jnp.sum(jnp.square(values - center), 0, keepdims=True))

    def normal(half, values, gain, shift, row):
        share = shares[half]
        share.wait()
        centers, spreads = share.read(0), share.read(1)
        center = jnp.sum(centers, 0, keepdims=True) / PARTS
        spread = jnp.sum(spreads, 0, keepdims=True)
        spread += NARROW * jnp.sum(jnp.square(centers - center), 0, keepdims=True)
        scale = lax.rsqrt(spread / D + EPSILON)
        stats[row : row + 1, HALVES[half]] = center
        stats[row + 1 : row + 2, HALVES[half]] = scale
        low_values = (values - center) * scale * gain + shift
        land_one[me, 0:NARROW, HALVES[half]] = low_values.astype(BF)

    def grow(lands, half, chip, target, factor, rows, first):
        pack(lands, chip, target, HALVES[half])
        term = dot_n(factor[chip], target[chip, :, HALVES[half]])
        if first:
            total[0:rows, HALVES[half]] = term
        else:
            total[0:rows, HALVES[half]] += term

    def grow_first(half, chip, first=False):
        grow(land_one, half, chip, whole, weight, 3 * NARROW, first)

    def grow_second(half, chip, first=False):
        grow(land_one, half, chip, whole, expander, HIDDEN, first)

    def edge_copy(half, count):
        rows, lanes = pl.ds(0, count), pl.ds(half * HALF, HALF)
        if half == 2:
            source, target = mixer_edge.at[rows], mixer_edge_in.at[rows]
        else:
            source, target = edge.at[:, rows, lanes], edge_in.at[:, rows, lanes]
        return remote(source, target, edge_sems, half, place.following)

    def edge_do(half, sender, act):
        inside = place.core == (0 if sender else 1)

        @pl.when(inside)
        def _():
            act(edge_copy(half, HD))

        @pl.when(jnp.logical_not(inside))
        def _():
            act(edge_copy(half, 48))

    biases = [column(triple_bias[0:1, :], NARROW), None, column(triple_bias[1:2, :], NARROW)]

    def place_triple(half):
        lanes = HALVES[half]
        for part in range(3):
            values = total[part * NARROW : (part + 1) * NARROW, lanes]
            if part != 1:
                values = values + biases[part]
            values = values.astype(BF)
            edge[part, 0:48, lanes] = values[NARROW - 48 : NARROW]
            edge[part, 48:TAIL, lanes] = values[NARROW - TAIL : NARROW - 48]
            wide[part, pl.ds(pl.multiple_of(TAIL + 8 * me, 8), NARROW), lanes] = values.astype(F32)
        edge_do(half, True, lambda copy: copy.start())
        for part in range(3):
            rows = slice(part * WIN + HD, (part + 1) * WIN)
            triple[rows, lanes] = wide[part, TAIL + HD : TAIL + WIN, lanes].astype(BF)

    def place_tail(half):
        lanes = HALVES[half]
        edge_do(half, False, lambda copy: copy.wait_recv())
        for part in range(3):
            near_rows = edge_in[part, 0:48, lanes].astype(F32)
            wide[part, pl.ds(pl.multiple_of(8 * me + 8, 8), 48), lanes] = near_rows
            wide[part, pl.ds(pl.multiple_of(8 * me, 8), 8), lanes] = edge_in[part, 48:TAIL, lanes].astype(F32)
            rows = slice(part * WIN, part * WIN + HD)
            triple[rows, lanes] = wide[part, TAIL : TAIL + HD, lanes].astype(BF)

    pending = {}

    def look(half, h):
        for tile in (half * HALF, half * HALF + TILE):
            reach = tile + TILE
            lanes = slice(tile, reach)
            queries = triple[HD * h : HD * h + HD, lanes] * jnp.asarray(ROOT, BF)
            keys = triple[WIN + HD * h : WIN + HD * h + HD, 0:reach]
            values = triple[2 * WIN + HD * h : 2 * WIN + HD * h + HD, 0:reach]
            scores = dot_f(keys, queries)
            key_place = lax.broadcasted_iota(jnp.int32, (TILE, TILE), 0)
            query_place = lax.broadcasted_iota(jnp.int32, (TILE, TILE), 1)
            edge_scores = jnp.where(key_place <= query_place, scores[tile:reach], -1e30)
            top = jnp.max(edge_scores, 0, keepdims=True)
            if tile:
                top = jnp.maximum(top, jnp.max(scores[0:tile], 0, keepdims=True))
            edge_weights = jnp.exp(edge_scores - top)
            norm = jnp.sum(edge_weights, 0, keepdims=True)
            if tile:
                weights = jnp.exp(scores[0:tile] - top)
                norm += jnp.sum(weights, 0, keepdims=True)
            slot = 2 if h == 3 else (tile // TILE) % 2
            if slot in pending and h < 3:
                pending.pop(slot).wait()
            inverse = 1.0 / norm
            if tile:
                stage[slot, 0:tile, :] = (weights * inverse).astype(BF)
            stage[slot, tile:reach, :] = (edge_weights * inverse).astype(BF)
            copy = pltpu.make_async_copy(
                stage.at[slot, pl.ds(0, reach), :],
                probs_out.at[h, pl.ds(0, reach), pl.ds(tile, TILE)],
                local.at[4 + slot],
            )
            copy.start()
            mixed[HD * h : HD * h + HD, lanes] = dot_n(values, stage[slot, 0:reach, :]).astype(BF)
            if h == 3:
                copy.wait()
            else:
                pending[slot] = copy

    def look_last(half):
        @pl.when(place.last)
        def _():
            look(half, 3)

    def mix(half):
        for step, chip in enumerate(reduces[half].order):
            reduces[half].put(chip, dot_f(mixer[chip], mixed[:, HALVES[half]]))
            reduces[half].give(step)

    def add_mixed(half):
        values = reduces[half].result() + stream[:, HALVES[half]] + mixer_shift
        after[:, HALVES[half]] = values
        send_center(half, values)

    def pull(half):
        grad = dot_n(reducer[...], cot_whole[:, :, HALVES[half]].reshape(D, HALF))
        low[:, HALVES[half]] = grad.astype(BF)

    bend_root = math.sqrt(2 / math.pi)

    def bend(half):
        for tile in (half * HALF, half * HALF + TILE):
            lanes = slice(tile, tile + TILE)
            pre = total[:, lanes] + bias_column
            square = pre * pre
            curve = jnp.tanh(bend_root * pre * (1 + 0.044715 * square))
            middle = 0.5 * (1 + curve)
            hidden[:, lanes] = (pre * middle).astype(BF)
            slope = middle + 0.5 * pre * (1 - curve * curve) * (bend_root * (1 + 3 * 0.044715 * square))
            grad_pre = low[:, lanes].astype(F32) * slope
            row_sums = jnp.broadcast_to(jnp.sum(grad_pre, 1, keepdims=True), (HIDDEN, 128))
            if tile:
                expand_sum[...] += row_sums
            else:
                expand_sum[...] = row_sums
            low[:, lanes] = grad_pre.astype(BF)

    def fall(half):
        for step, chip in enumerate(reduces[half].order):
            reduces[half].put(chip, dot_f(expander[chip], low[:, HALVES[half]]))
            reduces[half].give(step)
            if step == 1:
                reduces[half].first()

    spread_sems = (spread_send, spread_receive)
    spread_expand = Spread(
        place, "z", grads_expand, passing_expand, early_expand, None, None, None, None, spread_sems, 0
    )
    spread_reduce = Spread(
        place, "y", grads_reduce, passing_reduce, early_reduce, None, None, None, None, spread_sems, 4
    )

    def keep(spread, grads, own, onward, slots):
        low, high = pl.ds(0, SPLIT), pl.ds(SPLIT, CHIP - SPLIT)
        return [
            load(grads.at[place.at[spread.axis]], own, slots),
            load(grads.at[spread.block(1), low], onward.at[low], slots + 1),
            load(grads.at[spread.block(3), high], onward.at[high], slots + 2),
        ]

    def weigh_reduce(half):
        lanes = HALVES[half]
        for chip in range(4):
            put_grads(grads_reduce, "y", chip, dot_t(cot_whole[chip, :, lanes], hidden[:, lanes]), half == 1)

    def weigh_expand(half):
        lanes = HALVES[half]
        for chip in range(4):
            put_grads(grads_expand, "z", chip, dot_t(whole[chip, :, lanes], low[:, lanes]), half == 1)

    def back_start(half):
        lanes = HALVES[half]
        grad = reduces[half].result()
        normed = (after[:, lanes] - stats[2:3, lanes]) * stats[3:4, lanes]
        scaled = grad * gain
        shares[half].start(jnp.sum(scaled, 0, keepdims=True), jnp.sum(scaled * normed, 0, keepdims=True))
        gain_sum = jnp.sum(grad * normed, 1, keepdims=True)
        shift_sum = jnp.sum(grad, 1, keepdims=True)
        if half:
            sums[:, 0:1] += gain_sum
            sums[:, 1:2] += shift_sum
        else:
            sums[:, 0:1] = gain_sum
            sums[:, 1:2] = shift_sum
        grad_after[:, lanes] = scaled

    def back_end(half):
        lanes = HALVES[half]
        share = shares[half]
        share.wait()
        mean = jnp.sum(share.read(0), 0, keepdims=True) / D
        along = jnp.sum(share.read(1), 0, keepdims=True) / D
        normed = (after[:, lanes] - stats[2:3, lanes]) * stats[3:4, lanes]
        grad = stats[3:4, lanes] * (grad_after[:, lanes] - mean - normed * along) + cot[:, lanes]
        grad_after[:, lanes] = grad
        land_two[me, 0:NARROW, lanes] = grad.astype(BF)

    def grow_mixed(half, chip, first=False, last=False):
        lanes = HALVES[half]
        pack(land_two, chip, after_whole, lanes)
        term = dot_n(mixer[chip], after_whole[chip, :, lanes])
        if first:
            total[0:WIN, lanes] = term
        elif last:
            grad_mixed[:, lanes] = (total[0:WIN, lanes] + term).astype(BF)
        else:
            total[0:WIN, lanes] += term

    def back_result(half):
        for tile in (half * HALF, half * HALF + TILE):
            term = dot_f(reducer[...], hidden[:, tile : tile + TILE])
            for index in range(PARTS):
                rows = slice(index * NARROW, (index + 1) * NARROW)
                land_one[index, 0:NARROW, tile : tile + TILE] = term[rows].astype(BF)

    stream_load.wait()
    for half in range(2):
        send_center(half, stream[:, HALVES[half]])
    cot_load.wait()
    land_two[me, 0:NARROW, :] = cot[...].astype(BF)
    cots[0].start_first()
    gain, shift = column(first_gain[...], NARROW), column(first_shift[...], NARROW)
    triple_load.wait()
    for chip in range(4):
        for part in range(3):
            weight[chip, part * NARROW : (part + 1) * NARROW, :] = triple_raw[
                part, :, chip * CHIP : (chip + 1) * CHIP
            ]
    normal(0, stream[:, HALVES[0]], gain, shift, 0)
    firsts[0].start()
    normal(1, stream[:, HALVES[1]], gain, shift, 0)
    weight_copy = load(weight, weight_out, 1)
    mixer_load.wait()
    mixer_edge[0:48, :] = mixer_raw[NARROW - 48 : NARROW, :]
    mixer_edge[48:TAIL, :] = mixer_raw[NARROW - TAIL : NARROW - 48, :]
    sums[:, 3:4] = jnp.sum(cot[...], 1, keepdims=True)
    mixed[3 * HD : WIN, :] = jnp.zeros((HD, LEN), BF)
    firsts[0].near()
    firsts[1].start()
    grow_first(0, place.chip, True)
    firsts[0].middle()
    grow_first(0, place.left_chip)
    grow_first(0, place.right_chip)
    firsts[0].far()
    firsts[0].last()
    grow_first(0, place.far_chip)
    place_triple(0)
    firsts[1].near()
    edge_do(2, True, lambda copy: copy.start())
    cots[0].start_rest()
    grow_first(1, place.chip, True)
    look(0, 1)
    look(0, 2)
    firsts[1].middle()
    grow_first(1, place.left_chip)
    grow_first(1, place.right_chip)
    firsts[1].far()
    place_tail(0)
    edge_do(2, False, lambda copy: copy.wait_recv())
    for chip in range(4):
        lanes = slice(chip * CHIP, (chip + 1) * CHIP)
        wide[0, :, 0:CHIP] = jnp.zeros((WIN + TAIL, CHIP), F32)
        near_rows = mixer_edge_in[0:48, lanes].astype(F32)
        wide[0, pl.ds(pl.multiple_of(8 * me + 8, 8), 48), 0:CHIP] = near_rows
        wide[0, pl.ds(pl.multiple_of(8 * me, 8), 8), 0:CHIP] = mixer_edge_in[48:TAIL, lanes].astype(F32)
        rows = pl.ds(pl.multiple_of(TAIL + 8 * me, 8), NARROW)
        wide[0, rows, 0:CHIP] = mixer_raw[:, lanes].astype(F32)
        mixer[chip] = wide[0, TAIL : TAIL + WIN, 0:CHIP].astype(BF)
    look(0, 0)
    look_last(0)
    mix(0)
    firsts[1].last()
    grow_first(1, place.far_chip)
    place_triple(1)
    first_copy = load(whole, first_out, 7)
    reduces[0].first()
    reduces[0].second()
    cots[0].near()
    look(1, 1)
    look(1, 2)
    reduces[0].third()
    place_tail(1)
    look(1, 0)
    look_last(1)
    mix(1)
    mixer_shift = column(mixer_bias[...], NARROW)
    gain, shift = column(second_gain[...], NARROW), column(second_shift[...], NARROW)
    bias_column = column(expand_bias[...], HIDDEN)
    firsts[0].end()
    add_mixed(0)
    reduces[1].first()
    reduces[1].second()
    cots[0].middle()
    cots[0].far()
    cots[1].start()
    triple_copy = load(triple, triple_out, 8)
    mixed_copy = load(mixed, mixed_out, 9)
    expand_load.wait()
    for chip in range(4):
        expander[chip] = expand_raw[:, chip * CHIP : (chip + 1) * CHIP]
    reduce_load = load(reduce_weight, reducer, 3)
    normal(0, after[:, HALVES[0]], gain, shift, 2)
    firsts[0].start()
    reduces[1].third()
    cots[0].last()
    for chip in range(4):
        pack(land_two, chip, cot_whole, HALVES[0])
    reduce_load.wait()
    pull(0)
    firsts[0].near()
    firsts[1].end()
    add_mixed(1)
    after_copy = load(after, after_out, 13)
    first_copy.wait()
    grow_second(0, place.chip, True)
    cots[1].near()
    firsts[0].middle()
    grow_second(0, place.left_chip)
    grow_second(0, place.right_chip)
    normal(1, after[:, HALVES[1]], gain, shift, 2)
    firsts[1].start()
    firsts[0].far()
    cots[1].middle()
    firsts[0].last()
    grow_second(0, place.far_chip)
    reduces[0].end()
    bend(0)
    fall(0)
    firsts[1].near()
    reduces[0].second()
    grow_second(1, place.chip, True)
    weigh_expand(0)
    cots[1].far()
    cots[1].last()
    for chip in range(4):
        pack(land_two, chip, cot_whole, HALVES[1])
    pull(1)
    firsts[1].middle()
    grow_second(1, place.left_chip)
    grow_second(1, place.right_chip)
    reduces[0].third()
    firsts[1].far()
    weigh_reduce(0)
    firsts[1].last()
    grow_second(1, place.far_chip)
    reduces[1].end()
    bend(1)
    fall(1)
    cots[0].end()
    back_start(0)
    reduces[1].second()
    weigh_reduce(1)
    spread_reduce.start()
    reduces[1].third()
    back_end(0)
    cots[0].start()
    weigh_expand(1)
    spread_expand.start()
    kept = keep(spread_reduce, grads_reduce, own_reduce, onward_reduce, 16)
    kept += keep(spread_expand, grads_expand, own_expand, onward_expand, 19)
    cots[1].end()
    back_start(1)
    firsts[0].end()
    firsts[1].end()
    back_result(0)
    cots[0].near()
    grow_mixed(0, place.chip, True)
    back_end(1)
    cots[1].start()
    grad_after_copy = load(grad_after, grad_after_out, 14)
    back_result(1)
    parts_copy = load(land_one, parts_out, 10)
    cots[0].middle()
    grow_mixed(0, place.left_chip)
    grow_mixed(0, place.right_chip)
    cots[0].far()
    cots[1].near()
    cots[0].last()
    grow_mixed(0, place.far_chip, False, True)
    grow_mixed(1, place.chip, True)
    cots[1].middle()
    grow_mixed(1, place.left_chip)
    grow_mixed(1, place.right_chip)
    sums[:, 2:3] = jnp.sum(grad_after[...], 1, keepdims=True)
    whole_copies = [
        load(after_whole.at[chip], after_whole_out.at[chip], slot)
        for slot, chip in ((0, place.chip), (2, place.left_chip), (3, place.right_chip))
    ]
    cots[1].far()
    cots[1].last()
    grow_mixed(1, place.far_chip, False, True)
    whole_copies.append(load(after_whole.at[place.far_chip], after_whole_out.at[place.far_chip], 22))
    grad_mixed_copy = load(grad_mixed, grad_mixed_out, 15)
    reduces[0].end()
    reduces[1].end()
    for gather in cots:
        gather.end()
    for half in range(3):
        edge_do(half, True, lambda copy: copy.wait_send())
    for spread in (spread_reduce, spread_expand):
        spread.arrive(range(4))
        spread.leave(range(4))
    for copy in (
        weight_copy, triple_copy, mixed_copy, parts_copy, *kept, after_copy, grad_after_copy,
        grad_mixed_copy, *whole_copies, *pending.values(),
    ):
        copy.wait()


def forward(*arguments):
    wide_rows = WIN + TAIL
    return pl.pallas_call(
        forward_kernel,
        out_shape=(
            shape((3 * WIN, LEN), BF),
            shape((4, LEN, LEN), BF),
            shape((WIN, LEN), BF),
            shape((4, CHIP, LEN), BF),
            shape((4, CHIP, LEN), BF),
            shape((PARTS, ROWS, LEN), BF),
            shape((4, 3 * NARROW, CHIP), BF),
            *[shape((CHIP, HIDDEN), BF)] * 8,
            shape((NARROW, LEN), F32),
            shape((NARROW, LEN), F32),
            shape((WIN, LEN), BF),
            shape((8, LEN), F32),
            shape((NARROW, 128), F32),
            shape((HIDDEN, 128), F32),
        ),
        in_specs=vmem(7) + hbm(6),
        out_specs=tuple(hbm(18) + vmem(3)),
        scratch_shapes=[
            *[pltpu.VMEM((NARROW, LEN), F32)] * 4,
            pltpu.VMEM((WIN, LEN), BF),
            pltpu.VMEM((3, NARROW, D), BF),
            pltpu.VMEM((NARROW, D), BF),
            pltpu.VMEM((HIDDEN, D), BF),
            pltpu.VMEM((4, 3 * NARROW, CHIP), BF),
            pltpu.VMEM((4, WIN, CHIP), BF),
            pltpu.VMEM((4, HIDDEN, CHIP), BF),
            pltpu.VMEM((3, HD, LEN), BF),
            pltpu.VMEM((3, HD, LEN), BF),
            pltpu.VMEM((HD, D), BF),
            pltpu.VMEM((HD, D), BF),
            pltpu.VMEM((3, WIN + TAIL, LEN), F32),
            pltpu.VMEM((PARTS, ROWS, LEN), BF),
            pltpu.VMEM((PARTS, ROWS, LEN), BF),
            pltpu.VMEM((4, CHIP, LEN), BF),
            pltpu.VMEM((4, CHIP, LEN), BF),
            pltpu.VMEM((HIDDEN, LEN), F32),
            pltpu.VMEM((3 * WIN, LEN), BF),
            pltpu.VMEM((WIN, LEN), BF),
            pltpu.VMEM((3, LEN, TILE), BF),
            pltpu.VMEM((HIDDEN, LEN), BF),
            pltpu.VMEM((HIDDEN, LEN), BF),
            pltpu.VMEM((4, CHIP, HIDDEN), BF),
            pltpu.VMEM((4, CHIP, HIDDEN), BF),
            pltpu.VMEM((2, PARTS, 8, 128), F32),
            *REDUCE_BUFFERS,
            sems(23),
            sems(52),
            sems(52),
            sems(20),
            sems(20),
            sems(14),
            sems(14),
            sems(3),
            sems(3),
            sems(8),
            sems(8),
        ],
        compiler_params=params(1),
        name="forward",
    )(*arguments)


VECTORS = 12


def backward_kernel(
    stats, first_gain, reduce_bias, second_sums, expand_sum,
    stream_in, after_in_rows, grad_after_in, triple_in, probs_in, mixed_in, grad_mixed_in, first_in, after_in, parts_in, weight_in,
    own_expand_in, passing_expand_in, early_expand_in, onward_expand_in,
    own_reduce_in, passing_reduce_in, early_reduce_in, onward_reduce_in,
    result, grad_stream, out_triple, out_mixer, out_expand, out_reduce,
    out_gain, out_shift, out_bias, out_mixer_bias, out_second_gain, out_second_shift, out_expand_bias,
    out_reduce_bias,
    stream, after, grad_after, triple, probs, mixed, grad_mixed, first_whole, after_whole, weight,
    grad_triple, own, wide, edge, edge_in, keys_total, tiles, sums, table,
    parts_one, twin_one, one_in, left_two, right_two,
    parts_two, twin_two, two_in, left_four, right_four,
    own_expand, passing_expand, early_expand, onward_expand, late_expand, middle_expand, second_expand,
    own_reduce, passing_reduce, early_reduce, onward_reduce, late_reduce, middle_reduce, second_reduce,
    grads_mixer, passing_mixer, early_mixer, late_mixer, middle_mixer, second_mixer,
    grads_z, passing_z, early_z, late_z, middle_z, second_z,
    grads_y, passing_y, early_y, late_y, middle_y, second_y,
    local, probs_sems, reduce_send, reduce_receive, share_send, share_receive, edge_send, edge_receive,
    spread_send, spread_receive, table_send, table_receive,
):
    place = Place()
    me = place.me
    group = place.group

    def load(source, target, slot):
        copy = pltpu.make_async_copy(source, target, local.at[slot])
        copy.start()
        return copy

    triple_load = load(triple_in, triple, 0)
    grad_mixed_load = load(grad_mixed_in, grad_mixed, 1)
    mixed_load = load(mixed_in, mixed, 2)

    def probs_copy(h, tile):
        reach = tile + TILE
        return pltpu.make_async_copy(
            probs_in.at[h, pl.ds(0, reach), pl.ds(tile, TILE)],
            probs.at[h, pl.ds(0, reach), pl.ds(tile, TILE)],
            probs_sems.at[4 * h + tile // TILE],
        )

    tiles_of = ((TILE, 0), (3 * TILE, 2 * TILE))

    def probs_load(half, h):
        for tile in tiles_of[half]:
            probs_copy(h, tile).start()

    probs_load(1, 0)
    pass_loads = [
        load(onward_reduce_in, onward_reduce, 5),
        load(passing_reduce_in, passing_reduce, 6),
        load(onward_expand_in, onward_expand, 7),
        load(passing_expand_in, passing_expand, 8),
    ]
    probs_load(1, 1)
    parts_load = load(parts_in, parts_one, 3)
    probs_load(1, 2)

    @pl.when(place.last)
    def _():
        probs_load(1, 3)

    weight_load = load(weight_in, weight, 4)
    turn_loads = [
        load(early_reduce_in, early_reduce, 9),
        load(own_reduce_in, own_reduce, 10),
        load(early_expand_in, early_expand, 16),
        load(own_expand_in, own_expand, 17),
    ]
    for h in range(3):
        probs_load(0, h)

    @pl.when(place.last)
    def _():
        probs_load(0, 3)

    first_load = load(first_in, first_whole, 12)
    row_loads = [
        load(stream_in, stream, 13),
        load(after_in_rows, after, 14),
        load(grad_after_in, grad_after, 15),
    ]
    after_load = load(after_in, after_whole, 11)
    others = [lax.rem(group + i, 16) for i in range(1, 16)]
    greet([{"mp": peer} for peer in place.peers] + [{"dp": other} for other in others])
    reduce_sems = (reduce_send, reduce_receive)
    edge_sems = (edge_send, edge_receive)
    spread_sems = (spread_send, spread_receive)
    shares = [Share(place, tiles.at[half], (share_send, share_receive), 7 * half) for half in range(2)]
    one = (parts_one, twin_one, one_in, left_two, right_two)
    two = (parts_two, twin_two, two_in, left_four, right_four)
    outs = [Reduce(place, one, half, reduce_sems, 10 * half) for half in range(2)]
    reduces = [Reduce(place, two, half, reduce_sems, 20 + 10 * half) for half in range(2)]
    spread_expand = Spread(
        place, "z", None, passing_expand, early_expand, passing_expand, late_expand, middle_expand, second_expand, spread_sems, 0
    )
    spread_reduce = Spread(
        place, "y", None, passing_reduce, early_reduce, passing_reduce, late_reduce, middle_reduce, second_reduce, spread_sems, 9
    )
    spread_mixer = Spread(
        place, "z", grads_mixer, passing_mixer, early_mixer, passing_mixer, late_mixer, middle_mixer, second_mixer, spread_sems, 18
    )
    spread_z = Spread(
        place, "z", grads_z, passing_z, early_z, passing_z, late_z, middle_z, second_z, spread_sems, 27
    )
    spread_y = Spread(
        place, "y", grads_y, passing_y, early_y, passing_y, late_y, middle_y, second_y, spread_sems, 36
    )

    def edge_copy(step):
        if step == 2:
            piece, target = edge.at[3], edge_in.at[3]
        else:
            lanes = pl.ds(step * HALF, HALF)
            piece, target = edge.at[0:3, :, lanes], edge_in.at[0:3, :, lanes]
        return remote(piece, target, edge_sems, step, place.previous)

    mixed_load.wait()
    edge[3] = mixed[0:HD, :]
    edge_copy(2).start()
    grad_triple[...] = jnp.zeros((3 * WIN, LEN), BF)
    triple_load.wait()
    grad_mixed_load.wait()

    def attend(half, h):
        row = HD * h
        keys = triple[WIN + row : WIN + row + HD, :]
        values = triple[2 * WIN + row : 2 * WIN + row + HD, :]
        for tile in reversed(tiles_of[half]) if half == 0 else tiles_of[half]:
            probs_copy(h, tile).wait()
        for tile in tiles_of[half]:
            reach = tile + TILE
            lanes = slice(tile, reach)
            queries = triple[row : row + HD, lanes] * jnp.asarray(ROOT, BF)
            grad_out = grad_mixed[row : row + HD, lanes]
            delta = jnp.sum(
                grad_out.astype(F32) * mixed[row : row + HD, lanes].astype(F32), 0, keepdims=True
            )
            chances = probs[h, 0:reach, lanes]
            grad_probs = dot_f(values[:, 0:reach], grad_out)
            grad_scores = (chances.astype(F32) * (grad_probs - delta)).astype(BF)
            grad_queries = dot_n(keys[:, 0:reach], grad_scores) * ROOT
            grad_triple[row : row + HD, lanes] = grad_queries.astype(BF)
            key_term = dot_t(queries, grad_scores)
            value_term = dot_t(grad_out, chances)
            if reach == LEN:
                keys_total[h, 0] = key_term
                keys_total[h, 1] = value_term
            else:
                keys_total[h, 0, :, 0:reach] += key_term
                keys_total[h, 1, :, 0:reach] += value_term
        lanes = HALVES[half]
        grad_triple[WIN + row : WIN + row + HD, lanes] = keys_total[h, 0, :, lanes].astype(BF)
        grad_triple[2 * WIN + row : 2 * WIN + row + HD, lanes] = keys_total[h, 1, :, lanes].astype(BF)

    def attend_last(half):
        @pl.when(place.last)
        def _():
            attend(half, 3)

    def send_edge(half):
        for part in range(3):
            edge[part, :, HALVES[half]] = grad_triple[part * WIN : part * WIN + HD, HALVES[half]]
        edge_copy(half).start()

    def place_own(part, lanes):
        if part < 3:
            piece = grad_triple[part * WIN : (part + 1) * WIN, lanes]
        else:
            piece = mixed[:, lanes]
        piece = piece.astype(F32)
        wide[0 : 3 * HD, lanes] = piece[0 : 3 * HD]
        neighbour = edge_in[part, :, lanes].astype(F32)
        wide[3 * HD : WIN, lanes] = jnp.where(place.last, piece[3 * HD : WIN], neighbour)
        values = wide[pl.ds(pl.multiple_of(8 * me, 8), NARROW), lanes]
        own[part * NARROW : (part + 1) * NARROW, lanes] = values.astype(BF)
        return jnp.sum(values, 1, keepdims=True)

    def place_rows(half):
        edge_copy(half).wait_recv()
        for part in range(3):
            total = place_own(part, HALVES[half])
            if half == 1:
                sums[:, 2 + part : 3 + part] = total
            else:
                sums[:, 2 + part : 3 + part] += total

    def fall(half, rows=True):
        if rows:
            place_rows(half)
        for step, chip in enumerate(reduces[half].order):
            reduces[half].put(chip, dot_f(weight[chip], own[0 : 3 * NARROW, HALVES[half]]))
            reduces[half].give(step)
            if step == 1:
                reduces[half].first()

    def weigh(axis, grads, whole, rows):
        for chip in range(4):
            put_grads(grads, axis, chip, dot_t(whole[chip], own[rows, :]))

    attend(1, 0)
    send_edge(1)
    for copy in pass_loads:
        copy.wait()
    spread_reduce.pass_on(lambda rows: onward_reduce[rows])
    spread_expand.pass_on(lambda rows: onward_expand[rows])
    parts_load.wait()
    for half in (1, 0):
        for step in range(4):
            outs[half].give(step)
    attend(1, 1)
    outs[1].first()
    outs[0].first()
    attend(1, 2)
    attend_last(1)
    weight_load.wait()
    fall(1)
    attend(0, 0)
    send_edge(0)
    reduces[1].second()
    outs[1].second()
    attend(0, 1)
    for copy in turn_loads:
        copy.wait()
    spread_reduce.arrive((4, 5))
    spread_reduce.turn(own_reduce[...])
    spread_expand.arrive((4, 5))
    spread_expand.turn(own_expand[...])
    attend(0, 2)
    attend_last(0)
    outs[0].second()
    first_load.wait()
    place_rows(0)
    weigh("y", grads_y, first_whole, slice(WIN, 3 * NARROW))
    spread_y.start()
    weigh("z", grads_z, first_whole, slice(0, WIN))
    spread_z.start()
    reduces[1].third()
    fall(0, False)
    outs[1].third()
    edge_copy(2).wait_recv()
    place_own(3, slice(0, LEN))
    after_load.wait()
    weigh("z", grads_mixer, after_whole, slice(3 * NARROW, 4 * NARROW))
    spread_mixer.start()
    reduces[0].second()
    spread_z.arrive((0, 1))
    spread_z.pass_on(spread_z.mine)
    spread_y.arrive((0, 1))
    spread_y.pass_on(spread_y.mine)
    reduces[0].third()
    outs[0].third()
    for copy in row_loads:
        copy.wait()
    gain = column(first_gain[...], NARROW)
    shift = column(reduce_bias[...], NARROW)

    def back_start(half):
        lanes = HALVES[half]
        grad = reduces[half].result()
        normed = (stream[:, lanes] - stats[0:1, lanes]) * stats[1:2, lanes]
        scaled = grad * gain
        shares[half].start(jnp.sum(scaled, 0, keepdims=True), jnp.sum(scaled * normed, 0, keepdims=True))
        gain_sum = jnp.sum(grad * normed, 1, keepdims=True)
        shift_sum = jnp.sum(grad, 1, keepdims=True)
        if half == 1:
            sums[:, 0:1] = gain_sum
            sums[:, 1:2] = shift_sum
        else:
            sums[:, 0:1] += gain_sum
            sums[:, 1:2] += shift_sum
        grad_stream[:, lanes] = scaled

    def back_end(half):
        lanes = HALVES[half]
        share = shares[half]
        share.wait()
        mean = jnp.sum(share.read(0), 0, keepdims=True) / D
        along = jnp.sum(share.read(1), 0, keepdims=True) / D
        normed = (stream[:, lanes] - stats[0:1, lanes]) * stats[1:2, lanes]
        back = stats[1:2, lanes] * (grad_stream[:, lanes] - mean - normed * along)
        grad_stream[:, lanes] = back + grad_after[:, lanes]

    back_start(1)
    for half in range(2):
        result[:, HALVES[half]] = outs[half].result() + after[:, HALVES[half]] + shift
    out_expand[...] = spread_expand.result()
    out_reduce[...] = spread_reduce.result()
    back_end(1)
    back_start(0)
    columns = [
        sums[:, 0:1], sums[:, 1:2], sums[:, 2:3], sums[:, 4:5],
        second_sums[:, 2:3], second_sums[:, 0:1], second_sums[:, 1:2], second_sums[:, 3:4],
    ]
    columns += [expand_sum[NARROW * i : NARROW * (i + 1), 0:1] for i in range(4)]
    spot = lax.broadcasted_iota(jnp.int32, (NARROW, 128), 1)
    packed = jnp.zeros((NARROW, 128), F32)
    for i, values in enumerate(columns):
        packed = jnp.where(spot == i, values, packed)
    table[group] = packed.T[0:16]

    def table_copy(step, owner, device):
        return remote(table.at[owner], table.at[owner], (table_send, table_receive), step, device, "dp")

    for step, other in enumerate(others):
        table_copy(step, group, other).start()
    back_end(0)
    spread_z.arrive(range(2, 6))
    spread_z.turn(grads_z[place.at["z"]])
    spread_mixer.arrive((0, 1))
    spread_mixer.pass_on(spread_mixer.mine)
    spread_y.arrive(range(2, 6))
    spread_y.turn(grads_y[place.at["y"]])
    for step in range(15):
        table_copy(step, lax.rem(group + 15 - step, 16), group).wait_recv()
    vectors = jnp.sum(table[...], 0)
    out_gain[...] = vectors[0:1].reshape(NARROW)
    out_shift[...] = vectors[1:2].reshape(NARROW)
    out_bias[...] = vectors[2:4]
    out_mixer_bias[...] = vectors[4:5].reshape(NARROW)
    out_second_gain[...] = vectors[5:6].reshape(NARROW)
    out_second_shift[...] = vectors[6:7].reshape(NARROW)
    out_reduce_bias[...] = vectors[7:8].reshape(NARROW)
    out_expand_bias[...] = vectors[8:12]
    spread_mixer.arrive(range(2, 6))
    spread_mixer.turn(grads_mixer[place.at["z"]])
    rest = jnp.concatenate([spread_z.result(), spread_y.result()], 1)
    for part in range(3):
        out_triple[part] = rest[:, part * NARROW : (part + 1) * NARROW].T
    out_mixer[...] = spread_mixer.result().T
    for reduce in outs + reduces:
        reduce.end()
    for step in range(3):
        edge_copy(step).wait_send()
    for spread in (spread_expand, spread_reduce):
        spread.leave(range(4, 9))
    for spread in (spread_mixer, spread_z, spread_y):
        spread.leave(range(9))
    for step, other in enumerate(others):
        table_copy(step, group, other).wait_send()


def spread_scratch(lanes, whole):
    one = pltpu.VMEM((CHIP, lanes), BF)
    ends = [pltpu.VMEM((4, DEEP, lanes), BF), pltpu.VMEM((3, DEEP, lanes), BF)]
    return [pltpu.VMEM((4, CHIP, lanes), BF) if whole else one] + [one] * (3 if whole else 4) + ends


def backward(*arguments):
    width = 4 * NARROW
    return pl.pallas_call(
        backward_kernel,
        out_shape=(
            shape((NARROW, LEN), F32),
            shape((NARROW, LEN), F32),
            shape((3, NARROW, 100), F32),
            shape((NARROW, 100), F32),
            shape((100, HIDDEN), F32),
            shape((100, HIDDEN), F32),
            shape((NARROW,), F32),
            shape((NARROW,), F32),
            shape((2, NARROW), F32),
            shape((NARROW,), F32),
            shape((NARROW,), F32),
            shape((NARROW,), F32),
            shape((4, NARROW), F32),
            shape((NARROW,), F32),
        ),
        in_specs=vmem(5) + hbm(19),
        out_specs=tuple(vmem(14)),
        scratch_shapes=[
            *[pltpu.VMEM((NARROW, LEN), F32)] * 3,
            pltpu.VMEM((3 * WIN, LEN), BF),
            pltpu.VMEM((4, LEN, LEN), BF),
            pltpu.VMEM((WIN, LEN), BF),
            pltpu.VMEM((WIN, LEN), BF),
            pltpu.VMEM((4, CHIP, LEN), BF),
            pltpu.VMEM((4, CHIP, LEN), BF),
            pltpu.VMEM((4, 3 * NARROW, CHIP), BF),
            pltpu.VMEM((3 * WIN, LEN), BF),
            pltpu.VMEM((width, LEN), BF),
            pltpu.VMEM((WIN, LEN), F32),
            pltpu.VMEM((4, HD, LEN), BF),
            pltpu.VMEM((4, HD, LEN), BF),
            pltpu.VMEM((4, 2, HD, LEN), F32),
            pltpu.VMEM((2, PARTS, 8, 128), F32),
            pltpu.VMEM((NARROW, 128), F32),
            pltpu.VMEM((16, 16, NARROW), F32),
            *REDUCE_BUFFERS,
            *REDUCE_BUFFERS,
            *spread_scratch(HIDDEN, False),
            *spread_scratch(HIDDEN, False),
            *spread_scratch(NARROW, True),
            *spread_scratch(WIN, True),
            *spread_scratch(3 * NARROW - WIN, True),
            sems(18),
            sems(16),
            sems(40),
            sems(40),
            sems(14),
            sems(14),
            sems(3),
            sems(3),
            sems(45),
            sems(45),
            sems(15),
            sems(15),
        ],
        compiler_params=params(2),
        name="backward",
    )(*arguments)


def hand_over_kernel(*refs):
    count = len(refs) // 2
    for source, target in zip(refs[:count], refs[count:]):
        if source.shape == target.shape:
            target[...] = source[...]
        else:
            rows = [source[i : i + 1, :] for i in range(source.shape[0])]
            target[...] = jnp.concatenate(rows, 1).reshape(target.shape)


def hand_over(*arrays):
    count = len(arrays)
    return pl.pallas_call(
        hand_over_kernel,
        out_shape=tuple(
            shape((HIDDEN,) if array.shape == (4, NARROW) else array.shape, array.dtype) for array in arrays
        ),
        in_specs=vmem(count),
        out_specs=tuple(vmem(count)),
        compiler_params=pltpu.CompilerParams(vmem_limit_bytes=VMEM_LIMIT),
        name="hand_over",
    )(*arrays)


def shards(
    stream, first_gain, first_shift, triple_weight, triple_bias, mixer_weight, mixer_bias,
    second_gain, second_shift, expand_weight, expand_bias, reduce_weight, reduce_bias, cotangent,
):
    turned = stream.T
    (
        triple, probs, mixed, first_whole, after_whole, parts, weight,
        *spreads,
        after, grad_after, grad_mixed, stats, sums, expand_sum,
    ) = forward(
        first_gain, first_shift, triple_bias, mixer_bias, second_gain, second_shift, expand_bias,
        turned, cotangent.T, triple_weight.transpose(1, 2, 0), mixer_weight, expand_weight.T, reduce_weight,
    )
    (
        result, grad_stream, out_triple, out_mixer, out_expand, out_reduce,
        out_gain, out_shift, out_bias, out_mixer_bias, out_second_gain, out_second_shift, out_expand_bias,
        out_reduce_bias,
    ) = hand_over(*backward(
        stats, first_gain, reduce_bias, sums, expand_sum,
        turned, after, grad_after, triple, probs, mixed, grad_mixed, first_whole, after_whole, parts, weight, *spreads,
    ))
    return (
        result.T,
        grad_stream.T,
        out_gain,
        out_shift,
        out_triple.transpose(2, 0, 1),
        out_bias,
        out_mixer,
        out_mixer_bias,
        out_second_gain,
        out_second_shift,
        out_expand,
        out_expand_bias,
        out_reduce.T,
        out_reduce_bias,
    )


def solution(mesh):
    placed = (
        P("dp", "mp"),
        P("mp"),
        P("mp"),
        P(None, None, "mp"),
        P(None, "mp"),
        P("mp", None),
        P("mp"),
        P("mp"),
        P("mp"),
        P(None, "mp"),
        P("mp"),
        P("mp", None),
        P("mp"),
        P("dp", "mp"),
    )
    return jax.shard_map(
        shards,
        mesh=mesh,
        in_specs=placed,
        out_specs=(
            P("dp", "mp"),
            P("dp", "mp"),
            P("mp"),
            P("mp"),
            P("dp", None, "mp"),
            P(None, "mp"),
            P("mp", "dp"),
            P("mp"),
            P("mp"),
            P("mp"),
            P("dp", "mp"),
            P("mp"),
            P("mp", "dp"),
            P("mp"),
        ),
        check_vma=False,
    )
```

```python
import math

import jax
import jax.numpy as jnp
from jax import lax
from jax.experimental import pallas as pl
from jax.experimental.pallas import tpu as pltpu
from jax.sharding import PartitionSpec as P

HD = 64
LEN = 1024
D = 1600
PARTS = 8
NARROW = D // PARTS
HIDDEN = 800
CHIP = 400
ROWS = 208
DEEP = 112
SPLIT = 208
WIN = 256
TAIL = WIN - NARROW
HALF = LEN // 2
TILE = 256
EPSILON = 1e-05
ROOT = 1 / math.sqrt(HD)
MESH = pl.DeviceIdType.MESH
BF = jnp.bfloat16
F32 = jnp.float32
VMEM_LIMIT = 62 * 1024 * 1024


def dot_n(left, right):
    return lax.dot_general(left, right, (((1,), (0,)), ((), ())), preferred_element_type=F32)


def dot_t(left, right):
    return lax.dot_general(left, right, (((1,), (1,)), ((), ())), preferred_element_type=F32)


def dot_f(left, right):
    return lax.dot_general(left, right, (((0,), (0,)), ((), ())), preferred_element_type=F32)


class Place:
    def __init__(self):
        self.me = lax.axis_index("mp")
        self.chip = self.me // 2
        self.core = self.me % 2
        self.right_chip = lax.rem(self.chip + 1, 4)
        self.left_chip = lax.rem(self.chip + 3, 4)
        self.far_chip = lax.rem(self.chip + 2, 4)
        self.right = self.right_chip * 2 + self.core
        self.left = self.left_chip * 2 + self.core
        self.far = self.far_chip * 2 + self.core
        self.twin = self.chip * 2 + 1 - self.core
        self.peers = [lax.rem(self.me + i, PARTS) for i in range(1, PARTS)]
        self.previous = lax.rem(self.me + PARTS - 1, PARTS)
        self.following = lax.rem(self.me + 1, PARTS)
        self.last = self.me == PARTS - 1
        self.group = lax.axis_index("dp")
        self.at = {"z": self.group // 4, "y": self.group % 4}

    def along(self, axis, step):
        at = lax.rem(self.at[axis] + step, 4)
        z, y = (at, self.at["y"]) if axis == "z" else (self.at["z"], at)
        return at, z * 4 + y


def greet(devices):
    barrier = pltpu.get_barrier_semaphore()
    for device in devices:
        pl.semaphore_signal(barrier, inc=1, device_id=device, device_id_type=MESH)
    pl.semaphore_wait(barrier, len(devices))


def remote(source, target, sems, step, device, axis="mp"):
    send, receive = sems
    return pltpu.make_async_remote_copy(
        src_ref=source,
        dst_ref=target,
        send_sem=send.at[step],
        recv_sem=receive.at[step],
        device_id={axis: device},
        device_id_type=MESH,
    )


class Share:
    def __init__(self, place, tiles, sems, offset):
        self.place, self.tiles, self.sems, self.offset = place, tiles, sems, offset

    def copy(self, step, owner, device):
        tile = self.tiles.at[owner]
        return remote(tile, tile, self.sems, self.offset + step, device)

    def start(self, *vectors):
        rows = HALF // 128
        for i, vector in enumerate(vectors):
            for j in range(rows):
                piece = vector[:, 128 * j : 128 * j + 128]
                self.tiles[self.place.me, rows * i + j : rows * i + j + 1, :] = piece
        for step, peer in enumerate(self.place.peers):
            self.copy(step, self.place.me, peer).start()

    def wait(self):
        me = self.place.me
        for step in range(PARTS - 1):
            owner = lax.rem(me + PARTS - 1 - step, PARTS)
            self.copy(step, owner, me).wait_recv()
        for step, peer in enumerate(self.place.peers):
            self.copy(step, me, peer).wait_send()

    def read(self, index):
        rows = HALF // 128
        return jnp.concatenate([self.tiles[:, rows * index + j, :] for j in range(rows)], 1)


class Gather:
    COUNT = 13

    def __init__(self, place, blocks, half, sems, offset):
        self.place, self.blocks, self.base = place, blocks, half * HALF
        self.sems, self.offset = sems, offset

    def copy(self, step, owner, side, device):
        if side is None:
            lanes = pl.ds(self.base, HALF)
        else:
            lanes = pl.ds(self.base + side * TILE, TILE)
        block = self.blocks.at[owner, :, lanes]
        return remote(block, block, self.sems, self.offset + step, device)

    def other(self, owner):
        return owner + 1 - 2 * self.place.core

    def start(self):
        self.start_first()
        self.start_rest()

    def start_first(self):
        p = self.place
        self.copy(0, p.me, 0, p.right).start()
        self.copy(3, p.me, 1, p.left).start()

    def start_rest(self):
        p = self.place
        self.copy(1, p.me, 1, p.right).start()
        self.copy(4, p.me, 0, p.left).start()
        self.copy(6, p.me, None, p.twin).start()

    def near(self):
        p = self.place
        self.copy(0, p.left, 0, p.me).wait_recv()
        self.copy(2, p.left, 0, p.right).start()
        self.copy(7, p.left, 0, p.twin).start()
        self.copy(3, p.right, 1, p.me).wait_recv()
        self.copy(5, p.right, 1, p.left).start()
        self.copy(8, p.right, 1, p.twin).start()
        self.copy(6, p.twin, None, p.me).wait_recv()

    def middle(self):
        p = self.place
        self.copy(1, p.left, 1, p.me).wait_recv()
        self.copy(9, p.left, 1, p.twin).start()
        self.copy(4, p.right, 0, p.me).wait_recv()
        self.copy(10, p.right, 0, p.twin).start()
        self.copy(7, self.other(p.left), 0, p.me).wait_recv()
        self.copy(8, self.other(p.right), 1, p.me).wait_recv()
        self.copy(9, self.other(p.left), 1, p.me).wait_recv()
        self.copy(10, self.other(p.right), 0, p.me).wait_recv()

    def far(self):
        p = self.place
        self.copy(2, p.far, 0, p.me).wait_recv()
        self.copy(11, p.far, 0, p.twin).start()
        self.copy(5, p.far, 1, p.me).wait_recv()
        self.copy(12, p.far, 1, p.twin).start()

    def last(self):
        p = self.place
        self.copy(11, self.other(p.far), 0, p.me).wait_recv()
        self.copy(12, self.other(p.far), 1, p.me).wait_recv()

    def end(self):
        p = self.place
        for step, owner, side, device in (
            (0, p.me, 0, p.right),
            (1, p.me, 1, p.right),
            (2, p.left, 0, p.right),
            (3, p.me, 1, p.left),
            (4, p.me, 0, p.left),
            (5, p.right, 1, p.left),
            (6, p.me, None, p.twin),
            (7, p.left, 0, p.twin),
            (8, p.right, 1, p.twin),
            (9, p.left, 1, p.twin),
            (10, p.right, 0, p.twin),
            (11, p.far, 0, p.twin),
            (12, p.far, 1, p.twin),
        ):
            self.copy(step, owner, side, device).wait_send()


class Reduce:
    COUNT = 10

    def __init__(self, place, buffers, half, sems, offset):
        self.place, self.base = place, half * HALF
        self.parts, self.twin, self.left_one, self.left_two, self.right_two = buffers
        self.right_one = self.left_one
        self.sems, self.offset = sems, offset
        self.order = [place.far_chip, place.right_chip, place.left_chip, place.chip]
        self.lanes = slice(self.base, self.base + HALF)
        self.low = slice(self.base, self.base + TILE)
        self.high = slice(self.base + TILE, self.base + HALF)

    def copy(self, step):
        p = self.place
        both, low, high = pl.ds(self.base, HALF), pl.ds(self.base, TILE), pl.ds(self.base + TILE, TILE)
        if step < 4:
            chip = self.order[step]
            source = self.parts.at[2 * chip + 1 - p.core, :, both]
            target = self.twin.at[chip, :, both]
            device = p.twin
        elif step == 4:
            source, target, device = self.parts.at[p.far, :, low], self.left_one.at[:, low], p.right
        elif step == 5:
            source, target, device = self.parts.at[p.far, :, high], self.right_one.at[:, high], p.left
        elif step == 6:
            source, target, device = self.parts.at[p.right, :, high], self.left_two.at[:, high], p.right
        elif step == 7:
            source, target, device = self.parts.at[p.right, :, low], self.left_two.at[:, low], p.right
        elif step == 8:
            source, target, device = self.parts.at[p.left, :, low], self.right_two.at[:, low], p.left
        else:
            source, target, device = self.parts.at[p.left, :, high], self.right_two.at[:, high], p.left
        return remote(source, target, self.sems, self.offset + step, device)

    def arrived(self, step):
        both, low, high = pl.ds(self.base, HALF), pl.ds(self.base, TILE), pl.ds(self.base + TILE, TILE)
        if step < 4:
            target = self.twin.at[self.order[step], :, both]
        else:
            target = (
                self.left_one.at[:, low],
                self.right_one.at[:, high],
                self.left_two.at[:, high],
                self.left_two.at[:, low],
                self.right_two.at[:, low],
                self.right_two.at[:, high],
            )[step - 4]
        remote(target, target, self.sems, self.offset + step, self.place.me).wait_recv()

    def put(self, chip, term):
        for core in range(2):
            rows = term[core * NARROW : (core + 1) * NARROW]
            self.parts[2 * chip + core, 0:NARROW, self.lanes] = rows.astype(BF)

    def give(self, step):
        self.copy(step).start()

    def fold(self, step):
        self.arrived(step)
        chip = self.order[step]
        mine = 2 * chip + self.place.core
        total = self.parts[mine, :, self.lanes].astype(F32) + self.twin[chip, :, self.lanes].astype(F32)
        self.parts[mine, :, self.lanes] = total.astype(BF)

    def first(self):
        self.fold(0)
        self.copy(4).start()
        self.copy(5).start()

    def second(self):
        self.fold(1)
        self.copy(6).start()
        self.fold(2)
        self.copy(8).start()

    def third(self):
        p = self.place
        self.arrived(4)
        held = self.parts[p.right, :, self.low].astype(F32)
        self.parts[p.right, :, self.low] = (held + self.left_one[:, self.low].astype(F32)).astype(BF)
        self.copy(7).start()
        self.arrived(5)
        held = self.parts[p.left, :, self.high].astype(F32)
        self.parts[p.left, :, self.high] = (held + self.right_one[:, self.high].astype(F32)).astype(BF)
        self.copy(9).start()
        self.fold(3)

    def result(self):
        for step in range(6, 10):
            self.arrived(step)
        total = self.parts[self.place.me, 0:NARROW, self.lanes].astype(F32)
        total += self.left_two[0:NARROW, self.lanes].astype(F32)
        return total + self.right_two[0:NARROW, self.lanes].astype(F32)

    def end(self):
        for step in range(10):
            self.copy(step).wait_send()


REDUCE_BUFFERS = [
    pltpu.VMEM((PARTS, ROWS, LEN), BF),
    pltpu.VMEM((4, ROWS, LEN), BF),
    pltpu.VMEM((ROWS, LEN), BF),
    pltpu.VMEM((ROWS, LEN), BF),
    pltpu.VMEM((ROWS, LEN), BF),
]


class Spread:
    COUNT = 9
    LOW, HIGH = slice(0, SPLIT), slice(SPLIT, CHIP)

    def __init__(self, place, axis, grads, passing, early, onward, late, middle, second_in, sems, offset):
        self.place, self.axis, self.other = place, axis, "zy".replace(axis, "")
        self.grads, self.passing, self.early = grads, passing, early
        self.onward, self.late = onward, late
        self.middle, self.second_in = middle, second_in
        self.sems, self.offset = sems, offset

    def block(self, away):
        return self.place.along(self.axis, away)[0]

    def copy(self, step):
        low, high = pl.ds(0, SPLIT), pl.ds(SPLIT, CHIP - SPLIT)
        if step < 6:
            away, rows, target, way = (
                (2, low, self.passing, 1),
                (2, high, self.passing, 3),
                (1, high, self.early, 1),
                (3, low, self.early, 3),
                (None, low, self.late, 1),
                (None, high, self.late, 3),
            )[step]
            source = self.onward.at[rows] if away is None else self.grads.at[self.block(away), rows]
            device = self.place.along(self.axis, way)[1]
            target = target.at[rows]
        else:
            at, device = self.place.along(self.other, step - 5)
            source, target = self.middle.at[at], self.second_in.at[step - 6]
        return remote(source, target, self.sems, self.offset + step, device, "dp")

    def start(self):
        for step in range(4):
            self.copy(step).start()

    def arrive(self, steps):
        for step in steps:
            self.copy(step).wait_recv()

    def pass_on(self, held):
        for step, rows in ((4, self.LOW), (5, self.HIGH)):
            self.onward[rows] = (held(rows).astype(F32) + self.passing[rows].astype(F32)).astype(BF)
            self.copy(step).start()

    def mine(self, rows):
        return self.grads[self.block(1 if rows == self.LOW else 3), rows]

    def turn(self, own):
        total = own.astype(F32) + self.early[...].astype(F32) + self.late[...].astype(F32)
        for part in range(4):
            self.middle[part, 0:100] = total[100 * part : 100 * part + 100].astype(BF)
        for step in range(6, 9):
            self.copy(step).start()

    def result(self):
        self.arrive(range(6, 9))
        total = self.middle[self.place.at[self.other], 0:100].astype(F32)
        for step in range(3):
            total += self.second_in[step, 0:100].astype(F32)
        return total

    def leave(self, steps):
        for step in steps:
            self.copy(step).wait_send()


def pack(blocks, chip, whole, lanes):
    whole[chip, 0:NARROW, lanes] = blocks[2 * chip, 0:NARROW, lanes]
    whole[chip, NARROW:CHIP, lanes] = blocks[2 * chip + 1, 0:NARROW, lanes]


def put_grads(grads, axis, chip, term, add=False):
    if axis == "z":
        places = [(chip, slice(0, CHIP), slice(0, CHIP))]
    else:
        rows = slice(100 * chip, 100 * chip + 100)
        places = [(part, rows, slice(100 * part, 100 * part + 100)) for part in range(4)]
    for block, rows, source in places:
        values = term[source]
        if add:
            values += grads[block, rows].astype(F32)
        grads[block, rows] = values.astype(BF)


def column(vector, count):
    return jnp.broadcast_to(vector.reshape(1, count), (8, count)).T[:, 0:1]


def vmem(count):
    return [pl.BlockSpec(memory_space=pltpu.VMEM)] * count


def hbm(count):
    return [pl.BlockSpec(memory_space=pl.ANY)] * count


def sems(count):
    return pltpu.SemaphoreType.DMA((count,))


def shape(dims, kind):
    return jax.ShapeDtypeStruct(dims, kind)


def params(collective):
    return pltpu.CompilerParams(
        collective_id=collective, has_side_effects=True, vmem_limit_bytes=VMEM_LIMIT
    )


HALVES = (slice(0, HALF), slice(HALF, LEN))


def forward_kernel(
    first_gain, first_shift, triple_bias, mixer_bias, second_gain, second_shift, expand_bias,
    stream_in, cot_in, triple_weight, mixer_weight, expand_weight, reduce_weight,
    triple_out, probs_out, mixed_out, first_out, after_whole_out, parts_out, weight_out,
    own_expand, passing_expand, early_expand, onward_expand, own_reduce, passing_reduce, early_reduce,
    onward_reduce,
    after_out, grad_after_out, grad_mixed_out,
    stats, sums, expand_sum,
    stream, cot, after, grad_after, grad_mixed,
    triple_raw, mixer_raw, expand_raw, weight, mixer, expander,
    edge, edge_in, mixer_edge, mixer_edge_in, wide, land_one, land_two, whole, second_whole,
    total, triple, mixed, stage, hidden, low, grads_expand, grads_reduce, tiles,
    parts, twin, one_in, left_two, right_two,
    local, gather_send, gather_receive, reduce_send, reduce_receive, share_send, share_receive,
    edge_send, edge_receive, spread_send, spread_receive,
):
    place = Place()
    me = place.me

    def load(source, target, slot):
        copy = pltpu.make_async_copy(source, target, local.at[slot])
        copy.start()
        return copy

    stream_load = load(stream_in, stream, 11)
    triple_load = load(triple_weight, triple_raw, 1)
    cot_load = load(cot_in, cot, 12)
    mixer_load = load(mixer_weight, mixer_raw, 0)
    expand_load = load(expand_weight, expand_raw, 2)
    greet(
        [{"mp": peer} for peer in place.peers]
        + [{"dp": place.along(axis, step)[1]} for axis in "zy" for step in range(1, 4)]
    )
    gather_sems = (gather_send, gather_receive)
    edge_sems = (edge_send, edge_receive)
    shares = [Share(place, tiles.at[half], (share_send, share_receive), 7 * half) for half in range(2)]
    firsts = [Gather(place, land_one, half, gather_sems, 13 * half) for half in range(2)]
    cots = [Gather(place, land_two, half, gather_sems, 26 + 13 * half) for half in range(2)]
    buffers = (parts, twin, one_in, left_two, right_two)
    reduces = [Reduce(place, buffers, half, (reduce_send, reduce_receive), 10 * half) for half in range(2)]
    cot_whole = second_whole
    after_whole = second_whole
    reducer = expand_raw

    def send_center(half, values):
        center = jnp.sum(values, 0, keepdims=True) / NARROW
        shares[half].start(center, jnp.sum(jnp.square(values - center), 0, keepdims=True))

    def normal(half, values, gain, shift, row):
        share = shares[half]
        share.wait()
        centers, spreads = share.read(0), share.read(1)
        center = jnp.sum(centers, 0, keepdims=True) / PARTS
        spread = jnp.sum(spreads, 0, keepdims=True)
        spread += NARROW * jnp.sum(jnp.square(centers - center), 0, keepdims=True)
        scale = lax.rsqrt(spread / D + EPSILON)
        stats[row : row + 1, HALVES[half]] = center
        stats[row + 1 : row + 2, HALVES[half]] = scale
        low_values = (values - center) * scale * gain + shift
        land_one[me, 0:NARROW, HALVES[half]] = low_values.astype(BF)

    def grow(lands, half, chip, target, factor, rows, first):
        pack(lands, chip, target, HALVES[half])
        term = dot_n(factor[chip], target[chip, :, HALVES[half]])
        if first:
            total[0:rows, HALVES[half]] = term
        else:
            total[0:rows, HALVES[half]] += term

    def grow_first(half, chip, first=False):
        grow(land_one, half, chip, whole, weight, 3 * NARROW, first)

    def grow_second(half, chip, first=False):
        grow(land_one, half, chip, whole, expander, HIDDEN, first)

    def edge_copy(half, count):
        rows, lanes = pl.ds(0, count), pl.ds(half * HALF, HALF)
        if half == 2:
            source, target = mixer_edge.at[rows], mixer_edge_in.at[rows]
        else:
            source, target = edge.at[:, rows, lanes], edge_in.at[:, rows, lanes]
        return remote(source, target, edge_sems, half, place.following)

    def edge_do(half, sender, act):
        inside = place.core == (0 if sender else 1)

        @pl.when(inside)
        def _():
            act(edge_copy(half, HD))

        @pl.when(jnp.logical_not(inside))
        def _():
            act(edge_copy(half, 48))

    biases = [column(triple_bias[0:1, :], NARROW), None, column(triple_bias[1:2, :], NARROW)]

    def place_triple(half):
        lanes = HALVES[half]
        for part in range(3):
            values = total[part * NARROW : (part + 1) * NARROW, lanes]
            if part != 1:
                values = values + biases[part]
            values = values.astype(BF)
            edge[part, 0:48, lanes] = values[NARROW - 48 : NARROW]
            edge[part, 48:TAIL, lanes] = values[NARROW - TAIL : NARROW - 48]
            wide[part, pl.ds(pl.multiple_of(TAIL + 8 * me, 8), NARROW), lanes] = values.astype(F32)
        edge_do(half, True, lambda copy: copy.start())
        for part in range(3):
            rows = slice(part * WIN + HD, (part + 1) * WIN)
            triple[rows, lanes] = wide[part, TAIL + HD : TAIL + WIN, lanes].astype(BF)

    def place_tail(half):
        lanes = HALVES[half]
        edge_do(half, False, lambda copy: copy.wait_recv())
        for part in range(3):
            near_rows = edge_in[part, 0:48, lanes].astype(F32)
            wide[part, pl.ds(pl.multiple_of(8 * me + 8, 8), 48), lanes] = near_rows
            wide[part, pl.ds(pl.multiple_of(8 * me, 8), 8), lanes] = edge_in[part, 48:TAIL, lanes].astype(F32)
            rows = slice(part * WIN, part * WIN + HD)
            triple[rows, lanes] = wide[part, TAIL : TAIL + HD, lanes].astype(BF)

    pending = {}

    def look(half, h):
        for tile in (half * HALF, half * HALF + TILE):
            reach = tile + TILE
            lanes = slice(tile, reach)
            queries = triple[HD * h : HD * h + HD, lanes] * jnp.asarray(ROOT, BF)
            keys = triple[WIN + HD * h : WIN + HD * h + HD, 0:reach]
            values = triple[2 * WIN + HD * h : 2 * WIN + HD * h + HD, 0:reach]
            scores = dot_f(keys, queries)
            key_place = lax.broadcasted_iota(jnp.int32, (TILE, TILE), 0)
            query_place = lax.broadcasted_iota(jnp.int32, (TILE, TILE), 1)
            edge_scores = jnp.where(key_place <= query_place, scores[tile:reach], -1e30)
            top = jnp.max(edge_scores, 0, keepdims=True)
            if tile:
                top = jnp.maximum(top, jnp.max(scores[0:tile], 0, keepdims=True))
            edge_weights = jnp.exp(edge_scores - top)
            norm = jnp.sum(edge_weights, 0, keepdims=True)
            if tile:
                weights = jnp.exp(scores[0:tile] - top)
                norm += jnp.sum(weights, 0, keepdims=True)
            slot = 2 if h == 3 else (tile // TILE) % 2
            if slot in pending and h < 3:
                pending.pop(slot).wait()
            inverse = 1.0 / norm
            if tile:
                stage[slot, 0:tile, :] = (weights * inverse).astype(BF)
            stage[slot, tile:reach, :] = (edge_weights * inverse).astype(BF)
            copy = pltpu.make_async_copy(
                stage.at[slot, pl.ds(0, reach), :],
                probs_out.at[h, pl.ds(0, reach), pl.ds(tile, TILE)],
                local.at[4 + slot],
            )
            copy.start()
            mixed[HD * h : HD * h + HD, lanes] = dot_n(values, stage[slot, 0:reach, :]).astype(BF)
            if h == 3:
                copy.wait()
            else:
                pending[slot] = copy

    def look_last(half):
        @pl.when(place.last)
        def _():
            look(half, 3)

    def mix(half):
        for step, chip in enumerate(reduces[half].order):
            reduces[half].put(chip, dot_f(mixer[chip], mixed[:, HALVES[half]]))
            reduces[half].give(step)

    def add_mixed(half):
        values = reduces[half].result() + stream[:, HALVES[half]] + mixer_shift
        after[:, HALVES[half]] = values
        send_center(half, values)

    def pull(half):
        grad = dot_n(reducer[...], cot_whole[:, :, HALVES[half]].reshape(D, HALF))
        low[:, HALVES[half]] = grad.astype(BF)

    bend_root = math.sqrt(2 / math.pi)

    def bend(half):
        for tile in (half * HALF, half * HALF + TILE):
            lanes = slice(tile, tile + TILE)
            pre = total[:, lanes] + bias_column
            square = pre * pre
            curve = jnp.tanh(bend_root * pre * (1 + 0.044715 * square))
            middle = 0.5 * (1 + curve)
            hidden[:, lanes] = (pre * middle).astype(BF)
            slope = middle + 0.5 * pre * (1 - curve * curve) * (bend_root * (1 + 3 * 0.044715 * square))
            grad_pre = low[:, lanes].astype(F32) * slope
            row_sums = jnp.broadcast_to(jnp.sum(grad_pre, 1, keepdims=True), (HIDDEN, 128))
            if tile:
                expand_sum[...] += row_sums
            else:
                expand_sum[...] = row_sums
            low[:, lanes] = grad_pre.astype(BF)

    def fall(half):
        for step, chip in enumerate(reduces[half].order):
            reduces[half].put(chip, dot_f(expander[chip], low[:, HALVES[half]]))
            reduces[half].give(step)
            if step == 1:
                reduces[half].first()

    spread_sems = (spread_send, spread_receive)
    spread_expand = Spread(
        place, "z", grads_expand, passing_expand, early_expand, None, None, None, None, spread_sems, 0
    )
    spread_reduce = Spread(
        place, "y", grads_reduce, passing_reduce, early_reduce, None, None, None, None, spread_sems, 4
    )

    def keep(spread, grads, own, onward, slots):
        low, high = pl.ds(0, SPLIT), pl.ds(SPLIT, CHIP - SPLIT)
        return [
            load(grads.at[place.at[spread.axis]], own, slots),
            load(grads.at[spread.block(1), low], onward.at[low], slots + 1),
            load(grads.at[spread.block(3), high], onward.at[high], slots + 2),
        ]

    def weigh_reduce(half):
        lanes = HALVES[half]
        for chip in range(4):
            put_grads(grads_reduce, "y", chip, dot_t(cot_whole[chip, :, lanes], hidden[:, lanes]), half == 1)

    def weigh_expand(half):
        lanes = HALVES[half]
        for chip in range(4):
            put_grads(grads_expand, "z", chip, dot_t(whole[chip, :, lanes], low[:, lanes]), half == 1)

    def back_start(half):
        lanes = HALVES[half]
        grad = reduces[half].result()
        normed = (after[:, lanes] - stats[2:3, lanes]) * stats[3:4, lanes]
        scaled = grad * gain
        shares[half].start(jnp.sum(scaled, 0, keepdims=True), jnp.sum(scaled * normed, 0, keepdims=True))
        gain_sum = jnp.sum(grad * normed, 1, keepdims=True)
        shift_sum = jnp.sum(grad, 1, keepdims=True)
        if half:
            sums[:, 0:1] += gain_sum
            sums[:, 1:2] += shift_sum
        else:
            sums[:, 0:1] = gain_sum
            sums[:, 1:2] = shift_sum
        grad_after[:, lanes] = scaled

    def back_end(half):
        lanes = HALVES[half]
        share = shares[half]
        share.wait()
        mean = jnp.sum(share.read(0), 0, keepdims=True) / D
        along = jnp.sum(share.read(1), 0, keepdims=True) / D
        normed = (after[:, lanes] - stats[2:3, lanes]) * stats[3:4, lanes]
        grad = stats[3:4, lanes] * (grad_after[:, lanes] - mean - normed * along) + cot[:, lanes]
        grad_after[:, lanes] = grad
        land_two[me, 0:NARROW, lanes] = grad.astype(BF)

    def grow_mixed(half, chip, first=False, last=False):
        lanes = HALVES[half]
        pack(land_two, chip, after_whole, lanes)
        term = dot_n(mixer[chip], after_whole[chip, :, lanes])
        if first:
            total[0:WIN, lanes] = term
        elif last:
            grad_mixed[:, lanes] = (total[0:WIN, lanes] + term).astype(BF)
        else:
            total[0:WIN, lanes] += term

    def back_result(half):
        lanes = HALVES[half]
        term = dot_f(reducer[...], hidden[:, lanes])
        for index in range(PARTS):
            rows = slice(index * NARROW, (index + 1) * NARROW)
            land_one[index, 0:NARROW, lanes] = term[rows].astype(BF)
        lanes = pl.ds(half * HALF, HALF)
        return load(land_one.at[:, :, lanes], parts_out.at[:, :, lanes], 10 if half else 23)

    stream_load.wait()
    for half in range(2):
        send_center(half, stream[:, HALVES[half]])
    cot_load.wait()
    land_two[me, 0:NARROW, :] = cot[...].astype(BF)
    cots[0].start_first()
    gain, shift = column(first_gain[...], NARROW), column(first_shift[...], NARROW)
    triple_load.wait()
    for chip in range(4):
        for part in range(3):
            weight[chip, part * NARROW : (part + 1) * NARROW, :] = triple_raw[
                part, :, chip * CHIP : (chip + 1) * CHIP
            ]
    normal(0, stream[:, HALVES[0]], gain, shift, 0)
    firsts[0].start()
    normal(1, stream[:, HALVES[1]], gain, shift, 0)
    weight_copy = load(weight, weight_out, 1)
    mixer_load.wait()
    mixer_edge[0:48, :] = mixer_raw[NARROW - 48 : NARROW, :]
    mixer_edge[48:TAIL, :] = mixer_raw[NARROW - TAIL : NARROW - 48, :]
    sums[:, 3:4] = jnp.sum(cot[...], 1, keepdims=True)
    mixed[3 * HD : WIN, :] = jnp.zeros((HD, LEN), BF)
    firsts[0].near()
    firsts[1].start()
    grow_first(0, place.chip, True)
    firsts[0].middle()
    grow_first(0, place.left_chip)
    grow_first(0, place.right_chip)
    firsts[0].far()
    firsts[0].last()
    grow_first(0, place.far_chip)
    place_triple(0)
    firsts[1].near()
    edge_do(2, True, lambda copy: copy.start())
    cots[0].start_rest()
    grow_first(1, place.chip, True)
    look(0, 1)
    look(0, 2)
    firsts[1].middle()
    grow_first(1, place.left_chip)
    grow_first(1, place.right_chip)
    firsts[1].far()
    edge_do(2, False, lambda copy: copy.wait_recv())
    spare = slice(HALF, HALF + CHIP)
    for chip in range(4):
        lanes = slice(chip * CHIP, (chip + 1) * CHIP)
        wide[0, :, spare] = jnp.zeros((WIN + TAIL, CHIP), F32)
        near_rows = mixer_edge_in[0:48, lanes].astype(F32)
        wide[0, pl.ds(pl.multiple_of(8 * me + 8, 8), 48), spare] = near_rows
        wide[0, pl.ds(pl.multiple_of(8 * me, 8), 8), spare] = mixer_edge_in[48:TAIL, lanes].astype(F32)
        rows = pl.ds(pl.multiple_of(TAIL + 8 * me, 8), NARROW)
        wide[0, rows, spare] = mixer_raw[:, lanes].astype(F32)
        mixer[chip] = wide[0, TAIL : TAIL + WIN, spare].astype(BF)
    look_last(0)
    place_tail(0)
    look(0, 0)
    mix(0)
    firsts[1].last()
    grow_first(1, place.far_chip)
    place_triple(1)
    first_copy = load(whole, first_out, 7)
    reduces[0].first()
    reduces[0].second()
    cots[0].near()
    look(1, 1)
    look(1, 2)
    reduces[0].third()
    look_last(1)
    place_tail(1)
    look(1, 0)
    mix(1)
    mixer_shift = column(mixer_bias[...], NARROW)
    gain, shift = column(second_gain[...], NARROW), column(second_shift[...], NARROW)
    bias_column = column(expand_bias[...], HIDDEN)
    firsts[0].end()
    add_mixed(0)
    reduces[1].first()
    reduces[1].second()
    cots[0].middle()
    cots[0].far()
    cots[1].start()
    triple_copy = load(triple, triple_out, 8)
    mixed_copy = load(mixed, mixed_out, 9)
    expand_load.wait()
    for chip in range(4):
        expander[chip] = expand_raw[:, chip * CHIP : (chip + 1) * CHIP]
    reduce_load = load(reduce_weight, reducer, 3)
    normal(0, after[:, HALVES[0]], gain, shift, 2)
    firsts[0].start()
    reduces[1].third()
    cots[0].last()
    for chip in range(4):
        pack(land_two, chip, cot_whole, HALVES[0])
    reduce_load.wait()
    pull(0)
    firsts[0].near()
    firsts[1].end()
    add_mixed(1)
    after_copy = load(after, after_out, 13)
    first_copy.wait()
    grow_second(0, place.chip, True)
    cots[1].near()
    firsts[0].middle()
    grow_second(0, place.left_chip)
    grow_second(0, place.right_chip)
    normal(1, after[:, HALVES[1]], gain, shift, 2)
    firsts[1].start()
    firsts[0].far()
    cots[1].middle()
    firsts[0].last()
    grow_second(0, place.far_chip)
    reduces[0].end()
    bend(0)
    fall(0)
    firsts[1].near()
    reduces[0].second()
    grow_second(1, place.chip, True)
    weigh_expand(0)
    cots[1].far()
    cots[1].last()
    for chip in range(4):
        pack(land_two, chip, cot_whole, HALVES[1])
    pull(1)
    firsts[1].middle()
    grow_second(1, place.left_chip)
    grow_second(1, place.right_chip)
    reduces[0].third()
    firsts[1].far()
    weigh_reduce(0)
    firsts[1].last()
    grow_second(1, place.far_chip)
    reduces[1].end()
    bend(1)
    fall(1)
    cots[0].end()
    back_start(0)
    reduces[1].second()
    weigh_reduce(1)
    spread_reduce.start()
    reduces[1].third()
    back_end(0)
    cots[0].start()
    weigh_expand(1)
    spread_expand.start()
    kept = keep(spread_reduce, grads_reduce, own_reduce, onward_reduce, 16)
    kept += keep(spread_expand, grads_expand, own_expand, onward_expand, 19)
    cots[1].end()
    back_start(1)
    firsts[0].end()
    firsts[1].end()
    cots[0].near()
    grow_mixed(0, place.chip, True)
    parts_copies = [back_result(0)]
    back_end(1)
    cots[1].start()
    grad_after_copy = load(grad_after, grad_after_out, 14)
    cots[0].middle()
    grow_mixed(0, place.left_chip)
    grow_mixed(0, place.right_chip)
    cots[0].far()
    cots[0].last()
    grow_mixed(0, place.far_chip, False, True)
    cots[1].near()
    grow_mixed(1, place.chip, True)
    parts_copies.append(back_result(1))
    cots[1].middle()
    grow_mixed(1, place.left_chip)
    grow_mixed(1, place.right_chip)
    sums[:, 2:3] = jnp.sum(grad_after[...], 1, keepdims=True)
    whole_copies = [
        load(after_whole.at[chip], after_whole_out.at[chip], slot)
        for slot, chip in ((0, place.chip), (2, place.left_chip), (3, place.right_chip))
    ]
    cots[1].far()
    cots[1].last()
    grow_mixed(1, place.far_chip, False, True)
    whole_copies.append(load(after_whole.at[place.far_chip], after_whole_out.at[place.far_chip], 22))
    grad_mixed_copy = load(grad_mixed, grad_mixed_out, 15)
    reduces[0].end()
    reduces[1].end()
    for gather in cots:
        gather.end()
    for half in range(3):
        edge_do(half, True, lambda copy: copy.wait_send())
    for spread in (spread_reduce, spread_expand):
        spread.arrive(range(4))
        spread.leave(range(4))
    for copy in (
        weight_copy, triple_copy, mixed_copy, *parts_copies, *kept, after_copy, grad_after_copy,
        grad_mixed_copy, *whole_copies, *pending.values(),
    ):
        copy.wait()


def forward(*arguments):
    wide_rows = WIN + TAIL
    return pl.pallas_call(
        forward_kernel,
        out_shape=(
            shape((3 * WIN, LEN), BF),
            shape((4, LEN, LEN), BF),
            shape((WIN, LEN), BF),
            shape((4, CHIP, LEN), BF),
            shape((4, CHIP, LEN), BF),
            shape((PARTS, ROWS, LEN), BF),
            shape((4, 3 * NARROW, CHIP), BF),
            *[shape((CHIP, HIDDEN), BF)] * 8,
            shape((NARROW, LEN), F32),
            shape((NARROW, LEN), F32),
            shape((WIN, LEN), BF),
            shape((8, LEN), F32),
            shape((NARROW, 128), F32),
            shape((HIDDEN, 128), F32),
        ),
        in_specs=vmem(7) + hbm(6),
        out_specs=tuple(hbm(18) + vmem(3)),
        scratch_shapes=[
            *[pltpu.VMEM((NARROW, LEN), F32)] * 4,
            pltpu.VMEM((WIN, LEN), BF),
            pltpu.VMEM((3, NARROW, D), BF),
            pltpu.VMEM((NARROW, D), BF),
            pltpu.VMEM((HIDDEN, D), BF),
            pltpu.VMEM((4, 3 * NARROW, CHIP), BF),
            pltpu.VMEM((4, WIN, CHIP), BF),
            pltpu.VMEM((4, HIDDEN, CHIP), BF),
            pltpu.VMEM((3, HD, LEN), BF),
            pltpu.VMEM((3, HD, LEN), BF),
            pltpu.VMEM((HD, D), BF),
            pltpu.VMEM((HD, D), BF),
            pltpu.VMEM((3, WIN + TAIL, LEN), F32),
            pltpu.VMEM((PARTS, ROWS, LEN), BF),
            pltpu.VMEM((PARTS, ROWS, LEN), BF),
            pltpu.VMEM((4, CHIP, LEN), BF),
            pltpu.VMEM((4, CHIP, LEN), BF),
            pltpu.VMEM((HIDDEN, LEN), F32),
            pltpu.VMEM((3 * WIN, LEN), BF),
            pltpu.VMEM((WIN, LEN), BF),
            pltpu.VMEM((3, LEN, TILE), BF),
            pltpu.VMEM((HIDDEN, LEN), BF),
            pltpu.VMEM((HIDDEN, LEN), BF),
            pltpu.VMEM((4, CHIP, HIDDEN), BF),
            pltpu.VMEM((4, CHIP, HIDDEN), BF),
            pltpu.VMEM((2, PARTS, 8, 128), F32),
            *REDUCE_BUFFERS,
            sems(24),
            sems(52),
            sems(52),
            sems(20),
            sems(20),
            sems(14),
            sems(14),
            sems(3),
            sems(3),
            sems(8),
            sems(8),
        ],
        compiler_params=params(1),
        name="forward",
    )(*arguments)


VECTORS = 12


def backward_kernel(
    stats, first_gain, reduce_bias, second_sums, expand_sum,
    stream_in, after_in_rows, grad_after_in, triple_in, probs_in, mixed_in, grad_mixed_in, first_in, after_in, parts_in, weight_in,
    own_expand_in, passing_expand_in, early_expand_in, onward_expand_in,
    own_reduce_in, passing_reduce_in, early_reduce_in, onward_reduce_in,
    result, grad_stream, out_triple, out_mixer, out_expand, out_reduce,
    out_gain, out_shift, out_bias, out_mixer_bias, out_second_gain, out_second_shift, out_expand_bias,
    out_reduce_bias,
    stream, after, grad_after, triple, probs, mixed, grad_mixed, first_whole, after_whole, weight,
    grad_triple, own, wide, edge, edge_in, keys_total, tiles, sums, table,
    parts_one, twin_one, one_in, left_two, right_two,
    parts_two, twin_two, two_in, left_four, right_four,
    own_expand, passing_expand, early_expand, onward_expand, late_expand, middle_expand, second_expand,
    own_reduce, passing_reduce, early_reduce, onward_reduce, late_reduce, middle_reduce, second_reduce,
    grads_mixer, passing_mixer, early_mixer, late_mixer, middle_mixer, second_mixer,
    grads_z, passing_z, early_z, late_z, middle_z, second_z,
    grads_y, passing_y, early_y, late_y, middle_y, second_y,
    local, probs_sems, reduce_send, reduce_receive, share_send, share_receive, edge_send, edge_receive,
    spread_send, spread_receive, table_send, table_receive,
):
    place = Place()
    me = place.me
    group = place.group

    def load(source, target, slot):
        copy = pltpu.make_async_copy(source, target, local.at[slot])
        copy.start()
        return copy

    triple_load = load(triple_in, triple, 0)
    grad_mixed_load = load(grad_mixed_in, grad_mixed, 1)
    mixed_load = load(mixed_in, mixed, 2)

    def probs_copy(h, tile):
        reach = tile + TILE
        return pltpu.make_async_copy(
            probs_in.at[h, pl.ds(0, reach), pl.ds(tile, TILE)],
            probs.at[h, pl.ds(0, reach), pl.ds(tile, TILE)],
            probs_sems.at[4 * h + tile // TILE],
        )

    tiles_of = ((TILE, 0), (3 * TILE, 2 * TILE))

    def probs_load(half, h):
        for tile in tiles_of[half]:
            probs_copy(h, tile).start()

    probs_load(1, 0)
    pass_loads = [
        load(onward_reduce_in, onward_reduce, 5),
        load(passing_reduce_in, passing_reduce, 6),
        load(onward_expand_in, onward_expand, 7),
        load(passing_expand_in, passing_expand, 8),
    ]
    probs_load(1, 1)
    parts_load = load(parts_in, parts_one, 3)
    probs_load(1, 2)

    @pl.when(place.last)
    def _():
        probs_load(1, 3)

    weight_load = load(weight_in, weight, 4)
    after_load = load(after_in, after_whole, 11)
    turn_loads = [
        load(early_reduce_in, early_reduce, 9),
        load(own_reduce_in, own_reduce, 10),
        load(early_expand_in, early_expand, 16),
        load(own_expand_in, own_expand, 17),
    ]
    for h in range(3):
        probs_load(0, h)

    @pl.when(place.last)
    def _():
        probs_load(0, 3)

    first_load = load(first_in, first_whole, 12)
    row_loads = [
        load(stream_in, stream, 13),
        load(after_in_rows, after, 14),
        load(grad_after_in, grad_after, 15),
    ]
    others = [lax.rem(group + i, 16) for i in range(1, 16)]
    greet([{"mp": peer} for peer in place.peers] + [{"dp": other} for other in others])
    reduce_sems = (reduce_send, reduce_receive)
    edge_sems = (edge_send, edge_receive)
    spread_sems = (spread_send, spread_receive)
    shares = [Share(place, tiles.at[half], (share_send, share_receive), 7 * half) for half in range(2)]
    one = (parts_one, twin_one, one_in, left_two, right_two)
    two = (parts_two, twin_two, two_in, left_four, right_four)
    outs = [Reduce(place, one, half, reduce_sems, 10 * half) for half in range(2)]
    reduces = [Reduce(place, two, half, reduce_sems, 20 + 10 * half) for half in range(2)]
    spread_expand = Spread(
        place, "z", None, passing_expand, early_expand, passing_expand, late_expand, middle_expand, second_expand, spread_sems, 0
    )
    spread_reduce = Spread(
        place, "y", None, passing_reduce, early_reduce, passing_reduce, late_reduce, middle_reduce, second_reduce, spread_sems, 9
    )
    spread_mixer = Spread(
        place, "z", grads_mixer, passing_mixer, early_mixer, passing_mixer, late_mixer, middle_mixer, second_mixer, spread_sems, 18
    )
    spread_z = Spread(
        place, "z", grads_z, passing_z, early_z, passing_z, late_z, middle_z, second_z, spread_sems, 27
    )
    spread_y = Spread(
        place, "y", grads_y, passing_y, early_y, passing_y, late_y, middle_y, second_y, spread_sems, 36
    )

    def edge_copy(step):
        if step == 2:
            piece, target = edge.at[3], edge_in.at[3]
        else:
            lanes = pl.ds(step * HALF, HALF)
            piece, target = edge.at[0:3, :, lanes], edge_in.at[0:3, :, lanes]
        return remote(piece, target, edge_sems, step, place.previous)

    mixed_load.wait()
    edge[3] = mixed[0:HD, :]
    edge_copy(2).start()
    grad_triple[...] = jnp.zeros((3 * WIN, LEN), BF)
    triple_load.wait()
    grad_mixed_load.wait()

    def attend(half, h):
        row = HD * h
        keys = triple[WIN + row : WIN + row + HD, :]
        values = triple[2 * WIN + row : 2 * WIN + row + HD, :]
        for tile in reversed(tiles_of[half]) if half == 0 else tiles_of[half]:
            probs_copy(h, tile).wait()
        for tile in tiles_of[half]:
            reach = tile + TILE
            lanes = slice(tile, reach)
            queries = triple[row : row + HD, lanes] * jnp.asarray(ROOT, BF)
            grad_out = grad_mixed[row : row + HD, lanes]
            delta = jnp.sum(
                grad_out.astype(F32) * mixed[row : row + HD, lanes].astype(F32), 0, keepdims=True
            )
            chances = probs[h, 0:reach, lanes]
            grad_probs = dot_f(values[:, 0:reach], grad_out)
            grad_scores = (chances.astype(F32) * (grad_probs - delta)).astype(BF)
            grad_queries = dot_n(keys[:, 0:reach], grad_scores) * ROOT
            grad_triple[row : row + HD, lanes] = grad_queries.astype(BF)
            key_term = dot_t(queries, grad_scores)
            value_term = dot_t(grad_out, chances)
            if reach == LEN:
                keys_total[h, 0] = key_term
                keys_total[h, 1] = value_term
            else:
                keys_total[h, 0, :, 0:reach] += key_term
                keys_total[h, 1, :, 0:reach] += value_term
        lanes = HALVES[half]
        grad_triple[WIN + row : WIN + row + HD, lanes] = keys_total[h, 0, :, lanes].astype(BF)
        grad_triple[2 * WIN + row : 2 * WIN + row + HD, lanes] = keys_total[h, 1, :, lanes].astype(BF)

    def attend_last(half):
        @pl.when(place.last)
        def _():
            attend(half, 3)

    def send_edge(half):
        for part in range(3):
            edge[part, :, HALVES[half]] = grad_triple[part * WIN : part * WIN + HD, HALVES[half]]
        edge_copy(half).start()

    def place_own(part, lanes):
        if part < 3:
            piece = grad_triple[part * WIN : (part + 1) * WIN, lanes]
        else:
            piece = mixed[:, lanes]
        piece = piece.astype(F32)
        wide[0 : 3 * HD, lanes] = piece[0 : 3 * HD]
        neighbour = edge_in[part, :, lanes].astype(F32)
        wide[3 * HD : WIN, lanes] = jnp.where(place.last, piece[3 * HD : WIN], neighbour)
        values = wide[pl.ds(pl.multiple_of(8 * me, 8), NARROW), lanes]
        own[part * NARROW : (part + 1) * NARROW, lanes] = values.astype(BF)
        return jnp.sum(values, 1, keepdims=True)

    def place_rows(half):
        edge_copy(half).wait_recv()
        for part in range(3):
            total = place_own(part, HALVES[half])
            if half == 1:
                sums[:, 2 + part : 3 + part] = total
            else:
                sums[:, 2 + part : 3 + part] += total

    def fall(half, rows=True):
        if rows:
            place_rows(half)
        for step, chip in enumerate(reduces[half].order):
            reduces[half].put(chip, dot_f(weight[chip], own[0 : 3 * NARROW, HALVES[half]]))
            reduces[half].give(step)
            if step == 1:
                reduces[half].first()

    def weigh(axis, grads, whole, rows):
        for chip in range(4):
            put_grads(grads, axis, chip, dot_t(whole[chip], own[rows, :]))

    attend(1, 0)
    send_edge(1)
    for copy in pass_loads:
        copy.wait()
    spread_reduce.pass_on(lambda rows: onward_reduce[rows])
    spread_expand.pass_on(lambda rows: onward_expand[rows])
    parts_load.wait()
    for half in (1, 0):
        for step in range(4):
            outs[half].give(step)
    attend(1, 1)
    outs[1].first()
    outs[0].first()
    attend(1, 2)
    attend_last(1)
    weight_load.wait()
    fall(1)
    edge_copy(2).wait_recv()
    place_own(3, slice(0, LEN))
    after_load.wait()
    weigh("z", grads_mixer, after_whole, slice(3 * NARROW, 4 * NARROW))
    spread_mixer.start()
    attend(0, 0)
    send_edge(0)
    reduces[1].second()
    outs[1].second()
    attend(0, 1)
    for copy in turn_loads:
        copy.wait()
    spread_reduce.arrive((4, 5))
    spread_reduce.turn(own_reduce[...])
    spread_expand.arrive((4, 5))
    spread_expand.turn(own_expand[...])
    attend(0, 2)
    attend_last(0)
    spread_mixer.arrive((0, 1))
    spread_mixer.pass_on(spread_mixer.mine)
    first_load.wait()
    place_rows(0)
    weigh("y", grads_y, first_whole, slice(WIN, 3 * NARROW))
    spread_y.start()
    weigh("z", grads_z, first_whole, slice(0, WIN))
    spread_z.start()
    reduces[1].third()
    fall(0, False)
    outs[0].second()
    outs[1].third()
    spread_mixer.arrive(range(2, 6))
    spread_mixer.turn(grads_mixer[place.at["z"]])
    reduces[0].second()
    reduces[0].third()
    spread_z.arrive((0, 1))
    spread_z.pass_on(spread_z.mine)
    spread_y.arrive((0, 1))
    spread_y.pass_on(spread_y.mine)
    outs[0].third()
    for copy in row_loads:
        copy.wait()
    gain = column(first_gain[...], NARROW)
    shift = column(reduce_bias[...], NARROW)

    def back_start(half):
        lanes = HALVES[half]
        grad = reduces[half].result()
        normed = (stream[:, lanes] - stats[0:1, lanes]) * stats[1:2, lanes]
        scaled = grad * gain
        shares[half].start(jnp.sum(scaled, 0, keepdims=True), jnp.sum(scaled * normed, 0, keepdims=True))
        gain_sum = jnp.sum(grad * normed, 1, keepdims=True)
        shift_sum = jnp.sum(grad, 1, keepdims=True)
        if half == 1:
            sums[:, 0:1] = gain_sum
            sums[:, 1:2] = shift_sum
        else:
            sums[:, 0:1] += gain_sum
            sums[:, 1:2] += shift_sum
        grad_stream[:, lanes] = scaled

    def back_end(half):
        lanes = HALVES[half]
        share = shares[half]
        share.wait()
        mean = jnp.sum(share.read(0), 0, keepdims=True) / D
        along = jnp.sum(share.read(1), 0, keepdims=True) / D
        normed = (stream[:, lanes] - stats[0:1, lanes]) * stats[1:2, lanes]
        back = stats[1:2, lanes] * (grad_stream[:, lanes] - mean - normed * along)
        grad_stream[:, lanes] = back + grad_after[:, lanes]

    back_start(1)
    out_expand[...] = spread_expand.result()
    out_reduce[...] = spread_reduce.result()
    out_mixer[...] = spread_mixer.result().T
    back_end(1)
    back_start(0)
    columns = [
        sums[:, 0:1], sums[:, 1:2], sums[:, 2:3], sums[:, 4:5],
        second_sums[:, 2:3], second_sums[:, 0:1], second_sums[:, 1:2], second_sums[:, 3:4],
    ]
    columns += [expand_sum[NARROW * i : NARROW * (i + 1), 0:1] for i in range(4)]
    spot = lax.broadcasted_iota(jnp.int32, (NARROW, 128), 1)
    packed = jnp.zeros((NARROW, 128), F32)
    for i, values in enumerate(columns):
        packed = jnp.where(spot == i, values, packed)
    table[group] = packed.T[0:16]

    def table_copy(step, owner, device):
        return remote(table.at[owner], table.at[owner], (table_send, table_receive), step, device, "dp")

    for step, other in enumerate(others):
        table_copy(step, group, other).start()
    spread_z.arrive(range(2, 6))
    spread_z.turn(grads_z[place.at["z"]])
    spread_y.arrive(range(2, 6))
    spread_y.turn(grads_y[place.at["y"]])
    for half in range(2):
        result[:, HALVES[half]] = outs[half].result() + after[:, HALVES[half]] + shift
    back_end(0)
    for step in range(15):
        table_copy(step, lax.rem(group + 15 - step, 16), group).wait_recv()
    vectors = jnp.sum(table[...], 0)
    out_gain[...] = vectors[0:1].reshape(NARROW)
    out_shift[...] = vectors[1:2].reshape(NARROW)
    out_bias[...] = vectors[2:4]
    out_mixer_bias[...] = vectors[4:5].reshape(NARROW)
    out_second_gain[...] = vectors[5:6].reshape(NARROW)
    out_second_shift[...] = vectors[6:7].reshape(NARROW)
    out_reduce_bias[...] = vectors[7:8].reshape(NARROW)
    out_expand_bias[...] = vectors[8:12]
    rest = jnp.concatenate([spread_z.result(), spread_y.result()], 1)
    for part in range(3):
        out_triple[part] = rest[:, part * NARROW : (part + 1) * NARROW].T
    for reduce in outs + reduces:
        reduce.end()
    for step in range(3):
        edge_copy(step).wait_send()
    for spread in (spread_expand, spread_reduce):
        spread.leave(range(4, 9))
    for spread in (spread_mixer, spread_z, spread_y):
        spread.leave(range(9))
    for step, other in enumerate(others):
        table_copy(step, group, other).wait_send()


def spread_scratch(lanes, whole):
    one = pltpu.VMEM((CHIP, lanes), BF)
    ends = [pltpu.VMEM((4, DEEP, lanes), BF), pltpu.VMEM((3, DEEP, lanes), BF)]
    return [pltpu.VMEM((4, CHIP, lanes), BF) if whole else one] + [one] * (3 if whole else 4) + ends


def backward(*arguments):
    width = 4 * NARROW
    return pl.pallas_call(
        backward_kernel,
        out_shape=(
            shape((NARROW, LEN), F32),
            shape((NARROW, LEN), F32),
            shape((3, NARROW, 100), F32),
            shape((NARROW, 100), F32),
            shape((100, HIDDEN), F32),
            shape((100, HIDDEN), F32),
            shape((NARROW,), F32),
            shape((NARROW,), F32),
            shape((2, NARROW), F32),
            shape((NARROW,), F32),
            shape((NARROW,), F32),
            shape((NARROW,), F32),
            shape((4, NARROW), F32),
            shape((NARROW,), F32),
        ),
        in_specs=vmem(5) + hbm(19),
        out_specs=tuple(vmem(14)),
        scratch_shapes=[
            *[pltpu.VMEM((NARROW, LEN), F32)] * 3,
            pltpu.VMEM((3 * WIN, LEN), BF),
            pltpu.VMEM((4, LEN, LEN), BF),
            pltpu.VMEM((WIN, LEN), BF),
            pltpu.VMEM((WIN, LEN), BF),
            pltpu.VMEM((4, CHIP, LEN), BF),
            pltpu.VMEM((4, CHIP, LEN), BF),
            pltpu.VMEM((4, 3 * NARROW, CHIP), BF),
            pltpu.VMEM((3 * WIN, LEN), BF),
            pltpu.VMEM((width, LEN), BF),
            pltpu.VMEM((WIN, LEN), F32),
            pltpu.VMEM((4, HD, LEN), BF),
            pltpu.VMEM((4, HD, LEN), BF),
            pltpu.VMEM((4, 2, HD, LEN), F32),
            pltpu.VMEM((2, PARTS, 8, 128), F32),
            pltpu.VMEM((NARROW, 128), F32),
            pltpu.VMEM((16, 16, NARROW), F32),
            *REDUCE_BUFFERS,
            *REDUCE_BUFFERS,
            *spread_scratch(HIDDEN, False),
            *spread_scratch(HIDDEN, False),
            *spread_scratch(NARROW, True),
            *spread_scratch(WIN, True),
            *spread_scratch(3 * NARROW - WIN, True),
            sems(18),
            sems(16),
            sems(40),
            sems(40),
            sems(14),
            sems(14),
            sems(3),
            sems(3),
            sems(45),
            sems(45),
            sems(15),
            sems(15),
        ],
        compiler_params=params(2),
        name="backward",
    )(*arguments)


def hand_over_kernel(*refs):
    count = len(refs) // 2
    for source, target in zip(refs[:count], refs[count:]):
        if source.shape == target.shape:
            target[...] = source[...]
        else:
            rows = [source[i : i + 1, :] for i in range(source.shape[0])]
            target[...] = jnp.concatenate(rows, 1).reshape(target.shape)


def hand_over(*arrays):
    count = len(arrays)
    return pl.pallas_call(
        hand_over_kernel,
        out_shape=tuple(
            shape((HIDDEN,) if array.shape == (4, NARROW) else array.shape, array.dtype) for array in arrays
        ),
        in_specs=vmem(count),
        out_specs=tuple(vmem(count)),
        compiler_params=pltpu.CompilerParams(vmem_limit_bytes=VMEM_LIMIT),
        name="hand_over",
    )(*arrays)


def shards(
    stream, first_gain, first_shift, triple_weight, triple_bias, mixer_weight, mixer_bias,
    second_gain, second_shift, expand_weight, expand_bias, reduce_weight, reduce_bias, cotangent,
):
    turned = stream.T
    (
        triple, probs, mixed, first_whole, after_whole, parts, weight,
        *spreads,
        after, grad_after, grad_mixed, stats, sums, expand_sum,
    ) = forward(
        first_gain, first_shift, triple_bias, mixer_bias, second_gain, second_shift, expand_bias,
        turned, cotangent.T, triple_weight.transpose(1, 2, 0), mixer_weight, expand_weight.T, reduce_weight,
    )
    (
        result, grad_stream, out_triple, out_mixer, out_expand, out_reduce,
        out_gain, out_shift, out_bias, out_mixer_bias, out_second_gain, out_second_shift, out_expand_bias,
        out_reduce_bias,
    ) = hand_over(*backward(
        stats, first_gain, reduce_bias, sums, expand_sum,
        turned, after, grad_after, triple, probs, mixed, grad_mixed, first_whole, after_whole, parts, weight, *spreads,
    ))
    return (
        result.T,
        grad_stream.T,
        out_gain,
        out_shift,
        out_triple.transpose(2, 0, 1),
        out_bias,
        out_mixer,
        out_mixer_bias,
        out_second_gain,
        out_second_shift,
        out_expand,
        out_expand_bias,
        out_reduce.T,
        out_reduce_bias,
    )


def solution(mesh):
    placed = (
        P("dp", "mp"),
        P("mp"),
        P("mp"),
        P(None, None, "mp"),
        P(None, "mp"),
        P("mp", None),
        P("mp"),
        P("mp"),
        P("mp"),
        P(None, "mp"),
        P("mp"),
        P("mp", None),
        P("mp"),
        P("dp", "mp"),
    )
    return jax.shard_map(
        shards,
        mesh=mesh,
        in_specs=placed,
        out_specs=(
            P("dp", "mp"),
            P("dp", "mp"),
            P("mp"),
            P("mp"),
            P("dp", None, "mp"),
            P(None, "mp"),
            P("mp", "dp"),
            P("mp"),
            P("mp"),
            P("mp"),
            P("dp", "mp"),
            P("mp"),
            P("mp", "dp"),
            P("mp"),
        ),
        check_vma=False,
    )
```
